128 devices in a mesh: dp: 32 (over y_hi, z, x), tensor: 4 (over y_lo, core).
Axes of the slice: x: 4, y: 4 (y_hi: 2, y_lo: 2; y = y_hi * 2 + y_lo), z: 4, core: 2. Of those that a mesh axis runs over, the one named last changes fastest.
Arguments:
- tokens: bfloat16 [4608, 1024], P('dp', 'tensor'), may hold values from -6 to 6
- lengths: int32 [32, 4], P('dp'), may hold values from 1 to 72, 144 in all within a row
- attn_gain: float32 [1024], replicated, may hold values from 0.25 to 1.75
- w_query: bfloat16 [1024, 1024], P(None, 'tensor'), may hold values from -0.1875 to 0.1875
- key_weight: bfloat16 [1024, 512], P(None, 'tensor'), may hold values from -0.1875 to 0.1875
- value_weight: bfloat16 [1024, 512], P(None, 'tensor'), may hold values from -0.1875 to 0.1875
- query_gain: float32 [64], replicated, may hold values from 0.25 to 1.75
- key_gain: float32 [64], replicated, may hold values from 0.25 to 1.75
- w_output: bfloat16 [1024, 1024], P('tensor'), may hold values from -1 to 1
- mlp_gain: float32 [1024], replicated, may hold values from 0.25 to 1.75
- w_gate: bfloat16 [1024, 4608], P(None, 'tensor'), may hold values from -0.1875 to 0.1875
- w_up: bfloat16 [1024, 4608], P(None, 'tensor'), may hold values from -0.1875 to 0.1875
- w_down: bfloat16 [4608, 1024], P('tensor'), may hold values from -0.1875 to 0.1875
- cotangent: bfloat16 [4608, 1024], P('dp', 'tensor'), may hold values from -6 to 6
Outputs:
- block_out: bfloat16 [4608, 1024], P('dp', 'tensor')
- input_grad: bfloat16 [4608, 1024], P('dp', 'tensor')
- attn_gain_grad: float32 [1024], replicated
- w_query_grad: float32 [1024, 1024], P(None, 'tensor')
- w_key_grad: float32 [1024, 512], P(None, 'tensor')
- w_value_grad: float32 [1024, 512], P(None, 'tensor')
- query_gain_grad: float32 [64], replicated
- key_gain_grad: float32 [64], replicated
- w_output_grad: float32 [1024, 1024], P('tensor')
- mlp_gain_grad: float32 [1024], replicated
- w_gate_grad: float32 [1024, 4608], P(None, 'tensor')
- w_up_grad: float32 [1024, 4608], P(None, 'tensor')
- w_down_grad: float32 [4608, 1024], P('tensor')
The draws below stay inside these ranges and needn't reach their ends.
Inputs may be any that keep to these rules, and one draw needn't show every extreme that they name: `lengths`: each row sums to 144, and its largest entry is exactly 72.
All inputs are finite; a program needn't handle non-finite values.
Results may differ from the reference program's by a relative error of at most 0.035.
Values may be sent and summed in bfloat16 or wider, within the bound.
A program may use at most 128 MiB of HBM per device.

```python
import math
import jax
import jax.numpy as jnp
import numpy as np
from jax import lax

MODEL_WIDTH = 1024
QUERY_HEADS = 16
KEY_VALUE_HEADS = 8
HEAD_SIZE = 64
FF = 4608
GROUP_TOKENS = 144
DOC_DEV = 4
MAXLEN = 72
GROUPS = 32
TOKENS = 4608
N_DP = 32


def block_scale(rng, shape, pieces, least, largest):
    factor_of = 1.0
    for dim, blocks in pieces:
        heights = jax.random.uniform(jax.random.fold_in(jax.random.fold_in(rng, 6), dim), (blocks,), jnp.float32, least / len(pieces), largest / len(pieces))
        factor_of = factor_of * jnp.repeat(jnp.exp(heights), shape[dim] // blocks).reshape((-1,) + (1,) * (len(shape) - 1 - dim))
    return factor_of


def split_up(amount, total, most, skew):
    portions = [(1 << 20) // math.isqrt(grade ** skew) + 1 for grade in range(2, amount + 1)]
    spare, holding = total - most - (amount - 1), [1] * (amount - 1)
    while spare > 0:
        free = [i for i in range(amount - 1) if holding[i] < most]
        mass, remaining = sum([portions[i] for i in free]), spare
        for i in free:
            extra = min(most - holding[i], max(1, remaining * portions[i] // mass), spare)
            holding[i] = holding[i] + extra
            spare = spare - extra
    return np.array([most] + holding)


def ragged(own_key, amount, total, limit, slope):
    if amount == 2:
        one = jax.random.randint(own_key, (), max(1, total - limit), min(limit, total - 1) + 1)
        return jnp.stack([one, total - one])
    tallies = jnp.asarray(split_up(amount, total, limit, slope), jnp.int32)
    couples = (amount - 1) // 2
    donor, taker = tallies[1:1 + 2 * couples:2], tallies[2:2 + 2 * couples:2]
    slack = jnp.minimum(donor - 1, limit - taker)
    moved = jax.random.randint(jax.random.fold_in(own_key, 1), (couples,), 0, 1 << 20) % (slack + 1)
    tallies = tallies.at[1:1 + 2 * couples:2].set(donor - moved).at[2:2 + 2 * couples:2].set(taker + moved)
    return tallies[jax.random.permutation(jax.random.fold_in(own_key, 2), amount)]


def centred(stream_key, shape, width, reach, split=(), kind=jnp.bfloat16):
    drawn = width * jax.random.normal(stream_key, shape, jnp.float32)
    if split:
        drawn = drawn * block_scale(stream_key, shape, split, -0.22, 0.18)
    return jnp.clip(drawn, -reach, reach).astype(kind)


def setup_inputs(seed: int = 0) -> dict:
    key_list = jax.random.split(jax.random.key(seed), 15)
    tokens = centred(key_list[0], (TOKENS, MODEL_WIDTH), 1.0, 6.0, ((0, 32), (1, 4)))
    lengths = jax.vmap(lambda own: ragged(own, DOC_DEV, GROUP_TOKENS, MAXLEN, 2))(jax.random.split(key_list[1], GROUPS)).reshape((GROUPS, DOC_DEV)).astype(jnp.int32)
    attn_gain = jnp.clip(1.0 + 0.15 * jax.random.normal(key_list[2], (MODEL_WIDTH,), jnp.float32), 0.25, 1.75)
    w_query = centred(key_list[3], (MODEL_WIDTH, QUERY_HEADS * HEAD_SIZE), MODEL_WIDTH ** -0.5, 0.1875, ((1, 4),))
    key_weight = centred(key_list[4], (MODEL_WIDTH, KEY_VALUE_HEADS * HEAD_SIZE), MODEL_WIDTH ** -0.5, 0.1875, ((1, 4),))
    value_weight = centred(key_list[5], (MODEL_WIDTH, KEY_VALUE_HEADS * HEAD_SIZE), MODEL_WIDTH ** -0.5, 0.1875, ((1, 4),))
    query_gain = jnp.clip(1.0 + 0.15 * jax.random.normal(key_list[6], (HEAD_SIZE,), jnp.float32), 0.25, 1.75)
    key_gain = jnp.clip(1.0 + 0.15 * jax.random.normal(key_list[7], (HEAD_SIZE,), jnp.float32), 0.25, 1.75)
    w_output = centred(key_list[8], (QUERY_HEADS * HEAD_SIZE, MODEL_WIDTH), (HEAD_SIZE // 2) ** -0.5, 1.0, ((0, 4),))
    mlp_gain = jnp.clip(1.0 + 0.15 * jax.random.normal(key_list[9], (MODEL_WIDTH,), jnp.float32), 0.25, 1.75)
    w_gate = centred(key_list[10], (MODEL_WIDTH, FF), MODEL_WIDTH ** -0.5, 0.1875, ((1, 4),))
    w_up = centred(key_list[11], (MODEL_WIDTH, FF), MODEL_WIDTH ** -0.5, 0.1875, ((1, 4),))
    w_down = centred(key_list[12], (FF, MODEL_WIDTH), (FF // 4) ** -0.5, 0.1875, ((0, 4),))
    cotangent = centred(key_list[13], (TOKENS, MODEL_WIDTH), 1.0, 6.0, ((0, 32), (1, 4)))
    return {"tokens": tokens, "lengths": lengths, "attn_gain": attn_gain, "w_query": w_query, "key_weight": key_weight, "value_weight": value_weight, "query_gain": query_gain, "key_gain": key_gain, "w_output": w_output, "mlp_gain": mlp_gain, "w_gate": w_gate, "w_up": w_up, "w_down": w_down, "cotangent": cotangent}


EPS = 1e-05
THETA = 1000000.0
PRECISE = lax.Precision.HIGHEST

@jax.custom_vjp
def reduced_copy(v):
    return lax.optimization_barrier(v.astype(jnp.bfloat16)).astype(jnp.float32)

@jax.custom_vjp
def reduced_gradient(v):
    return v

def low_keep(v):
    return (reduced_copy(v), None)

def low_pass(kept, grad):
    return (grad,)

def back_keep(v):
    return (v, None)

def back_low(kept, grad):
    return (reduced_copy(grad),)
reduced_copy.defvjp(low_keep, low_pass)
reduced_gradient.defvjp(back_keep, back_low)

def to_wide(array_item):
    return array_item.astype(jnp.float32)

def matrix_product(left_side, right_side):
    return jnp.dot(left_side, right_side, precision=PRECISE)

def normalize(value_rows, gain):
    return value_rows * lax.rsqrt(lax.optimization_barrier(jnp.mean(value_rows * value_rows, axis=-1, keepdims=True)) + EPS) * gain

def rotary_tables(position):
    half_width = HEAD_SIZE // 2
    frequency = THETA ** (-jnp.arange(half_width, dtype=jnp.float32) * 2.0 / HEAD_SIZE)
    angles = position.astype(jnp.float32)[:, None] * frequency[None, :]
    return (jnp.cos(angles), jnp.sin(angles))

def rotate(value_rows, cosine, sine_table):
    half_width = value_rows.shape[-1] // 2
    first_half = value_rows[..., :half_width]
    second_half = value_rows[..., half_width:]
    cosine = cosine[:, None, :]
    sine_table = sine_table[:, None, :]
    return jnp.concatenate([first_half * cosine - second_half * sine_table, second_half * cosine + first_half * sine_table], axis=-1)

def attend(block_arrays):
    query_rows, keys_rotated, value_rows_reduced, segment_row = block_arrays
    keys_expanded = jnp.repeat(keys_rotated, QUERY_HEADS // KEY_VALUE_HEADS, axis=1)
    values_expanded = jnp.repeat(value_rows_reduced, QUERY_HEADS // KEY_VALUE_HEADS, axis=1)
    scores = reduced_gradient(jnp.einsum('qhd,khd->hqk', query_rows, keys_expanded, precision=PRECISE) * HEAD_SIZE ** (-0.5))
    row_index = jnp.arange(GROUP_TOKENS, dtype=jnp.int32)
    allowed = (segment_row[:, None] == segment_row[None, :]) & (row_index[:, None] >= row_index[None, :])
    masked = jnp.where(allowed[None], scores, -1e+30)
    row_peak = lax.optimization_barrier(jnp.max(masked, axis=-1, keepdims=True))
    weights = jnp.exp(masked - row_peak)
    probs = reduced_copy(weights / lax.optimization_barrier(jnp.sum(weights, axis=-1, keepdims=True)))
    return jnp.einsum('hqk,khd->qhd', probs, values_expanded, precision=PRECISE)

def reference(tokens, lengths, attn_gain, w_query, key_weight, value_weight, query_gain, key_gain, w_output, mlp_gain, w_gate, w_up, w_down, cotangent):
    row_index = jnp.arange(GROUP_TOKENS, dtype=jnp.int32)
    seq_ends = jnp.cumsum(lengths, axis=1).astype(jnp.int32)
    segment_index = lax.optimization_barrier(jnp.sum((row_index[None, :, None] >= seq_ends[:, None, :]).astype(jnp.int32), axis=2)).astype(jnp.int32)
    starts = (seq_ends - lengths).astype(jnp.int32)
    choose = segment_index[:, :, None] == jnp.arange(DOC_DEV, dtype=jnp.int32)[None, None, :]
    picked = lax.optimization_barrier(jnp.sum(jnp.where(choose, starts[:, None, :], 0), axis=2)).astype(jnp.int32)
    position = (row_index[None, :] - picked).reshape(-1)
    cosine, sine_table = rotary_tables(position)

    def forward(resid, gain_one, query_w, key_matrix, value_matrix, query_g, key_g, output_w, gain_two, gate_w, up_w, down_w):
        first_normed_input = reduced_copy(normalize(resid, gain_one))
        query_raw = reduced_gradient(matrix_product(first_normed_input, query_w)).reshape(-1, QUERY_HEADS, HEAD_SIZE)
        key_unrotated = reduced_gradient(matrix_product(first_normed_input, key_matrix)).reshape(-1, KEY_VALUE_HEADS, HEAD_SIZE)
        value_rows = reduced_copy(reduced_gradient(matrix_product(first_normed_input, value_matrix))).reshape(-1, KEY_VALUE_HEADS, HEAD_SIZE)
        query_rows = reduced_copy(rotate(normalize(query_raw, query_g), cosine, sine_table))
        keys_rotated = reduced_copy(rotate(normalize(key_unrotated, key_g), cosine, sine_table))
        layer_blocks = (query_rows.reshape(N_DP, GROUP_TOKENS, QUERY_HEADS, HEAD_SIZE), keys_rotated.reshape(N_DP, GROUP_TOKENS, KEY_VALUE_HEADS, HEAD_SIZE), value_rows.reshape(N_DP, GROUP_TOKENS, KEY_VALUE_HEADS, HEAD_SIZE), segment_index)
        attended = lax.map(jax.checkpoint(attend), layer_blocks).reshape(-1, QUERY_HEADS * HEAD_SIZE)
        heads_out = reduced_copy(reduced_gradient(attended))
        hidden = resid + reduced_gradient(matrix_product(heads_out, output_w))
        normed_two = reduced_copy(normalize(hidden, gain_two))
        gate_proj = reduced_gradient(matrix_product(normed_two, gate_w))
        up_proj = reduced_gradient(matrix_product(normed_two, up_w))
        activation = reduced_copy(jax.nn.silu(gate_proj) * up_proj)
        return hidden + matrix_product(activation, down_w)
    inputs_wide = tuple((to_wide(array_item) for array_item in (tokens, attn_gain, w_query, key_weight, value_weight, query_gain, key_gain, w_output, mlp_gain, w_gate, w_up, w_down)))
    block_out, pullback = jax.vjp(forward, *inputs_wide)
    gradients = pullback(to_wide(cotangent))
    return (block_out.astype(jnp.bfloat16), gradients[0].astype(jnp.bfloat16), gradients[1], gradients[2], gradients[3], gradients[4], gradients[5], gradients[6], gradients[7], gradients[8], gradients[9], gradients[10], gradients[11])
```

```python
import functools
import jax
import jax.numpy as jnp
from jax import lax
from jax.experimental import pallas as pl
from jax.experimental.pallas import tpu as pltpu
from jax.sharding import PartitionSpec as P

HEAD_SIZE = 64
MESH = pl.DeviceIdType.MESH


def add_into(out, parts, step):
    lead = out.shape[0]
    rows = out.shape[1]
    per = rows // step

    def add_step(i, _):
        b = i // per
        r = pl.multiple_of((i % per) * step, 16)
        total = parts[0][b, pl.ds(r, step), :].astype(jnp.float32)
        for part in parts[1:]:
            total = total + part[b, pl.ds(r, step), :].astype(jnp.float32)
        out[b, pl.ds(r, step), :] = total.astype(jnp.bfloat16)
        return 0

    lax.fori_loop(0, lead * per, add_step, 0)


COPIES = ("t1p", "t1m", "i1p", "i1m", "m1p", "m1m", "t2p", "t2m", "i2p", "i2m", "m2p", "m2m", "y", "a2p", "a2m", "f2p", "f2m", "a1p", "a1m", "f1p", "f1m")
KEYS = len(COPIES)


class Chunk:
    def __init__(self, src, dst, t1, r1, m1, s1, t2, r2, m2, s2, yb, send, recv, step, where):
        self.src, self.dst = src, dst
        self.t1, self.r1, self.m1, self.s1 = t1, r1, m1, s1
        self.t2, self.r2, self.m2, self.s2, self.yb = t2, r2, m2, s2, yb
        self.send, self.recv, self.step = send, recv, step
        y, z, x = where
        self.where = where

        def dev(yy, zz, xx):
            return {"dp": (yy * 4 + zz) * 4 + xx}

        up = lambda v: lax.rem(v + 1, 4)
        down = lambda v: lax.rem(v + 3, 4)
        xp, xm = dev(y, z, up(x)), dev(y, z, down(x))
        zp, zm = dev(y, up(z), x), dev(y, down(z), x)
        self.ynb = dev(1 - y, z, x)
        self.first = ((x, xp, xm), (z, zp, zm))
        self.second = ((z, zp, zm), (x, xp, xm))
        self.live = {}

    def go(self, h, name, src, dst, device):
        k = h * KEYS + COPIES.index(name)
        c = pltpu.make_async_remote_copy(
            src_ref=src, dst_ref=dst, send_sem=self.send.at[k], recv_sem=self.recv.at[k],
            device_id=device, device_id_type=MESH)
        c.start()
        self.live[h, name] = c

    def got(self, h, *names):
        for n in names:
            self.live[h, n].wait_recv()

    def start1(self):
        for h in range(2):
            p, plus, minus = self.first[h]
            k2, kp, km = lax.rem(p + 2, 4), lax.rem(p + 1, 4), lax.rem(p + 3, 4)
            H, T, R = self.src.at[h], self.t1.at[h], self.r1.at[h]
            self.go(h, "t1p", H.at[k2, pl.ds(0, 2)], T.at[0], plus)
            self.go(h, "t1m", H.at[k2, pl.ds(2, 2)], T.at[1], minus)
            self.go(h, "i1p", H.at[kp, pl.ds(2, 2)], R.at[0, pl.ds(2, 2)], plus)
            self.go(h, "i1m", H.at[km, pl.ds(0, 2)], R.at[1, pl.ds(0, 2)], minus)

    def mid1(self):
        for h in range(2):
            p, plus, minus = self.first[h]
            kp, km = lax.rem(p + 1, 4), lax.rem(p + 3, 4)
            H, T, R, M = self.src.at[h], self.t1.at[h], self.r1.at[h], self.m1.at[h]
            self.got(h, "t1p")
            add_into(M.at[0], (H.at[kp, pl.ds(0, 2)], T.at[0]), self.step)
            self.go(h, "m1p", M.at[0], R.at[0, pl.ds(0, 2)], plus)
            self.got(h, "t1m")
            add_into(M.at[1], (H.at[km, pl.ds(2, 2)], T.at[1]), self.step)
            self.go(h, "m1m", M.at[1], R.at[1, pl.ds(2, 2)], minus)

    def fin1(self):
        for h in range(2):
            p = self.first[h][0]
            R = self.r1.at[h]
            self.got(h, "i1p", "i1m", "m1p", "m1m")
            add_into(self.s1.at[h], (self.src.at[h, p], R.at[0], R.at[1]), self.step)
            p, plus, minus = self.second[h]
            k2, kp, km = lax.rem(p + 2, 4), lax.rem(p + 1, 4), lax.rem(p + 3, 4)
            H, T, R = self.s1.at[h], self.t2.at[h], self.r2.at[h]
            half = T.shape[1]
            lo, hi = pl.ds(0, half), pl.ds(half, half)
            self.go(h, "t2p", H.at[k2, lo], T.at[0], plus)
            self.go(h, "t2m", H.at[k2, hi], T.at[1], minus)
            self.go(h, "i2p", H.at[kp, hi], R.at[0, hi], plus)
            self.go(h, "i2m", H.at[km, lo], R.at[1, lo], minus)

    def mid2(self):
        for h in range(2):
            p, plus, minus = self.second[h]
            kp, km = lax.rem(p + 1, 4), lax.rem(p + 3, 4)
            H, T, R, M = self.s1.at[h], self.t2.at[h], self.r2.at[h], self.m2.at[h]
            half = T.shape[1]
            lo, hi = pl.ds(0, half), pl.ds(half, half)
            step = min(self.step, half)
            self.got(h, "t2p")
            add_into(M.at[pl.ds(0, 1)], (H.at[pl.ds(kp, 1), lo], T.at[pl.ds(0, 1)]), step)
            self.go(h, "m2p", M.at[0], R.at[0, lo], plus)
            self.got(h, "t2m")
            add_into(M.at[pl.ds(1, 1)], (H.at[pl.ds(km, 1), hi], T.at[pl.ds(1, 1)]), step)
            self.go(h, "m2m", M.at[1], R.at[1, hi], minus)

    def fin2(self):
        for h in range(2):
            p = self.second[h][0]
            R = self.r2.at[h]
            self.got(h, "i2p", "i2m", "m2p", "m2m")
            add_into(self.s2.at[pl.ds(h, 1)], (self.s1.at[h, pl.ds(p, 1)], R.at[pl.ds(0, 1)], R.at[pl.ds(1, 1)]), self.step)
            self.go(h, "y", self.s2.at[h], self.yb.at[h], self.ynb)

    def finy(self):
        for h in range(2):
            a = self.first[h][0]
            p, plus, minus = self.second[h]
            self.got(h, "y")
            add_into(self.dst.at[h, a, pl.ds(p, 1)], (self.s2.at[pl.ds(h, 1)], self.yb.at[pl.ds(h, 1)]), self.step)
            blk = self.dst.at[h, a, p]
            self.go(h, "a2p", blk, blk, plus)
            self.go(h, "a2m", blk, blk, minus)

    def ag2(self):
        for h in range(2):
            a = self.first[h][0]
            p, plus, minus = self.second[h]
            kp, km = lax.rem(p + 1, 4), lax.rem(p + 3, 4)
            half = self.t2.shape[2]
            self.got(h, "a2p")
            blk = self.dst.at[h, a, km, pl.ds(0, half)]
            self.go(h, "f2p", blk, blk, plus)
            self.got(h, "a2m")
            blk = self.dst.at[h, a, kp, pl.ds(half, half)]
            self.go(h, "f2m", blk, blk, minus)

    def ag1s(self):
        for h in range(2):
            p, plus, minus = self.first[h]
            self.got(h, "f2p", "f2m")
            blk = self.dst.at[h, p]
            self.go(h, "a1p", blk, blk, plus)
            self.go(h, "a1m", blk, blk, minus)

    def ag1(self):
        for h in range(2):
            p, plus, minus = self.first[h]
            kp, km = lax.rem(p + 1, 4), lax.rem(p + 3, 4)
            self.got(h, "a1p")
            blk = self.dst.at[h, km, pl.ds(0, 2)]
            self.go(h, "f1p", blk, blk, plus)
            self.got(h, "a1m")
            blk = self.dst.at[h, kp, pl.ds(2, 2)]
            self.go(h, "f1m", blk, blk, minus)

    def end(self):
        for h in range(2):
            self.got(h, "f1p", "f1m")
        for c in self.live.values():
            c.wait_send()

    def stages(self):
        return [self.start1, self.mid1, self.fin1, self.mid2, self.fin2, self.finy, self.ag2, self.ag1s, self.ag1, self.end]


def run_chunks(chunks, lag=2):
    todo = [c.stages() for c in chunks]
    last = max(lag * i + len(t) for i, t in enumerate(todo))
    for t in range(last):
        ready = [(i, t - lag * i) for i in range(len(todo)) if 0 <= t - lag * i < len(todo[i])]
        for i, s in ready:
            if s == 0:
                todo[i][s]()
        for i, s in ready:
            if s > 0:
                todo[i][s]()


def coords():
    d = lax.axis_index("dp")
    return d // 16, (d // 4) % 4, d % 4


def scratch_for(shape):
    _, _, _, R, C = shape
    bf = jnp.bfloat16
    return [
        pltpu.VMEM((2, 2, 2, R, C), bf), pltpu.VMEM((2, 2, 4, R, C), bf), pltpu.VMEM((2, 2, 2, R, C), bf), pltpu.VMEM((2, 4, R, C), bf),
        pltpu.VMEM((2, 2, R // 2, C), bf), pltpu.VMEM((2, 2, R, C), bf), pltpu.VMEM((2, 2, R // 2, C), bf), pltpu.VMEM((2, R, C), bf), pltpu.VMEM((2, R, C), bf),
        pltpu.SemaphoreType.DMA((2 * KEYS,)), pltpu.SemaphoreType.DMA((2 * KEYS,)),
    ]

NS = 11

def enter(y, z, x):
    barrier = pltpu.get_barrier_semaphore()
    peers = [(y, z, lax.rem(x + i, 4)) for i in (1, 2, 3)] + [(y, lax.rem(z + i, 4), x) for i in (1, 2, 3)] + [(1 - y, z, x)]
    for a, b, c in peers:
        pl.semaphore_signal(barrier, inc=1, device_id={"dp": (a * 4 + b) * 4 + c}, device_id_type=MESH)
    pl.semaphore_wait(barrier, len(peers))


def small_sum(where, vec, out, slots, mine, send, recv):
    y, z, x = where
    value = vec[...]
    for s, (p, n, dev) in enumerate((
        (x, 4, lambda v: (y * 4 + z) * 4 + v), (z, 4, lambda v: (y * 4 + v) * 4 + x), (y, 2, lambda v: (v * 4 + z) * 4 + x))):
        mine[s] = value
        slots[s, p] = value
        cs = []
        for i in range(1, n):
            k = s * 3 + i - 1
            c = pltpu.make_async_remote_copy(
                src_ref=mine.at[s], dst_ref=slots.at[s, p], send_sem=send.at[k], recv_sem=recv.at[k],
                device_id={"dp": dev(lax.rem(p + i, n))}, device_id_type=MESH)
            c.start()
            cs.append(c)
        for c in cs:
            c.wait()
        value = slots[s, 0]
        for i in range(1, n):
            value = value + slots[s, i]
    out[...] = value


def reduce_kernel(n, steps, *refs):
    ins, vec = refs[:n], refs[n]
    outs, vout = refs[n + 1:2 * n + 1], refs[2 * n + 1]
    rest = refs[2 * n + 2:]
    where = coords()
    enter(*where)
    chunks = [Chunk(ins[i], outs[i], *rest[NS * i:NS * i + NS], steps[i], where) for i in range(n)]
    if vec is not None:
        small_sum(where, vec, vout, *rest[NS * n:])
    run_chunks(chunks)


def all_reduce(arrays, vec):
    n = len(arrays)
    shapes = [a.shape for a in arrays]
    steps = [16 if s[-1] > 128 else s[-2] // 2 for s in shapes]
    V = pl.BlockSpec(memory_space=pltpu.VMEM)
    scratch = sum([scratch_for(s) for s in shapes], [])
    scratch += [pltpu.VMEM((3, 4) + vec.shape, jnp.float32), pltpu.VMEM((3,) + vec.shape, jnp.float32),
                pltpu.SemaphoreType.DMA((9,)), pltpu.SemaphoreType.DMA((9,))]
    return pl.pallas_call(
        functools.partial(reduce_kernel, n, steps),
        out_shape=[jax.ShapeDtypeStruct(s, jnp.bfloat16) for s in shapes] + [jax.ShapeDtypeStruct(vec.shape, jnp.float32)],
        in_specs=[V] * (n + 1), out_specs=[V] * (n + 1), scratch_shapes=scratch,
        compiler_params=pltpu.CompilerParams(collective_id=0, has_side_effects=True, vmem_limit_bytes=60 * 1024 * 1024),
        name="dp_sum",
    )(*arrays, vec)


def tensor_place():
    t = lax.axis_index("tensor")
    core, side = lax.rem(t, 2), t // 2
    return side, core, side * 2 + (1 - core), (1 - side) * 2 + core


def send(src, dst, sems, k, peer):
    c = pltpu.make_async_remote_copy(
        src_ref=src, dst_ref=dst, send_sem=sems[0].at[k], recv_sem=sems[1].at[k],
        device_id={"tensor": peer}, device_id_type=MESH)
    c.start()
    return c


def greet(sib, far):
    barrier = pltpu.get_barrier_semaphore()
    for peer in (sib, far):
        pl.semaphore_signal(barrier, inc=1, device_id={"tensor": peer}, device_id_type=MESH)
    pl.semaphore_wait(barrier, 2)


def columns(block):
    return pl.ds(pl.multiple_of(block * 256, 256), 256)


def gather_kernel(a, b, oa, ob, s_sem, r_sem):
    side, core, sib, far = tensor_place()
    me = side * 2 + core
    sems = (s_sem, r_sem)
    greet(sib, far)
    first = []
    for i, (v, o) in enumerate(((a, oa), (b, ob))):
        there = o.at[:, columns(me)]
        first.append((send(v, there, sems, 3 * i, far), send(v, there, sems, 3 * i + 1, sib)))
    for v, o in ((a, oa), (b, ob)):
        o[:, columns(me)] = v[...]
    passed = []
    for i, o in enumerate((oa, ob)):
        first[i][0].wait_recv()
        there = o.at[:, columns(far)]
        passed.append(send(there, there, sems, 3 * i + 2, sib))
    for i in range(2):
        first[i][0].wait_send()
        first[i][1].wait()
        passed[i].wait()


def gather_pair(a, b):
    V = pl.BlockSpec(memory_space=pltpu.VMEM)
    shape = jax.ShapeDtypeStruct((a.shape[0], 4 * a.shape[1]), a.dtype)
    return pl.pallas_call(
        gather_kernel, out_shape=[shape, shape], in_specs=[V, V], out_specs=[V, V],
        scratch_shapes=[pltpu.SemaphoreType.DMA((6,)), pltpu.SemaphoreType.DMA((6,))],
        compiler_params=pltpu.CompilerParams(collective_id=1, has_side_effects=True), name="gather_pair",
    )(a, b)


def sum_steps(part, out, low, near, mid, away, sems, base, place, scatter):
    side, core, sib, far = place
    live = []

    def one():
        low[...] = part[...].astype(jnp.bfloat16)
        for s in range(2):
            live.append(send(low.at[:, columns(s * 2 + 1 - core)], near.at[s], sems, base + s, sib))

    def two():
        order = (1 - side, side)
        for s in range(2):
            live[s].wait_recv()
        for i, s in enumerate(order):
            mid[s] = (low[:, columns(s * 2 + core)].astype(jnp.float32) + near[s].astype(jnp.float32)).astype(jnp.bfloat16)
            if i == 0 or not scatter:
                live.append(send(mid.at[s], away.at[s], sems, base + 2 + i, far))

    def three():
        if scatter:
            live[2].wait_recv()
            out[...] = mid[side].astype(jnp.float32) + away[side].astype(jnp.float32)
            return
        for i, s in enumerate((1 - side, side)):
            live[2 + i].wait_recv()
        for i, s in enumerate((1 - side, side)):
            there = out.at[:, columns(s * 2 + core)]
            out[:, columns(s * 2 + core)] = (mid[s].astype(jnp.float32) + away[s].astype(jnp.float32)).astype(jnp.bfloat16)
            live.append(send(there, there, sems, base + 4 + i, sib))

    def four():
        for c in live[4:]:
            c.wait_recv()
        for c in live:
            c.wait_send()

    return [one, two, three, four]


def sums_kernel(kinds, *refs):
    n = len(kinds)
    ins, outs, rest = refs[:n], refs[n:2 * n], refs[2 * n:]
    sems = rest[-2:]
    place = tensor_place()
    side, core, sib, far = place
    greet(sib, far)
    plans = []
    for i, kind in enumerate(kinds):
        if kind == "small":
            near, mid, away = rest[4 * i + 1:4 * i + 4]
            hold = []

            def one(v=ins[i], near=near, k=6 * i, hold=hold):
                hold.append(send(v, near, sems, k, sib))

            def two(v=ins[i], near=near, mid=mid, away=away, k=6 * i, hold=hold):
                hold[0].wait()
                mid[...] = v[...] + near[...]
                hold.append(send(mid, away, sems, k + 1, far))

            def three(o=outs[i], mid=mid, away=away, hold=hold):
                hold[1].wait()
                o[...] = mid[...] + away[...]

            plans.append([one, two, three, lambda: None])
        else:
            plans.append(sum_steps(ins[i], outs[i], *rest[4 * i:4 * i + 4], sems, 6 * i, place, kind == "own"))
    for step in range(4):
        for plan in plans:
            plan[step]()


def tensor_sums(arrays, kinds, collective_id):
    V = pl.BlockSpec(memory_space=pltpu.VMEM)
    out_shape, scratch = [], []
    for a, kind in zip(arrays, kinds):
        r, w = a.shape
        if kind == "small":
            out_shape.append(jax.ShapeDtypeStruct((r, w), jnp.float32))
            scratch += [pltpu.VMEM((r, w), jnp.float32)] * 4
        else:
            out_shape.append(jax.ShapeDtypeStruct((r, w), jnp.bfloat16) if kind == "all" else jax.ShapeDtypeStruct((r, w // 4), jnp.float32))
            scratch += [pltpu.VMEM((r, w), jnp.bfloat16)] + [pltpu.VMEM((2, r, w // 4), jnp.bfloat16)] * 3
    n = len(arrays)
    scratch += [pltpu.SemaphoreType.DMA((6 * n,)), pltpu.SemaphoreType.DMA((6 * n,))]
    return pl.pallas_call(
        functools.partial(sums_kernel, kinds), out_shape=out_shape, in_specs=[V] * n, out_specs=[V] * n,
        scratch_shapes=scratch,
        compiler_params=pltpu.CompilerParams(collective_id=collective_id, has_side_effects=True), name="tensor_sums",
    )(*arrays)


EPS = 1e-05
THETA = 1000000.0


def dot_rows(left_side, right_side):
    return lax.dot_general(
        left_side, right_side, (((0,), (0,)), ((), ())), preferred_element_type=jnp.float32
    )


def dot_last(left_side, right_side):
    return lax.dot_general(
        left_side, right_side, (((1,), (1,)), ((), ())), preferred_element_type=jnp.float32
    )


def layout(row_lengths, row_count):
    row_index = jnp.arange(row_count, dtype=jnp.int32)
    seq_ends = jnp.cumsum(row_lengths)
    segment_index = jnp.sum((row_index[:, None] >= seq_ends[None, :]).astype(jnp.int32), axis=1)
    starts = seq_ends - row_lengths
    choose = segment_index[:, None] == jnp.arange(row_lengths.shape[0], dtype=jnp.int32)[None, :]
    picked = jnp.sum(jnp.where(choose, starts[None, :], 0), axis=1)
    return (segment_index, row_index - picked)


def rotary_tables(position):
    half_width = HEAD_SIZE // 2
    frequency = THETA ** (-jnp.arange(half_width, dtype=jnp.float32) * 2.0 / HEAD_SIZE)
    angles = position.astype(jnp.float32)[:, None] * frequency[None, :]
    return (jnp.cos(angles), jnp.sin(angles))


def rotate(value_rows, cosine, sine_table):
    half_width = value_rows.shape[-1] // 2
    first_half = value_rows[..., :half_width]
    second_half = value_rows[..., half_width:]
    cosine = cosine[:, None, :]
    sine_table = sine_table[:, None, :]
    return jnp.concatenate(
        [
            first_half * cosine - second_half * sine_table,
            second_half * cosine + first_half * sine_table,
        ],
        axis=-1,
    )


def norm_back(upstream, plain_values, inverse):
    return inverse * (
        upstream - plain_values * jnp.mean(upstream * plain_values, axis=-1, keepdims=True)
    )


def body(
    tokens,
    lengths,
    attn_gain,
    w_query,
    key_weight,
    value_weight,
    query_gain,
    key_gain,
    w_output,
    mlp_gain,
    w_gate,
    w_up,
    w_down,
    cotangent,
):
    score_scale = HEAD_SIZE ** (-0.5)
    whole_tokens, whole_cot = gather_pair(tokens, cotangent)
    row_count = whole_tokens.shape[0]
    head_count = w_query.shape[1] // HEAD_SIZE
    groups = key_weight.shape[1] // HEAD_SIZE
    shared = head_count // groups
    segment_index, position = layout(lengths[0], row_count)
    row_index = jnp.arange(row_count, dtype=jnp.int32)
    allowed = (
        (segment_index[:, None] == segment_index[None, :])
        & (row_index[:, None] >= row_index[None, :])
    )[None, None]
    cosine, sine_table = rotary_tables(position)
    resid = whole_tokens.astype(jnp.float32)
    inverse_one = lax.rsqrt(jnp.mean(resid * resid, axis=-1, keepdims=True) + EPS)
    plain_one = resid * inverse_one
    first_normed_input = (plain_one * attn_gain).astype(jnp.bfloat16)
    query_raw = jnp.dot(first_normed_input, w_query, preferred_element_type=jnp.float32).reshape(
        row_count, head_count, HEAD_SIZE
    )
    key_unrotated = jnp.dot(
        first_normed_input, key_weight, preferred_element_type=jnp.float32
    ).reshape(row_count, groups, HEAD_SIZE)
    value_low = (
        jnp.dot(first_normed_input, value_weight, preferred_element_type=jnp.float32)
        .astype(jnp.bfloat16)
        .reshape(row_count, groups, HEAD_SIZE)
    )
    query_inverse = lax.rsqrt(jnp.mean(query_raw * query_raw, axis=-1, keepdims=True) + EPS)
    query_plain = query_raw * query_inverse
    query_low = (
        rotate(query_plain * query_gain, cosine, sine_table)
        .astype(jnp.bfloat16)
        .reshape(row_count, groups, shared, HEAD_SIZE)
    )
    key_inverse = lax.rsqrt(jnp.mean(key_unrotated * key_unrotated, axis=-1, keepdims=True) + EPS)
    key_plain = key_unrotated * key_inverse
    key_low = rotate(key_plain * key_gain, cosine, sine_table).astype(jnp.bfloat16)

    def score_block():
        raw_scores = (
            jnp.einsum("qjgd,kjd->jgqk", query_low, key_low, preferred_element_type=jnp.float32)
            * score_scale
        )
        return jnp.where(allowed, raw_scores, -1e30)

    scores = score_block()
    row_peak = jnp.max(scores, axis=-1, keepdims=True)
    weights = jnp.exp(scores - row_peak)
    denominator = jnp.sum(weights, axis=-1, keepdims=True)
    probs_low = (weights / denominator).astype(jnp.bfloat16)
    log_total = row_peak + jnp.log(denominator)
    heads_out = (
        jnp.einsum("jgqk,kjd->qjgd", probs_low, value_low, preferred_element_type=jnp.float32)
        .astype(jnp.bfloat16)
        .reshape(row_count, head_count * HEAD_SIZE)
    )
    attn_part = jnp.dot(heads_out, w_output, preferred_element_type=jnp.float32)
    hidden = resid + tensor_sums([attn_part], ("all",), 2)[0].astype(jnp.float32)
    inverse_two = lax.rsqrt(jnp.mean(hidden * hidden, axis=-1, keepdims=True) + EPS)
    plain_two = hidden * inverse_two
    normed_two = (plain_two * mlp_gain).astype(jnp.bfloat16)
    gate_proj = jnp.dot(normed_two, w_gate, preferred_element_type=jnp.float32)
    up_proj = jnp.dot(normed_two, w_up, preferred_element_type=jnp.float32)
    gate_sigmoid = jax.nn.sigmoid(gate_proj)
    activation = (gate_proj * gate_sigmoid * up_proj).astype(jnp.bfloat16)
    mlp_part = jnp.dot(activation, w_down, preferred_element_type=jnp.float32)
    own_width = tokens.shape[1]
    column = lax.axis_index("tensor") * own_width
    w_down_grad = dot_rows(activation, whole_cot).astype(jnp.bfloat16)
    w_down_blocks = w_down_grad.reshape(1152, 8, 128).transpose(1, 0, 2).reshape(2, 4, 4, 288, 128)
    d_act = dot_last(whole_cot, w_down)
    d_gate_low = (d_act * up_proj * gate_sigmoid * (1.0 + gate_proj * (1.0 - gate_sigmoid))).astype(
        jnp.bfloat16
    )
    d_up_low = (d_act * gate_proj * gate_sigmoid).astype(jnp.bfloat16)
    w_gate_grad = dot_rows(normed_two, d_gate_low)
    w_up_grad = dot_rows(normed_two, d_up_low)
    d_two_part = dot_last(d_gate_low, w_gate) + dot_last(d_up_low, w_up)
    d_two, mlp_own = tensor_sums([d_two_part, mlp_part], ("all", "own"), 3)
    d_two = d_two.astype(jnp.float32)
    block_out = (lax.dynamic_slice_in_dim(hidden, column, own_width, 1) + mlp_own).astype(
        jnp.bfloat16
    )
    mlp_gain_grad = jnp.sum(d_two * plain_two, axis=0)
    d_hidden = whole_cot.astype(jnp.float32) + norm_back(d_two * mlp_gain, plain_two, inverse_two)
    d_hidden_low = d_hidden.astype(jnp.bfloat16)
    w_output_turned = dot_rows(d_hidden_low, heads_out)
    d_heads = (
        dot_last(d_hidden_low, w_output)
        .astype(jnp.bfloat16)
        .reshape(row_count, groups, shared, HEAD_SIZE)
    )
    probs = jnp.exp(score_block() - log_total)
    probs_back = probs.astype(jnp.bfloat16)
    d_value_low = (
        jnp.einsum("jgqk,qjgd->kjd", probs_back, d_heads, preferred_element_type=jnp.float32)
        .astype(jnp.bfloat16)
        .reshape(row_count, groups * HEAD_SIZE)
    )
    d_probs = jnp.einsum("qjgd,kjd->jgqk", d_heads, value_low, preferred_element_type=jnp.float32)
    d_scores_low = (probs * (d_probs - jnp.sum(d_probs * probs, axis=-1, keepdims=True))).astype(
        jnp.bfloat16
    )
    d_query_post = (
        jnp.einsum(
            "jgqk,kjd->qjgd", d_scores_low, key_low, preferred_element_type=jnp.float32
        ).reshape(row_count, head_count, HEAD_SIZE)
        * score_scale
    )
    d_key_post = (
        jnp.einsum("jgqk,qjgd->kjd", d_scores_low, query_low, preferred_element_type=jnp.float32)
        * score_scale
    )
    d_query_turn = rotate(d_query_post, cosine, -sine_table)
    d_key_turn = rotate(d_key_post, cosine, -sine_table)
    query_gain_part = jnp.sum(d_query_turn * query_plain, axis=(0, 1))
    key_gain_part = jnp.sum(d_key_turn * key_plain, axis=(0, 1))
    d_query_low = (
        norm_back(d_query_turn * query_gain, query_plain, query_inverse)
        .astype(jnp.bfloat16)
        .reshape(row_count, head_count * HEAD_SIZE)
    )
    d_key_low = (
        norm_back(d_key_turn * key_gain, key_plain, key_inverse)
        .astype(jnp.bfloat16)
        .reshape(row_count, groups * HEAD_SIZE)
    )
    w_query_grad = dot_rows(first_normed_input, d_query_low)
    w_key_grad = dot_rows(first_normed_input, d_key_low)
    w_value_grad = dot_rows(first_normed_input, d_value_low)
    d_one_part = (
        dot_last(d_query_low, w_query)
        + dot_last(d_key_low, key_weight)
        + dot_last(d_value_low, value_weight)
    )
    gains = jnp.pad(jnp.concatenate([query_gain_part, key_gain_part])[None], ((0, 7), (0, 0)))
    d_one, gains = tensor_sums([d_one_part, gains], ("all", "small"), 4)
    d_one = d_one.astype(jnp.float32)
    attn_gain_grad = jnp.sum(d_one * plain_one, axis=0)
    d_input = d_hidden + norm_back(d_one * attn_gain, plain_one, inverse_one)
    input_grad = lax.dynamic_slice_in_dim(d_input, column, own_width, 1).astype(jnp.bfloat16)
    vec = jnp.concatenate([attn_gain_grad.reshape(8, 128), mlp_gain_grad.reshape(8, 128), gains], axis=0)
    attn_grads = jnp.concatenate([w_query_grad, w_key_grad, w_value_grad, w_output_turned], axis=1).astype(jnp.bfloat16)
    down, gate, up, attn, vec = all_reduce(
        [
            w_down_blocks,
            w_gate_grad.astype(jnp.bfloat16).reshape(2, 4, 4, 32, 1152),
            w_up_grad.astype(jnp.bfloat16).reshape(2, 4, 4, 32, 1152),
            attn_grads.reshape(2, 4, 4, 32, 768),
        ],
        vec,
    )
    attn = attn.reshape(1024, 768).astype(jnp.float32)
    return (
        block_out,
        input_grad,
        vec[:8].reshape(1024),
        attn[:, :256],
        attn[:, 256:384],
        attn[:, 384:512],
        vec[16, :64],
        vec[16, 64:],
        attn[:, 512:].T,
        vec[8:16].reshape(1024),
        gate.reshape(1024, 1152).astype(jnp.float32),
        up.reshape(1024, 1152).astype(jnp.float32),
        down.reshape(8, 1152, 128).transpose(1, 0, 2).reshape(1152, 1024).astype(jnp.float32),
    )


def solution(mesh):
    in_specs = (
        P("dp", "tensor"),
        P("dp", None),
        P(),
        P(None, "tensor"),
        P(None, "tensor"),
        P(None, "tensor"),
        P(),
        P(),
        P("tensor", None),
        P(),
        P(None, "tensor"),
        P(None, "tensor"),
        P("tensor", None),
        P("dp", "tensor"),
    )
    out_specs = (
        P("dp", "tensor"),
        P("dp", "tensor"),
        P(),
        P(None, "tensor"),
        P(None, "tensor"),
        P(None, "tensor"),
        P(),
        P(),
        P("tensor", None),
        P(),
        P(None, "tensor"),
        P(None, "tensor"),
        P("tensor", None),
    )
    return jax.shard_map(body, mesh=mesh, in_specs=in_specs, out_specs=out_specs, check_vma=False)
```

```python
import functools
import jax
import jax.numpy as jnp
from jax import lax
from jax.experimental import pallas as pl
from jax.experimental.pallas import tpu as pltpu
from jax.sharding import PartitionSpec as P

HEAD_SIZE = 64
MESH = pl.DeviceIdType.MESH


def add_into(out, parts, step):
    lead = out.shape[0]
    rows = out.shape[1]
    per = rows // step

    def add_step(i, _):
        b = i // per
        r = pl.multiple_of((i % per) * step, 16)
        total = parts[0][b, pl.ds(r, step), :].astype(jnp.float32)
        for part in parts[1:]:
            total = total + part[b, pl.ds(r, step), :].astype(jnp.float32)
        out[b, pl.ds(r, step), :] = total.astype(jnp.bfloat16)
        return 0

    lax.fori_loop(0, lead * per, add_step, 0)


(T1P, T1M, I1P, I1M, M1P, M1M, T2P, T2M, I2P, I2M, M2P, M2M, Y, A2P, A2M, F2P, F2M, A1P, A1M, F1P, F1M) = range(21)
KEYS = 21


class Chunk:
    def __init__(self, src, dst, t1, r1, m1, s1, t2, r2, m2, s2, yb, send, recv, step, where):
        self.src, self.dst = src, dst
        self.t1, self.r1, self.m1, self.s1 = t1, r1, m1, s1
        self.t2, self.r2, self.m2, self.s2, self.yb = t2, r2, m2, s2, yb
        self.send, self.recv, self.step = send, recv, step
        y, z, x = where
        self.where = where

        def dev(yy, zz, xx):
            return {"dp": (yy * 4 + zz) * 4 + xx}

        up = lambda v: lax.rem(v + 1, 4)
        down = lambda v: lax.rem(v + 3, 4)
        xp, xm = dev(y, z, up(x)), dev(y, z, down(x))
        zp, zm = dev(y, up(z), x), dev(y, down(z), x)
        self.ynb = dev(1 - y, z, x)
        self.first = ((x, xp, xm), (z, zp, zm))
        self.second = ((z, zp, zm), (x, xp, xm))
        self.live = {}

    def go(self, h, name, src, dst, device):
        k = h * KEYS + name
        c = pltpu.make_async_remote_copy(
            src_ref=src, dst_ref=dst, send_sem=self.send.at[k], recv_sem=self.recv.at[k],
            device_id=device, device_id_type=MESH)
        c.start()
        self.live[h, name] = c

    def got(self, h, *names):
        for n in names:
            self.live[h, n].wait_recv()

    def start1(self):
        for h in range(2):
            p, plus, minus = self.first[h]
            k2, kp, km = lax.rem(p + 2, 4), lax.rem(p + 1, 4), lax.rem(p + 3, 4)
            H, T, R = self.src.at[h], self.t1.at[h], self.r1.at[h]
            self.go(h, T1P, H.at[k2, pl.ds(0, 2)], T.at[0], plus)
            self.go(h, T1M, H.at[k2, pl.ds(2, 2)], T.at[1], minus)
            self.go(h, I1P, H.at[kp, pl.ds(2, 2)], R.at[0, pl.ds(2, 2)], plus)
            self.go(h, I1M, H.at[km, pl.ds(0, 2)], R.at[1, pl.ds(0, 2)], minus)

    def mid1(self):
        for h in range(2):
            p, plus, minus = self.first[h]
            kp, km = lax.rem(p + 1, 4), lax.rem(p + 3, 4)
            H, T, R, M = self.src.at[h], self.t1.at[h], self.r1.at[h], self.m1.at[h]
            self.got(h, T1P)
            add_into(M.at[0], (H.at[kp, pl.ds(0, 2)], T.at[0]), self.step)
            self.go(h, M1P, M.at[0], R.at[0, pl.ds(0, 2)], plus)
            self.got(h, T1M)
            add_into(M.at[1], (H.at[km, pl.ds(2, 2)], T.at[1]), self.step)
            self.go(h, M1M, M.at[1], R.at[1, pl.ds(2, 2)], minus)

    def fin1(self):
        for h in range(2):
            p = self.first[h][0]
            R = self.r1.at[h]
            self.got(h, I1P, I1M, M1P, M1M)
            add_into(self.s1.at[h], (self.src.at[h, p], R.at[0], R.at[1]), self.step)
            p, plus, minus = self.second[h]
            k2, kp, km = lax.rem(p + 2, 4), lax.rem(p + 1, 4), lax.rem(p + 3, 4)
            H, T, R = self.s1.at[h], self.t2.at[h], self.r2.at[h]
            half = T.shape[1]
            lo, hi = pl.ds(0, half), pl.ds(half, half)
            self.go(h, T2P, H.at[k2, lo], T.at[0], plus)
            self.go(h, T2M, H.at[k2, hi], T.at[1], minus)
            self.go(h, I2P, H.at[kp, hi], R.at[0, hi], plus)
            self.go(h, I2M, H.at[km, lo], R.at[1, lo], minus)

    def mid2(self):
        for h in range(2):
            p, plus, minus = self.second[h]
            kp, km = lax.rem(p + 1, 4), lax.rem(p + 3, 4)
            H, T, R, M = self.s1.at[h], self.t2.at[h], self.r2.at[h], self.m2.at[h]
            half = T.shape[1]
            lo, hi = pl.ds(0, half), pl.ds(half, half)
            step = min(self.step, half)
            self.got(h, T2P)
            add_into(M.at[pl.ds(0, 1)], (H.at[pl.ds(kp, 1), lo], T.at[pl.ds(0, 1)]), step)
            self.go(h, M2P, M.at[0], R.at[0, lo], plus)
            self.got(h, T2M)
            add_into(M.at[pl.ds(1, 1)], (H.at[pl.ds(km, 1), hi], T.at[pl.ds(1, 1)]), step)
            self.go(h, M2M, M.at[1], R.at[1, hi], minus)

    def fin2(self):
        for h in range(2):
            p = self.second[h][0]
            R = self.r2.at[h]
            self.got(h, I2P, I2M, M2P, M2M)
            add_into(self.s2.at[pl.ds(h, 1)], (self.s1.at[h, pl.ds(p, 1)], R.at[pl.ds(0, 1)], R.at[pl.ds(1, 1)]), self.step)
            self.go(h, Y, self.s2.at[h], self.yb.at[h], self.ynb)

    def finy(self):
        for h in range(2):
            a = self.first[h][0]
            p, plus, minus = self.second[h]
            self.got(h, Y)
            add_into(self.dst.at[h, a, pl.ds(p, 1)], (self.s2.at[pl.ds(h, 1)], self.yb.at[pl.ds(h, 1)]), self.step)
            blk = self.dst.at[h, a, p]
            self.go(h, A2P, blk, blk, plus)
            self.go(h, A2M, blk, blk, minus)

    def ag2(self):
        for h in range(2):
            a = self.first[h][0]
            p, plus, minus = self.second[h]
            kp, km = lax.rem(p + 1, 4), lax.rem(p + 3, 4)
            half = self.t2.shape[2]
            self.got(h, A2P)
            blk = self.dst.at[h, a, km, pl.ds(0, half)]
            self.go(h, F2P, blk, blk, plus)
            self.got(h, A2M)
            blk = self.dst.at[h, a, kp, pl.ds(half, half)]
            self.go(h, F2M, blk, blk, minus)

    def ag1s(self):
        for h in range(2):
            p, plus, minus = self.first[h]
            self.got(h, F2P, F2M)
            blk = self.dst.at[h, p]
            self.go(h, A1P, blk, blk, plus)
            self.go(h, A1M, blk, blk, minus)

    def ag1(self):
        for h in range(2):
            p, plus, minus = self.first[h]
            kp, km = lax.rem(p + 1, 4), lax.rem(p + 3, 4)
            self.got(h, A1P)
            blk = self.dst.at[h, km, pl.ds(0, 2)]
            self.go(h, F1P, blk, blk, plus)
            self.got(h, A1M)
            blk = self.dst.at[h, kp, pl.ds(2, 2)]
            self.go(h, F1M, blk, blk, minus)

    def end(self):
        for h in range(2):
            self.got(h, F1P, F1M)
        for c in self.live.values():
            c.wait_send()

    def stages(self):
        return [self.start1, self.mid1, self.fin1, self.mid2, self.fin2, self.finy, self.ag2, self.ag1s, self.ag1, self.end]


def coords():
    d = lax.axis_index("dp")
    return d // 16, (d // 4) % 4, d % 4


def scratch_for(shape):
    _, _, _, R, C = shape
    bf = jnp.bfloat16
    return [
        pltpu.VMEM((2, 2, 2, R, C), bf), pltpu.VMEM((2, 2, 4, R, C), bf), pltpu.VMEM((2, 2, 2, R, C), bf), pltpu.VMEM((2, 4, R, C), bf),
        pltpu.VMEM((2, 2, R // 2, C), bf), pltpu.VMEM((2, 2, R, C), bf), pltpu.VMEM((2, 2, R // 2, C), bf), pltpu.VMEM((2, R, C), bf), pltpu.VMEM((2, R, C), bf),
        pltpu.SemaphoreType.DMA((2 * KEYS,)), pltpu.SemaphoreType.DMA((2 * KEYS,)),
    ]

NS = 11

def tensor_place():
    t = lax.axis_index("tensor")
    core, side = lax.rem(t, 2), t // 2
    return side, core, side * 2 + (1 - core), (1 - side) * 2 + core


def send(src, dst, sems, k, peer):
    c = pltpu.make_async_remote_copy(
        src_ref=src, dst_ref=dst, send_sem=sems[0].at[k], recv_sem=sems[1].at[k],
        device_id={"tensor": peer}, device_id_type=MESH)
    c.start()
    return c


def greet(sib, far):
    barrier = pltpu.get_barrier_semaphore()
    for peer in (sib, far):
        pl.semaphore_signal(barrier, inc=1, device_id={"tensor": peer}, device_id_type=MESH)
    pl.semaphore_wait(barrier, 2)


def columns(block):
    return pl.ds(pl.multiple_of(block * 256, 256), 256)


def sum_steps(part, out, low, near, mid, away, sems, base, place, scatter):
    side, core, sib, far = place
    live = []

    def one():
        low[...] = part[...].astype(jnp.bfloat16)
        for s in range(2):
            live.append(send(low.at[:, columns(s * 2 + 1 - core)], near.at[s], sems, base + s, sib))

    def two():
        order = (1 - side, side)
        for s in range(2):
            live[s].wait_recv()
        for i, s in enumerate(order):
            mid[s] = (low[:, columns(s * 2 + core)].astype(jnp.float32) + near[s].astype(jnp.float32)).astype(jnp.bfloat16)
            if i == 0 or not scatter:
                live.append(send(mid.at[s], away.at[s], sems, base + 2 + i, far))

    def three():
        if scatter:
            live[2].wait_recv()
            out[...] = mid[side].astype(jnp.float32) + away[side].astype(jnp.float32)
            return
        for i, s in enumerate((1 - side, side)):
            live[2 + i].wait_recv()
        for i, s in enumerate((1 - side, side)):
            there = out.at[:, columns(s * 2 + core)]
            out[:, columns(s * 2 + core)] = (mid[s].astype(jnp.float32) + away[s].astype(jnp.float32)).astype(jnp.bfloat16)
            live.append(send(there, there, sems, base + 4 + i, sib))

    def four():
        for c in live[4:]:
            c.wait_recv()
        for c in live:
            c.wait_send()

    return [one, two, three, four]


class SmallSum:
    def __init__(self, where, vec, out, slots, mine, send_sem, recv_sem):
        y, z, x = where
        self.vec, self.out, self.slots, self.mine = vec, out, slots, mine
        self.sems = (send_sem, recv_sem)
        self.axes = (
            (x, 4, lambda v: (y * 4 + z) * 4 + v),
            (z, 4, lambda v: (y * 4 + v) * 4 + x),
            (y, 2, lambda v: (v * 4 + z) * 4 + x),
        )
        self.live = []

    def begin(self, s, value):
        p, n, dev = self.axes[s]
        self.mine[s] = value
        self.slots[s, p] = value
        self.live = []
        for i in range(1, n):
            k = s * 3 + i - 1
            c = pltpu.make_async_remote_copy(
                src_ref=self.mine.at[s], dst_ref=self.slots.at[s, p], send_sem=self.sems[0].at[k], recv_sem=self.sems[1].at[k],
                device_id={"dp": dev(lax.rem(p + i, n))}, device_id_type=MESH)
            c.start()
            self.live.append(c)

    def close(self, s):
        for c in self.live:
            c.wait()
        value = self.slots[s, 0]
        for i in range(1, self.axes[s][1]):
            value = value + self.slots[s, i]
        return value

    def one(self):
        self.begin(0, self.vec[...])

    def two(self):
        self.begin(1, self.close(0))

    def three(self):
        self.begin(2, self.close(1))

    def four(self):
        self.out[...] = self.close(2)


def small_steps(v, out, near, mid, away, sems, base, place):
    side, core, sib, far = place
    live = []

    def one():
        live.append(send(v, near, sems, base, sib))

    def two():
        live[0].wait()
        mid[...] = v[...] + near[...]
        live.append(send(mid, away, sems, base + 1, far))

    def three():
        live[1].wait()
        out[...] = mid[...] + away[...]

    return [one, two, three]


def swap_halves(v):
    n = v.shape[1]
    lane = lax.broadcasted_iota(jnp.int32, v.shape, 1) % 64
    return jnp.where(lane < 32, pltpu.roll(v, n - 32, 1), pltpu.roll(v, 32, 1))


def head_means(v, heads):
    return [jnp.mean(v[:, 64 * h:64 * h + 64], axis=-1, keepdims=True) for h in range(heads)]


def spread(cols, heads):
    return jnp.concatenate([jnp.broadcast_to(c, (c.shape[0], 64)) for c in cols], axis=1)


CHUNK_SHAPES = ((2, 4, 4, 32, 1152),) * 3 + ((2, 4, 4, 32, 768),)


def big_kernel(*refs):
    (
        r_tokens, r_cotangent, r_lengths, r_frequency, r_attn_gain, r_mlp_gain, r_q_gain, r_k_gain,
        r_w_query, r_w_key, r_w_value, r_w_output, h_gate, h_up, h_down,
    ) = refs[:15]
    h_sums, (r_vec_sum, r_block_out, r_input_grad) = refs[15:19], refs[19:22]
    rest = refs[22:]
    groups = [rest[NS * c:NS * c + NS] for c in range(4)]
    rest = rest[NS * 4:]
    small_refs, grads, sums, rest = rest[:4], rest[4:8], rest[8:12], rest[12:]
    (r_vec, r_d_two, r_own, r_d_one, r_gains, r_gains_sum, r_part, r_d_hidden, r_d_low, r_d_qkv) = rest[:10]
    (r_x, r_cot, r_normed_one, r_normed_two, r_attended, r_hidden, r_d_two_part, r_mlp_part) = rest[10:18]
    (r_q_low, r_k_low, r_v_low, r_q_plain, r_k_plain, r_q_inv, r_k_inv, r_cosine, r_sine, r_p, r_heads_out) = rest[18:29]
    (r_act, r_d_gate, r_d_up, w_gate, w_up, w_down) = rest[29:35]
    rest = rest[35:]
    ts, tb, tc, ta, td = rest[:4], rest[4:8], rest[8:12], rest[12:16], rest[16:19]
    sems, load_sem, store_sem = rest[19:21], rest[21], rest[22]
    where, place = coords(), tensor_place()
    side, core, sib, far = place
    me = side * 2 + core
    y, z, x = where
    f32, bf = jnp.float32, jnp.bfloat16
    loads = []
    for k, (there, here) in enumerate(((h_gate, w_gate), (h_up, w_up), (h_down, w_down))):
        loads.append(pltpu.make_async_copy(there, here, load_sem.at[k]))
        loads[k].start()
    barrier = pltpu.get_barrier_semaphore()
    peers = [(y, z, lax.rem(x + k, 4)) for k in (1, 2, 3)] + [(y, lax.rem(z + k, 4), x) for k in (1, 2, 3)] + [(1 - y, z, x)]
    for a, b, c in peers:
        pl.semaphore_signal(barrier, inc=1, device_id={"dp": (a * 4 + b) * 4 + c}, device_id_type=MESH)
    for peer in (sib, far):
        pl.semaphore_signal(barrier, inc=1, device_id={"tensor": peer}, device_id_type=MESH)
    pl.semaphore_wait(barrier, len(peers) + 2)

    c0, c1, c2, c3 = [Chunk(grads[c], sums[c], *groups[c], 16, where) for c in range(4)]
    r_attn = grads[3]
    small = SmallSum(where, r_vec, r_vec_sum, *small_refs)
    attended = sum_steps(r_part, r_attended, *ts, sems, 0, place, False)
    two = sum_steps(r_d_two_part, r_d_two, *ta, sems, 6, place, False)
    own = sum_steps(r_mlp_part, r_own, *tb, sems, 12, place, True)
    one = sum_steps(r_part, r_d_one, *tc, sems, 18, place, False)
    gains = small_steps(r_gains, r_gains_sum, *td, sems, 24, place)
    rows = r_x.shape[0]
    stores = []

    def leave(c, chunk):
        def finish():
            chunk.end()
            out = pltpu.make_async_copy(sums[c], h_sums[c], store_sem.at[c])
            out.start()
            stores.append(out)

        return finish

    def row_blocks(step, start):
        return lax.fori_loop(0, rows // 16, lambda b, v: step(pl.ds(pl.multiple_of(b * 16, 16), 16), v), start)

    pairs = ((r_tokens, r_x), (r_cotangent, r_cot))
    moves = {}

    def gather_start():
        for k, (v, o) in enumerate(pairs):
            there = o.at[:, columns(me)]
            moves[k] = (send(v, there, sems, 26 + 3 * k, far), send(v, there, sems, 27 + 3 * k, sib))
        for v, o in pairs:
            o[:, columns(me)] = v[...]

    def gather_pass(k):
        moves[k][0].wait_recv()
        there = pairs[k][1].at[:, columns(far)]
        moves[k + 2] = (send(there, there, sems, 28 + 3 * k, sib),)

    def gather_end(k):
        moves[k][0].wait_send()
        moves[k][1].wait()
        moves[k + 2][0].wait()

    def tables():
        lengths = r_lengths[...]
        one_length = [lengths[:, k:k + 1] for k in range(4)]
        ends = [one_length[0]]
        for k in range(1, 4):
            ends.append(ends[-1] + one_length[k])

        def segment(row):
            total = jnp.zeros(row.shape, jnp.int32)
            for end in ends:
                total = total + jnp.where(row >= end, 1, 0)
            return total

        row = lax.broadcasted_iota(jnp.int32, (rows, 128), 0)
        start = jnp.zeros(row.shape, jnp.int32)
        for end, length in zip(ends, one_length):
            start = start + jnp.where(row >= end, length, 0)
        angles = (row - start).astype(f32) * r_frequency[...]
        lane = lax.broadcasted_iota(jnp.int32, (rows, 128), 1) % 64
        cosine, sine = jnp.cos(angles), jnp.sin(angles)
        sine = jnp.where(lane < 32, -sine, sine)
        for k in (0, 128):
            r_cosine[:, k:k + 128] = cosine
            r_sine[:, k:k + 128] = sine
        query_row = lax.broadcasted_iota(jnp.int32, (rows, rows), 0)
        key_row = lax.broadcasted_iota(jnp.int32, (rows, rows), 1)
        moves[9] = (segment(query_row) == segment(key_row)) & (query_row >= key_row)

    def attn_norm():
        gain = r_attn_gain[...]

        def block(at, v):
            resid = r_x[at, :].astype(f32)
            inverse = lax.rsqrt(jnp.mean(resid * resid, axis=-1, keepdims=True) + EPS)
            r_normed_one[at, :] = (resid * inverse * gain).astype(bf)
            return v

        row_blocks(block, 0)

    def attention():
        normed = r_normed_one[...]
        r_v_low[...] = jnp.dot(normed, r_w_value[...], preferred_element_type=f32).astype(bf)
        for weight, gain, low, plain_ref, inv_ref, heads in (
            (r_w_query, r_q_gain, r_q_low, r_q_plain, r_q_inv, 4), (r_w_key, r_k_gain, r_k_low, r_k_plain, r_k_inv, 2)):
            width = 64 * heads
            raw = jnp.dot(normed, weight[...], preferred_element_type=f32)
            inv = spread([lax.rsqrt(m + EPS) for m in head_means(raw * raw, heads)], heads)
            plain = raw * inv
            inv_ref[...] = inv
            plain_ref[...] = plain
            scaled = plain * gain[...]
            low[...] = (scaled * r_cosine[:, :width] + swap_halves(scaled) * r_sine[:, :width]).astype(bf)
        out = []
        for h in range(4):
            at = slice(64 * (h // 2), 64 * (h // 2) + 64)
            scores = dot_last(r_q_low[:, 64 * h:64 * h + 64], r_k_low[:, at]) * HEAD_SIZE ** (-0.5)
            scores = jnp.where(moves[9], scores, -1e30)
            weights = jnp.exp(scores - jnp.max(scores, axis=-1, keepdims=True))
            p = weights / jnp.sum(weights, axis=-1, keepdims=True)
            r_p[h] = p
            out.append(jnp.dot(p.astype(bf), r_v_low[:, at], preferred_element_type=f32))
        heads_out = jnp.concatenate(out, axis=1).astype(bf)
        r_heads_out[...] = heads_out
        r_part[...] = jnp.dot(heads_out, r_w_output[...], preferred_element_type=f32)

    def mlp_norm():
        gain = r_mlp_gain[...]

        def block(at, v):
            hidden = r_x[at, :].astype(f32) + r_attended[at, :].astype(f32)
            r_hidden[at, :] = hidden
            inverse = lax.rsqrt(jnp.mean(hidden * hidden, axis=-1, keepdims=True) + EPS)
            r_normed_two[at, :] = (hidden * inverse * gain).astype(bf)
            return v

        row_blocks(block, 0)

    def mlp_units():
        for load in loads:
            load.wait()

        def tile(j, v):
            at = pl.ds(pl.multiple_of(j * 384, 128), 384)
            gate = jnp.dot(r_normed_two[...], w_gate[:, at], preferred_element_type=f32)
            up = jnp.dot(r_normed_two[...], w_up[:, at], preferred_element_type=f32)
            s = jax.nn.sigmoid(gate)
            silu = gate * s
            r_act[:, at] = (silu * up).astype(bf)
            d_act = dot_last(r_cot[...], w_down[at, :])
            r_d_gate[:, at] = (d_act * up * s * (1.0 + gate * (1.0 - s))).astype(bf)
            r_d_up[:, at] = (d_act * silu).astype(bf)
            return v

        lax.fori_loop(0, 3, tile, 0)

    def weight_grad(left, right, out):
        def tile(j, v):
            part = dot_rows(left[:, columns(j)], right[...]).astype(bf)
            out[j // 2, pl.ds((j % 2) * 2, 2)] = part.reshape(2, 4, 32, right.shape[1])
            return v

        return lambda: lax.fori_loop(0, 4, tile, 0)

    down_grad = weight_grad(r_cot, r_act, grads[0])
    gate_grad = weight_grad(r_normed_two, r_d_gate, grads[1])
    up_grad = weight_grad(r_normed_two, r_d_up, grads[2])

    def mlp_back():
        def tile(j, v):
            at = columns(j)
            r_d_two_part[:, at] = dot_last(r_d_gate[...], w_gate[at, :]) + dot_last(r_d_up[...], w_up[at, :])
            return v

        lax.fori_loop(0, 4, tile, 0)

    def mlp_out():
        def tile(j, v):
            at = columns(j)
            r_mlp_part[:, at] = jnp.dot(r_act[...], w_down[:, at], preferred_element_type=f32)
            return v

        lax.fori_loop(0, 4, tile, 0)

    def back_mlp_norm():
        gain = r_mlp_gain[...]

        def block(b, total):
            at = pl.ds(pl.multiple_of(b * 16, 16), 16)
            hidden = r_hidden[at, :]
            inverse = lax.rsqrt(jnp.mean(hidden * hidden, axis=-1, keepdims=True) + EPS)
            plain = hidden * inverse
            d_two = r_d_two[at, :].astype(jnp.float32)
            u = d_two * gain
            d_hidden = r_cot[at, :].astype(jnp.float32) + inverse * (
                u - plain * jnp.mean(u * plain, axis=-1, keepdims=True))
            r_d_hidden[at, :] = d_hidden
            r_d_low[at, :] = d_hidden.astype(jnp.bfloat16)
            return total + jnp.sum(d_two * plain, axis=0, keepdims=True)

        total = lax.fori_loop(0, rows // 16, block, jnp.zeros((1, 1024), jnp.float32))
        r_vec[...] = jnp.zeros((8, 1024), jnp.float32)
        r_vec[1:2, :] = total
        mine = columns(me)
        r_block_out[...] = (r_hidden[:, mine] + r_own[...]).astype(jnp.bfloat16)

    hold = {}

    def back_output():
        d_low = r_d_low[...]
        hold[0] = dot_last(d_low, r_w_output[...]).astype(jnp.bfloat16)
        r_attn[:, :, :, :, 512:768] = dot_rows(d_low, r_heads_out[...]).astype(jnp.bfloat16).reshape(2, 4, 4, 32, 256)

    def back_scores():
        d_heads = hold[0]
        scale = HEAD_SIZE ** (-0.5)
        d_query, d_key, d_value = [], [], []
        for j in range(2):
            at = slice(64 * j, 64 * j + 64)
            key, value = r_k_low[:, at], r_v_low[:, at]
            dk, dv = 0.0, 0.0
            for h in (2 * j, 2 * j + 1):
                p = r_p[h]
                dh = d_heads[:, 64 * h:64 * h + 64]
                d_probs = dot_last(dh, value)
                ds = (p * (d_probs - jnp.sum(d_probs * p, axis=-1, keepdims=True))).astype(jnp.bfloat16)
                d_query.append(jnp.dot(ds, key, preferred_element_type=jnp.float32) * scale)
                dk = dk + dot_rows(ds, r_q_low[:, 64 * h:64 * h + 64])
                dv = dv + dot_rows(p.astype(jnp.bfloat16), dh)
            d_key.append(dk * scale)
            d_value.append(dv)
        r_d_qkv[:, 384:512] = jnp.concatenate(d_value, axis=1).astype(jnp.bfloat16)
        hold[1] = jnp.concatenate(d_query, axis=1)
        hold[2] = jnp.concatenate(d_key, axis=1)

    def back_head_norm():
        r_gains[...] = jnp.zeros((8, 128), jnp.float32)
        for d, plain_ref, gain_ref, inv_ref, heads, put, place_at in (
            (hold[1], r_q_plain, r_q_gain, r_q_inv, 4, 0, 0), (hold[2], r_k_plain, r_k_gain, r_k_inv, 2, 256, 64)):
            width = 64 * heads
            turned = d * r_cosine[:, :width] - swap_halves(d) * r_sine[:, :width]
            plain = plain_ref[...]
            sums = jnp.sum(turned * plain, axis=0, keepdims=True)
            total = sums[:, :64]
            for h in range(1, heads):
                total = total + sums[:, 64 * h:64 * h + 64]
            r_gains[0:1, place_at:place_at + 64] = total
            u = turned * gain_ref[...]
            inv = inv_ref[...]
            back = inv * (u - plain * spread(head_means(u * plain, heads), heads))
            r_d_qkv[:, put:put + width] = back.astype(jnp.bfloat16)

    def back_project():
        dq, dk, dv = r_d_qkv[:, :256], r_d_qkv[:, 256:384], r_d_qkv[:, 384:512]
        r_part[...] = (
            dot_last(dq, r_w_query[...]) + dot_last(dk, r_w_key[...]) + dot_last(dv, r_w_value[...]))

    def back_attn_weights():
        r_attn[:, :, :, :, 0:512] = dot_rows(r_normed_one[...], r_d_qkv[...]).astype(jnp.bfloat16).reshape(2, 4, 4, 32, 512)

    def back_attn_norm():
        gain = r_attn_gain[...]
        mine = columns(me)

        def block(b, total):
            at = pl.ds(pl.multiple_of(b * 16, 16), 16)
            resid = r_x[at, :].astype(jnp.float32)
            inverse = lax.rsqrt(jnp.mean(resid * resid, axis=-1, keepdims=True) + EPS)
            plain = resid * inverse
            d_one = r_d_one[at, :].astype(jnp.float32)
            u = d_one * gain
            r_d_hidden[at, :] = r_d_hidden[at, :] + inverse * (
                u - plain * jnp.mean(u * plain, axis=-1, keepdims=True))
            return total + jnp.sum(d_one * plain, axis=0, keepdims=True)

        total = lax.fori_loop(0, rows // 16, block, jnp.zeros((1, 1024), jnp.float32))
        r_vec[0:1, :] = total
        r_vec[2:3, 0:128] = r_gains_sum[0:1, :]
        r_input_grad[...] = r_d_hidden[:, mine].astype(jnp.bfloat16)

    for step in (
        gather_start, tables, lambda: gather_pass(0), lambda: gather_pass(1), lambda: gather_end(0),
        attn_norm, attention, attended[0], lambda: gather_end(1), attended[1], attended[2], attended[3],
        mlp_norm, mlp_units, down_grad, c0.start1, gate_grad, c1.start1, mlp_back, two[0], up_grad, two[1], c0.mid1, c2.start1,
        mlp_out, two[2], own[0], two[3], own[1], own[2], c0.fin1, own[3], back_mlp_norm,
        back_output, c1.mid1, back_scores, c0.mid2, back_head_norm, back_project,
        one[0], gains[0], back_attn_weights, c3.start1, c0.fin2, one[1], gains[1], c1.fin1, c2.mid1, one[2], gains[2], c0.finy, one[3],
        back_attn_norm, small.one, c1.mid2, c0.ag2, c2.fin1, c3.mid1, c1.fin2, small.two, c0.ag1s, c1.finy, c2.mid2, c3.fin1,
        c1.ag2, c2.fin2, c3.mid2, small.three, c1.ag1s, c2.finy, c3.fin2, c0.ag1, c2.ag2, c3.finy, c2.ag1s, c3.ag2, small.four,
        c3.ag1s, c1.ag1, leave(0, c0), c2.ag1, leave(1, c1), c3.ag1, leave(2, c2), leave(3, c3),
    ):
        step()
    for out in stores:
        out.wait()


def big(arrays):
    V, A = pl.BlockSpec(memory_space=pltpu.VMEM), pl.BlockSpec(memory_space=pl.ANY)
    f32, bf = jnp.float32, jnp.bfloat16
    S = jax.ShapeDtypeStruct
    out_shape = [S(s, bf) for s in CHUNK_SHAPES] + [S((8, 1024), f32), S((144, 256), bf), S((144, 256), bf)]
    B = lambda *shape: pltpu.VMEM(shape, bf)
    F = lambda *shape: pltpu.VMEM(shape, f32)
    D = lambda n: pltpu.SemaphoreType.DMA((n,))
    scratch = sum([scratch_for(s) for s in CHUNK_SHAPES], [])
    scratch += [F(3, 4, 8, 1024), F(3, 8, 1024), D(9), D(9)]
    scratch += [B(*s) for s in CHUNK_SHAPES] * 2
    scratch += [F(8, 1024), B(144, 1024), F(144, 256), B(144, 1024), F(8, 128), F(8, 128), F(144, 1024), F(144, 1024), B(144, 1024), B(144, 512)]
    scratch += [B(144, 1024), B(144, 1024), B(144, 1024), B(144, 1024), B(144, 1024), F(144, 1024), F(144, 1024), F(144, 1024)]
    scratch += [B(144, 256), B(144, 128), B(144, 128), F(144, 256), F(144, 128), F(144, 256), F(144, 128), F(144, 256), F(144, 256), F(4, 144, 144), B(144, 256)]
    scratch += [B(144, 1152), B(144, 1152), B(144, 1152), B(1024, 1152), B(1024, 1152), B(1152, 1024)]
    scratch += ([B(144, 1024)] + [B(2, 144, 256)] * 3) * 4 + [F(8, 128)] * 3
    scratch += [D(32), D(32), D(3), D(4)]
    return pl.pallas_call(
        big_kernel, out_shape=out_shape, in_specs=[V] * 12 + [A] * 3, out_specs=[A] * 4 + [V] * 3, scratch_shapes=scratch,
        compiler_params=pltpu.CompilerParams(collective_id=0, has_side_effects=True, vmem_limit_bytes=61 * 1024 * 1024),
        name="block",
    )(*arrays)


def widen_kernel(gate, up, down, attn, o_gate, o_up, o_down, o_q, o_k, o_v, o_out):
    o_gate[...] = gate[...].astype(jnp.float32)
    o_up[...] = up[...].astype(jnp.float32)
    o_down[...] = down[...].astype(jnp.float32).T
    wide = attn[...].astype(jnp.float32)
    o_q[...] = wide[:, :256]
    o_k[...] = wide[:, 256:384]
    o_v[...] = wide[:, 384:512]
    o_out[...] = wide[:, 512:768].T


def widen(gate, up, down, attn):
    S = lambda *s: jax.ShapeDtypeStruct(s, jnp.float32)
    row = lambda w: pl.BlockSpec((128, w), lambda b: (b, 0))
    col = lambda h: pl.BlockSpec((h, 128), lambda b: (0, b))
    return pl.pallas_call(
        widen_kernel, grid=(8,),
        in_specs=[row(1152), row(1152), row(1152), row(768)],
        out_specs=[row(1152), row(1152), col(1152), row(256), row(128), row(128), col(256)],
        out_shape=[S(1024, 1152), S(1024, 1152), S(1152, 1024), S(1024, 256), S(1024, 128), S(1024, 128), S(256, 1024)],
        compiler_params=pltpu.CompilerParams(vmem_limit_bytes=60 * 1024 * 1024),
        name="widen",
    )(gate, up, down, attn)


EPS = 1e-05
THETA = 1000000.0


def dot_rows(left_side, right_side):
    return lax.dot_general(
        left_side, right_side, (((0,), (0,)), ((), ())), preferred_element_type=jnp.float32
    )


def dot_last(left_side, right_side):
    return lax.dot_general(
        left_side, right_side, (((1,), (1,)), ((), ())), preferred_element_type=jnp.float32
    )


def body(
    tokens,
    lengths,
    attn_gain,
    w_query,
    key_weight,
    value_weight,
    query_gain,
    key_gain,
    w_output,
    mlp_gain,
    w_gate,
    w_up,
    w_down,
    cotangent,
):
    frequency = THETA ** (-jnp.arange(32, dtype=jnp.float32) * 2.0 / HEAD_SIZE)
    down, gate, up, attn, vec, block_out, input_grad = big(
        (
            tokens,
            cotangent,
            lengths,
            jnp.tile(frequency[None], (1, 4)),
            attn_gain[None],
            mlp_gain[None],
            jnp.tile(query_gain[None], (1, 4)),
            jnp.tile(key_gain[None], (1, 2)),
            w_query,
            key_weight,
            value_weight,
            w_output,
            w_gate,
            w_up,
            w_down,
        )
    )
    gate, up, down, w_q, w_k, w_v, w_o = widen(
        gate.reshape(1024, 1152), up.reshape(1024, 1152), down.reshape(1024, 1152), attn.reshape(1024, 768)
    )
    return (
        block_out,
        input_grad,
        vec[0],
        w_q,
        w_k,
        w_v,
        vec[2, :64],
        vec[2, 64:128],
        w_o,
        vec[1],
        gate,
        up,
        down,
    )


def solution(mesh):
    in_specs = (
        P("dp", "tensor"),
        P("dp", None),
        P(),
        P(None, "tensor"),
        P(None, "tensor"),
        P(None, "tensor"),
        P(),
        P(),
        P("tensor", None),
        P(),
        P(None, "tensor"),
        P(None, "tensor"),
        P("tensor", None),
        P("dp", "tensor"),
    )
    out_specs = (
        P("dp", "tensor"),
        P("dp", "tensor"),
        P(),
        P(None, "tensor"),
        P(None, "tensor"),
        P(None, "tensor"),
        P(),
        P(),
        P("tensor", None),
        P(),
        P(None, "tensor"),
        P(None, "tensor"),
        P("tensor", None),
    )
    return jax.shard_map(body, mesh=mesh, in_specs=in_specs, out_specs=out_specs, check_vma=False)
```

```python
import math
import functools
import jax
import jax.numpy as jnp
from jax import lax
from jax.experimental import pallas as pl
from jax.experimental.pallas import tpu as pltpu
from jax.sharding import PartitionSpec as P

HEAD_SIZE = 64
MESH = pl.DeviceIdType.MESH


def add_into(out, parts, step):
    lead = out.shape[0]
    rows = out.shape[1]
    per = rows // step

    def add_step(i, _):
        b = i // per
        r = pl.multiple_of((i % per) * step, 16)
        total = parts[0][b, pl.ds(r, step), :].astype(jnp.float32)
        for part in parts[1:]:
            total = total + part[b, pl.ds(r, step), :].astype(jnp.float32)
        out[b, pl.ds(r, step), :] = total.astype(jnp.bfloat16)
        return 0

    lax.fori_loop(0, lead * per, add_step, 0)


(T1P, T1M, I1P, I1M, M1P, M1M, T2P, T2M, I2P, I2M, M2P, M2M, Y, A2P, A2M, F2P, F2M, A1P, A1M, F1P, F1M, YA, YB, YC, YD) = range(25)
KEYS = 25


class Chunk:
    def __init__(self, src, dst, t1, r1, m1, s1, t2, r2, m2, s2, yb, send, recv, step, where):
        self.src, self.dst = src, dst
        self.t1, self.r1, self.m1, self.s1 = t1, r1, m1, s1
        self.t2, self.r2, self.m2, self.s2, self.yb = t2, r2, m2, s2, yb
        self.send, self.recv, self.step = send, recv, step
        y, z, x = where
        self.where = where

        def dev(yy, zz, xx):
            return {"dp": (yy * 4 + zz) * 4 + xx}

        up = lambda v: lax.rem(v + 1, 4)
        down = lambda v: lax.rem(v + 3, 4)
        xp, xm = dev(y, z, up(x)), dev(y, z, down(x))
        zp, zm = dev(y, up(z), x), dev(y, down(z), x)
        self.ynb = dev(1 - y, z, x)
        self.first = ((x, xp, xm), (z, zp, zm))
        self.second = ((z, zp, zm), (x, xp, xm))
        self.live = {}
        R, C = src.shape[3:]
        self.lo = (pl.ds(0, R // 2), pl.ds(0, C))
        self.hi = (pl.ds(R // 2, R // 2), pl.ds(0, C))

    def go(self, h, name, src, dst, device):
        k = h * KEYS + name
        c = pltpu.make_async_remote_copy(
            src_ref=src, dst_ref=dst, send_sem=self.send.at[k], recv_sem=self.recv.at[k],
            device_id=device, device_id_type=MESH)
        c.start()
        self.live[h, name] = c

    def got(self, h, *names):
        for n in names:
            self.live[h, n].wait_recv()

    def start1(self):
        for h in range(2):
            p, plus, minus = self.first[h]
            k2, kp, km = lax.rem(p + 2, 4), lax.rem(p + 1, 4), lax.rem(p + 3, 4)
            H, T, R = self.src.at[h], self.t1.at[h], self.r1.at[h]
            self.go(h, T1P, H.at[k2, pl.ds(0, 2)], T.at[0], plus)
            self.go(h, T1M, H.at[k2, pl.ds(2, 2)], T.at[1], minus)
            self.go(h, I1P, H.at[kp, pl.ds(2, 2)], R.at[0, pl.ds(2, 2)], plus)
            self.go(h, I1M, H.at[km, pl.ds(0, 2)], R.at[1, pl.ds(0, 2)], minus)

    def mid1(self):
        for h in range(2):
            p, plus, minus = self.first[h]
            kp, km = lax.rem(p + 1, 4), lax.rem(p + 3, 4)
            H, T, R, M = self.src.at[h], self.t1.at[h], self.r1.at[h], self.m1.at[h]
            self.got(h, T1P)
            add_into(M.at[0], (H.at[kp, pl.ds(0, 2)], T.at[0]), self.step)
            self.go(h, M1P, M.at[0], R.at[0, pl.ds(0, 2)], plus)
            self.got(h, T1M)
            add_into(M.at[1], (H.at[km, pl.ds(2, 2)], T.at[1]), self.step)
            self.go(h, M1M, M.at[1], R.at[1, pl.ds(2, 2)], minus)

    def fin1(self):
        for h in range(2):
            p = self.first[h][0]
            R = self.r1.at[h]
            self.got(h, I1P, I1M, M1P, M1M)
            add_into(self.s1.at[h], (self.src.at[h, p], R.at[0], R.at[1]), self.step)
            p, plus, minus = self.second[h]
            k2, kp, km = lax.rem(p + 2, 4), lax.rem(p + 1, 4), lax.rem(p + 3, 4)
            H, T, R, lo, hi = self.s1.at[h], self.t2.at[h], self.r2.at[h], self.lo, self.hi
            self.go(h, T2P, H.at[(k2,) + lo], T.at[lo], plus)
            self.go(h, T2M, H.at[(k2,) + hi], T.at[hi], minus)
            self.go(h, I2P, H.at[(kp,) + hi], R.at[(0,) + hi], plus)
            self.go(h, I2M, H.at[(km,) + lo], R.at[(1,) + lo], minus)

    def mid2(self):
        for h in range(2):
            p, plus, minus = self.second[h]
            kp, km = lax.rem(p + 1, 4), lax.rem(p + 3, 4)
            R, own = self.r2.at[h], (pl.ds(h, 1),)
            for name, arrived, k, part, slot, to in ((M2P, T2P, kp, self.lo, 0, plus), (M2M, T2M, km, self.hi, 1, minus)):
                self.got(h, arrived)
                add_into(self.m2.at[own + part], (self.s1.at[(h, pl.ds(k, 1)) + part], self.t2.at[own + part]), 16)
                self.go(h, name, self.m2.at[(h,) + part], R.at[(slot,) + part], to)

    def fin2(self):
        for h in range(2):
            p = self.second[h][0]
            R = self.r2.at[h]
            self.got(h, I2P, I2M, M2P, M2M)
            add_into(self.s2.at[pl.ds(h, 1)], (self.s1.at[h, pl.ds(p, 1)], R.at[pl.ds(0, 1)], R.at[pl.ds(1, 1)]), self.step)
            self.go(h, Y, self.s2.at[h], self.yb.at[h], self.ynb)

    def finy(self):
        for h in range(2):
            a = self.first[h][0]
            p, plus, minus = self.second[h]
            self.got(h, Y)
            add_into(self.dst.at[h, a, pl.ds(p, 1)], (self.s2.at[pl.ds(h, 1)], self.yb.at[pl.ds(h, 1)]), self.step)
            blk = self.dst.at[h, a, p]
            self.go(h, A2P, blk, blk, plus)
            self.go(h, A2M, blk, blk, minus)

    def ag2(self):
        for h in range(2):
            a = self.first[h][0]
            p, plus, minus = self.second[h]
            kp, km = lax.rem(p + 1, 4), lax.rem(p + 3, 4)
            self.got(h, A2P)
            blk = self.dst.at[(h, a, km) + self.lo]
            self.go(h, F2P, blk, blk, plus)
            self.got(h, A2M)
            blk = self.dst.at[(h, a, kp) + self.hi]
            self.go(h, F2M, blk, blk, minus)

    def ag1s(self):
        for h in range(2):
            p, plus, minus = self.first[h]
            self.got(h, F2P, F2M)
            blk = self.dst.at[h, p]
            self.go(h, A1P, blk, blk, plus)
            self.go(h, A1M, blk, blk, minus)

    def ag1(self):
        for h in range(2):
            p, plus, minus = self.first[h]
            kp, km = lax.rem(p + 1, 4), lax.rem(p + 3, 4)
            self.got(h, A1P)
            blk = self.dst.at[h, km, pl.ds(0, 2)]
            self.go(h, F1P, blk, blk, plus)
            self.got(h, A1M)
            blk = self.dst.at[h, kp, pl.ds(2, 2)]
            self.go(h, F1M, blk, blk, minus)

    def end(self):
        for h in range(2):
            self.got(h, F1P, F1M)
        for c in self.live.values():
            c.wait_send()

    def stages(self):
        return [self.start1, self.mid1, self.fin1, self.mid2, self.fin2, self.finy, self.ag2, self.ag1s, self.ag1, self.end]


class HalfChunk(Chunk):
    def __init__(self, src, whole, *rest):
        *_, where = rest
        super().__init__(src, whole.at[where[0]], *rest)
        R, C = src.shape[3:]
        self.lo = (pl.ds(0, R), pl.ds(0, 640))
        self.hi = (pl.ds(0, R), pl.ds(640, C - 640))

    def fin2(self):
        for h in range(2):
            a = self.first[h][0]
            p, plus, minus = self.second[h]
            R = self.r2.at[h]
            self.got(h, I2P, I2M, M2P, M2M)
            add_into(self.dst.at[h, a, pl.ds(p, 1)], (self.s1.at[h, pl.ds(p, 1)], R.at[pl.ds(0, 1)], R.at[pl.ds(1, 1)]), self.step)
            blk = self.dst.at[h, a, p]
            self.go(h, A2P, blk, blk, plus)
            self.go(h, A2M, blk, blk, minus)

    def across(self, h, name, k):
        blk = self.dst.at[h, k]
        self.go(h, name, blk, blk, self.ynb)

    def ag1s(self):
        super().ag1s()
        for h in range(2):
            self.across(h, YA, self.first[h][0])

    def ag1(self):
        super().ag1()
        for h in range(2):
            p = self.first[h][0]
            self.across(h, YB, lax.rem(p + 3, 4))
            self.across(h, YC, lax.rem(p + 1, 4))

    def last(self):
        for h in range(2):
            self.got(h, F1P, F1M)
            self.across(h, YD, lax.rem(self.first[h][0] + 2, 4))

    def end(self):
        for h in range(2):
            self.got(h, YA, YB, YC, YD)
        for c in self.live.values():
            c.wait_send()


def coords():
    d = lax.axis_index("dp")
    return d // 16, (d // 4) % 4, d % 4


def scratch_for(shape):
    _, _, _, R, C = shape
    bf = jnp.bfloat16
    return [
        pltpu.VMEM((2, 2, 2, R, C), bf), pltpu.VMEM((2, 2, 4, R, C), bf), pltpu.VMEM((2, 2, 2, R, C), bf), pltpu.VMEM((2, 4, R, C), bf),
        pltpu.VMEM((2, R, C), bf), pltpu.VMEM((2, 2, R, C), bf), pltpu.VMEM((2, R, C), bf), pltpu.VMEM((2, R, C), bf), pltpu.VMEM((2, R, C), bf),
        pltpu.SemaphoreType.DMA((2 * KEYS,)), pltpu.SemaphoreType.DMA((2 * KEYS,)),
    ]

NS = 11

def tensor_place():
    t = lax.axis_index("tensor")
    core, side = lax.rem(t, 2), t // 2
    return side, core, side * 2 + (1 - core), (1 - side) * 2 + core


def send(src, dst, sems, k, peer):
    c = pltpu.make_async_remote_copy(
        src_ref=src, dst_ref=dst, send_sem=sems[0].at[k], recv_sem=sems[1].at[k],
        device_id={"tensor": peer}, device_id_type=MESH)
    c.start()
    return c


def greet(sib, far):
    barrier = pltpu.get_barrier_semaphore()
    for peer in (sib, far):
        pl.semaphore_signal(barrier, inc=1, device_id={"tensor": peer}, device_id_type=MESH)
    pl.semaphore_wait(barrier, 2)


def columns(block):
    return pl.ds(pl.multiple_of(block * 256, 256), 256)


def sum_steps(part, out, low, near, mid, away, sems, base, place, scatter):
    side, core, sib, far = place
    live = []

    def one():
        low[...] = part[...].astype(jnp.bfloat16)
        for s in range(2):
            live.append(send(low.at[:, columns(s * 2 + 1 - core)], near.at[s], sems, base + s, sib))

    def two():
        order = (1 - side, side)
        for s in range(2):
            live[s].wait_recv()
        for i, s in enumerate(order):
            mid[s] = (low[:, columns(s * 2 + core)].astype(jnp.float32) + near[s].astype(jnp.float32)).astype(jnp.bfloat16)
            if i == 0 or not scatter:
                live.append(send(mid.at[s], away.at[s], sems, base + 2 + i, far))

    def three():
        if scatter:
            live[2].wait_recv()
            out[...] = mid[side].astype(jnp.float32) + away[side].astype(jnp.float32)
            return
        for i, s in enumerate((1 - side, side)):
            live[2 + i].wait_recv()
        for i, s in enumerate((1 - side, side)):
            there = out.at[:, columns(s * 2 + core)]
            out[:, columns(s * 2 + core)] = (mid[s].astype(jnp.float32) + away[s].astype(jnp.float32)).astype(jnp.bfloat16)
            live.append(send(there, there, sems, base + 4 + i, sib))

    def four():
        for c in live[4:]:
            c.wait_recv()
        for c in live:
            c.wait_send()

    return [one, two, three, four]


class SmallSum:
    def __init__(self, where, vec, out, slots, mine, send_sem, recv_sem):
        y, z, x = where
        self.vec, self.out, self.slots, self.mine = vec, out, slots, mine
        self.sems = (send_sem, recv_sem)
        self.axes = (
            (x, 4, lambda v: (y * 4 + z) * 4 + v),
            (z, 4, lambda v: (y * 4 + v) * 4 + x),
            (y, 2, lambda v: (v * 4 + z) * 4 + x),
        )
        self.live = []

    def begin(self, s, value):
        p, n, dev = self.axes[s]
        self.mine[s] = value
        self.slots[s, p] = value
        self.live = []
        for i in range(1, n):
            k = s * 3 + i - 1
            c = pltpu.make_async_remote_copy(
                src_ref=self.mine.at[s], dst_ref=self.slots.at[s, p], send_sem=self.sems[0].at[k], recv_sem=self.sems[1].at[k],
                device_id={"dp": dev(lax.rem(p + i, n))}, device_id_type=MESH)
            c.start()
            self.live.append(c)

    def close(self, s):
        for c in self.live:
            c.wait()
        value = self.slots[s, 0]
        for i in range(1, self.axes[s][1]):
            value = value + self.slots[s, i]
        return value

    def one(self):
        self.begin(0, self.vec[...])

    def two(self):
        self.begin(1, self.close(0))

    def three(self):
        self.begin(2, self.close(1))

    def four(self):
        self.out[...] = self.close(2)


def small_steps(v, out, near, mid, away, sems, base, place):
    side, core, sib, far = place
    live = []

    def one():
        live.append(send(v, near, sems, base, sib))

    def two():
        live[0].wait()
        mid[...] = v[...] + near[...]
        live.append(send(mid, away, sems, base + 1, far))

    def three():
        live[1].wait()
        out[...] = mid[...] + away[...]

    return [one, two, three]


def swap_halves(v):
    n = v.shape[1]
    lane = lax.broadcasted_iota(jnp.int32, v.shape, 1) % 64
    return jnp.where(lane < 32, pltpu.roll(v, n - 32, 1), pltpu.roll(v, 32, 1))


def head_means(v, heads):
    return [jnp.mean(v[:, 64 * h:64 * h + 64], axis=-1, keepdims=True) for h in range(heads)]


def spread(cols, heads):
    return jnp.concatenate([jnp.broadcast_to(c, (c.shape[0], 64)) for c in cols], axis=1)


CHUNK_SHAPES = ((2, 4, 4, 16, 1152), (2, 4, 4, 32, 1152), (2, 4, 4, 32, 1152), (2, 4, 4, 32, 768))
SUM_SHAPES = ((2,) + CHUNK_SHAPES[0],) + CHUNK_SHAPES[1:]


def big_kernel(*refs):
    (
        r_tokens, r_cotangent, r_lengths, r_attn_gain, r_mlp_gain, r_q_gain, r_k_gain,
        r_w_query, r_w_key, r_w_value, r_w_output, h_gate, h_up, h_down,
    ) = refs[:14]
    h_sums, (r_vec_sum, r_block_out, r_input_grad) = refs[14:18], refs[18:21]
    rest = refs[21:]
    groups = [rest[NS * c:NS * c + NS] for c in range(4)]
    rest = rest[NS * 4:]
    small_refs, grads, sums, rest = rest[:4], rest[4:8], rest[8:12], rest[12:]
    (r_vec, r_d_two, r_own, r_d_one, r_gains, r_gains_sum, r_part, r_d_hidden, r_d_low, r_d_qkv) = rest[:10]
    (r_x, r_cot, r_normed_one, r_normed_two, r_attended, r_hidden, r_d_two_part, r_mlp_part) = rest[10:18]
    (r_q_low, r_k_low, r_v_low, r_q_plain, r_k_plain, r_q_inv, r_k_inv, r_cosine, r_sine, r_p, r_heads_out) = rest[18:29]
    (r_acts, r_d_gate, r_d_up, w_gate, w_up, w_down, r_cots) = rest[29:36]
    rest = rest[36:]
    r_act = r_acts.at[pl.ds(0, 144)]
    ts, tb, tc, ta, td = rest[:4], rest[4:8], rest[8:12], rest[12:16], rest[16:19]
    sems, load_sem, store_sem = rest[19:21], rest[21], rest[22]
    where, place = coords(), tensor_place()
    side, core, sib, far = place
    me = side * 2 + core
    y, z, x = where
    f32, bf = jnp.float32, jnp.bfloat16
    loads = []
    for k, (there, here) in enumerate(((h_gate, w_gate), (h_up, w_up), (h_down, w_down))):
        loads.append(pltpu.make_async_copy(there, here, load_sem.at[k]))
        loads[k].start()
    barrier = pltpu.get_barrier_semaphore()
    peers = [(y, z, lax.rem(x + k, 4)) for k in (1, 2, 3)] + [(y, lax.rem(z + k, 4), x) for k in (1, 2, 3)] + [(1 - y, z, x)]
    for a, b, c in peers:
        pl.semaphore_signal(barrier, inc=1, device_id={"dp": (a * 4 + b) * 4 + c}, device_id_type=MESH)
    for peer in (sib, far):
        pl.semaphore_signal(barrier, inc=1, device_id={"tensor": peer}, device_id_type=MESH)
    pl.semaphore_wait(barrier, len(peers) + 2)

    c0 = HalfChunk(grads[0], sums[0], *groups[0], 16, where)
    c1, c2, c3 = [Chunk(grads[c], sums[c], *groups[c], 16, where) for c in range(1, 4)]
    r_attn = grads[3]
    small = SmallSum(where, r_vec, r_vec_sum, *small_refs)
    attended = sum_steps(r_part, r_attended, *ts, sems, 0, place, False)
    two = sum_steps(r_d_two_part, r_d_two, *ta, sems, 6, place, False)
    own = sum_steps(r_mlp_part, r_own, *tb, sems, 12, place, True)
    one = sum_steps(r_part, r_d_one, *tc, sems, 18, place, False)
    gains = small_steps(r_gains, r_gains_sum, *td, sems, 24, place)
    rows = r_x.shape[0]
    stores = []

    def leave(c, chunk):
        def finish():
            chunk.end()
            out = pltpu.make_async_copy(sums[c], h_sums[c], store_sem.at[c])
            out.start()
            stores.append(out)

        return finish

    def row_blocks(step, start):
        return lax.fori_loop(0, rows // 16, lambda b, v: step(pl.ds(pl.multiple_of(b * 16, 16), 16), v), start)

    pairs = ((r_tokens, r_x), (r_cotangent, r_cot))
    moves = {}

    def gather_start():
        for k, (v, o) in enumerate(pairs):
            there = o.at[:, columns(me)]
            moves[k] = (send(v, there, sems, 26 + 3 * k, far), send(v, there, sems, 27 + 3 * k, sib))
        for v, o in pairs:
            o[:, columns(me)] = v[...]

    def gather_pass(k):
        moves[k][0].wait_recv()
        there = pairs[k][1].at[:, columns(far)]
        moves[k + 2] = (send(there, there, sems, 28 + 3 * k, sib),)

    def gather_end(k):
        moves[k][0].wait_send()
        moves[k][1].wait()
        moves[k + 2][0].wait()

    def tables():
        lengths = r_lengths[...]
        one_length = [lengths[:, k:k + 1] for k in range(4)]
        ends = [one_length[0]]
        for k in range(1, 4):
            ends.append(ends[-1] + one_length[k])

        def segment(row):
            total = jnp.zeros(row.shape, jnp.int32)
            for end in ends:
                total = total + jnp.where(row >= end, 1, 0)
            return total

        row = lax.broadcasted_iota(jnp.int32, (rows, 128), 0)
        start = jnp.zeros(row.shape, jnp.int32)
        for end, length in zip(ends, one_length):
            start = start + jnp.where(row >= end, length, 0)
        lane = lax.broadcasted_iota(jnp.int32, (rows, 128), 1) % 64
        power = (lane % 32).astype(f32) * (-2.0 / HEAD_SIZE)
        angles = (row - start).astype(f32) * jnp.exp(power * math.log(THETA))
        cosine, sine = jnp.cos(angles), jnp.sin(angles)
        sine = jnp.where(lane < 32, -sine, sine)
        for k in (0, 128):
            r_cosine[:, k:k + 128] = cosine
            r_sine[:, k:k + 128] = sine
        query_row = lax.broadcasted_iota(jnp.int32, (rows, rows), 0)
        key_row = lax.broadcasted_iota(jnp.int32, (rows, rows), 1)
        moves[9] = (segment(query_row) == segment(key_row)) & (query_row >= key_row)

    def attn_norm():
        gain = r_attn_gain[...]

        def block(at, v):
            resid = r_x[at, :].astype(f32)
            inverse = lax.rsqrt(jnp.mean(resid * resid, axis=-1, keepdims=True) + EPS)
            r_normed_one[at, :] = (resid * inverse * gain).astype(bf)
            return v

        row_blocks(block, 0)

    def attention():
        normed = r_normed_one[...]
        r_v_low[...] = jnp.dot(normed, r_w_value[...], preferred_element_type=f32).astype(bf)
        for weight, gain, low, plain_ref, inv_ref, heads in (
            (r_w_query, r_q_gain, r_q_low, r_q_plain, r_q_inv, 4), (r_w_key, r_k_gain, r_k_low, r_k_plain, r_k_inv, 2)):
            width = 64 * heads
            raw = jnp.dot(normed, weight[...], preferred_element_type=f32)
            inv = spread([lax.rsqrt(m + EPS) for m in head_means(raw * raw, heads)], heads)
            plain = raw * inv
            inv_ref[...] = inv
            plain_ref[...] = plain
            scaled = plain * jnp.concatenate([gain[...]] * heads, axis=1)
            low[...] = (scaled * r_cosine[:, :width] + swap_halves(scaled) * r_sine[:, :width]).astype(bf)
        out = []
        for h in range(4):
            at = slice(64 * (h // 2), 64 * (h // 2) + 64)
            scores = dot_last(r_q_low[:, 64 * h:64 * h + 64], r_k_low[:, at]) * HEAD_SIZE ** (-0.5)
            scores = jnp.where(moves[9], scores, -1e30)
            weights = jnp.exp(scores - jnp.max(scores, axis=-1, keepdims=True))
            p = weights / jnp.sum(weights, axis=-1, keepdims=True)
            r_p[h] = p
            out.append(jnp.dot(p.astype(bf), r_v_low[:, at], preferred_element_type=f32))
        heads_out = jnp.concatenate(out, axis=1).astype(bf)
        r_heads_out[...] = heads_out
        r_part[...] = jnp.dot(heads_out, r_w_output[...], preferred_element_type=f32)

    def mlp_norm():
        gain = r_mlp_gain[...]

        def block(at, v):
            hidden = r_x[at, :].astype(f32) + r_attended[at, :].astype(f32)
            r_hidden[at, :] = hidden
            inverse = lax.rsqrt(jnp.mean(hidden * hidden, axis=-1, keepdims=True) + EPS)
            r_normed_two[at, :] = (hidden * inverse * gain).astype(bf)
            return v

        row_blocks(block, 0)

    def mlp_units():
        for load in loads:
            load.wait()

        def tile(j, v):
            at = pl.ds(pl.multiple_of(j * 384, 128), 384)
            gate = jnp.dot(r_normed_two[...], w_gate[:, at], preferred_element_type=f32)
            up = jnp.dot(r_normed_two[...], w_up[:, at], preferred_element_type=f32)
            s = jax.nn.sigmoid(gate)
            silu = gate * s
            r_act[:, at] = (silu * up).astype(bf)
            d_act = dot_last(r_cot[...], w_down[at, :])
            r_d_gate[:, at] = (d_act * up * s * (1.0 + gate * (1.0 - s))).astype(bf)
            r_d_up[:, at] = (d_act * silu).astype(bf)
            return v

        lax.fori_loop(0, 3, tile, 0)

    def weight_grad(left, right, out):
        def tile(j, v):
            part = dot_rows(left[:, columns(j)], right[...]).astype(bf)
            out[j // 2, pl.ds((j % 2) * 2, 2)] = part.reshape(2, 4, 32, right.shape[1])
            return v

        return lambda: lax.fori_loop(0, 4, tile, 0)

    def swap_y(k, src, dst):
        c = pltpu.make_async_remote_copy(
            src_ref=src, dst_ref=dst, send_sem=sems[0].at[32 + k], recv_sem=sems[1].at[32 + k],
            device_id={"dp": c0.ynb["dp"]}, device_id_type=MESH)
        c.start()
        moves[20 + k] = c

    def swap_cot():
        half = lambda v: pl.ds(pl.multiple_of(v * 512, 512), 512)
        swap_y(0, r_cot.at[:, half(1 - y)], r_cots.at[pl.ds(144, 144)])
        r_cots[0:144, :] = r_cot[:, half(y)]

    def swap_act():
        swap_y(1, r_act, r_acts.at[pl.ds(144, 144)])

    def down_grad():
        moves[20].wait()
        moves[21].wait()

        def tile(j, v):
            grads[0][j] = dot_rows(r_cots[:, columns(j)], r_acts[...]).astype(bf).reshape(4, 4, 16, 1152)
            return v

        lax.fori_loop(0, 2, tile, 0)

    gate_grad = weight_grad(r_normed_two, r_d_gate, grads[1])
    up_grad = weight_grad(r_normed_two, r_d_up, grads[2])

    def mlp_back():
        def tile(j, v):
            at = columns(j)
            r_d_two_part[:, at] = dot_last(r_d_gate[...], w_gate[at, :]) + dot_last(r_d_up[...], w_up[at, :])
            return v

        lax.fori_loop(0, 4, tile, 0)

    def mlp_out():
        def tile(j, v):
            at = columns(j)
            r_mlp_part[:, at] = jnp.dot(r_act[...], w_down[:, at], preferred_element_type=f32)
            return v

        lax.fori_loop(0, 4, tile, 0)

    def back_mlp_norm():
        gain = r_mlp_gain[...]

        def block(b, total):
            at = pl.ds(pl.multiple_of(b * 16, 16), 16)
            hidden = r_hidden[at, :]
            inverse = lax.rsqrt(jnp.mean(hidden * hidden, axis=-1, keepdims=True) + EPS)
            plain = hidden * inverse
            d_two = r_d_two[at, :].astype(jnp.float32)
            u = d_two * gain
            d_hidden = r_cot[at, :].astype(jnp.float32) + inverse * (
                u - plain * jnp.mean(u * plain, axis=-1, keepdims=True))
            r_d_hidden[at, :] = d_hidden
            r_d_low[at, :] = d_hidden.astype(jnp.bfloat16)
            return total + jnp.sum(d_two * plain, axis=0, keepdims=True)

        total = lax.fori_loop(0, rows // 16, block, jnp.zeros((1, 1024), jnp.float32))
        r_vec[...] = jnp.zeros((8, 1024), jnp.float32)
        r_vec[1:2, :] = total
        mine = columns(me)
        r_block_out[...] = (r_hidden[:, mine] + r_own[...]).astype(jnp.bfloat16)

    hold = {}

    def back_output():
        d_low = r_d_low[...]
        hold[0] = dot_last(d_low, r_w_output[...]).astype(jnp.bfloat16)
        r_attn[:, :, :, :, 512:768] = dot_rows(d_low, r_heads_out[...]).astype(jnp.bfloat16).reshape(2, 4, 4, 32, 256)

    def back_scores():
        d_heads = hold[0]
        scale = HEAD_SIZE ** (-0.5)
        d_query, d_key, d_value = [], [], []
        for j in range(2):
            at = slice(64 * j, 64 * j + 64)
            key, value = r_k_low[:, at], r_v_low[:, at]
            dk, dv = 0.0, 0.0
            for h in (2 * j, 2 * j + 1):
                p = r_p[h]
                dh = d_heads[:, 64 * h:64 * h + 64]
                d_probs = dot_last(dh, value)
                ds = (p * (d_probs - jnp.sum(d_probs * p, axis=-1, keepdims=True))).astype(jnp.bfloat16)
                d_query.append(jnp.dot(ds, key, preferred_element_type=jnp.float32) * scale)
                dk = dk + dot_rows(ds, r_q_low[:, 64 * h:64 * h + 64])
                dv = dv + dot_rows(p.astype(jnp.bfloat16), dh)
            d_key.append(dk * scale)
            d_value.append(dv)
        r_d_qkv[:, 384:512] = jnp.concatenate(d_value, axis=1).astype(jnp.bfloat16)
        hold[1] = jnp.concatenate(d_query, axis=1)
        hold[2] = jnp.concatenate(d_key, axis=1)

    def back_head_norm():
        r_gains[...] = jnp.zeros((8, 128), jnp.float32)
        for d, plain_ref, gain_ref, inv_ref, heads, put, place_at in (
            (hold[1], r_q_plain, r_q_gain, r_q_inv, 4, 0, 0), (hold[2], r_k_plain, r_k_gain, r_k_inv, 2, 256, 64)):
            width = 64 * heads
            turned = d * r_cosine[:, :width] - swap_halves(d) * r_sine[:, :width]
            plain = plain_ref[...]
            sums = jnp.sum(turned * plain, axis=0, keepdims=True)
            total = sums[:, :64]
            for h in range(1, heads):
                total = total + sums[:, 64 * h:64 * h + 64]
            r_gains[0:1, place_at:place_at + 64] = total
            u = turned * jnp.concatenate([gain_ref[...]] * heads, axis=1)
            inv = inv_ref[...]
            back = inv * (u - plain * spread(head_means(u * plain, heads), heads))
            r_d_qkv[:, put:put + width] = back.astype(jnp.bfloat16)

    def back_project():
        dq, dk, dv = r_d_qkv[:, :256], r_d_qkv[:, 256:384], r_d_qkv[:, 384:512]
        r_part[...] = (
            dot_last(dq, r_w_query[...]) + dot_last(dk, r_w_key[...]) + dot_last(dv, r_w_value[...]))

    def back_attn_weights():
        r_attn[:, :, :, :, 0:512] = dot_rows(r_normed_one[...], r_d_qkv[...]).astype(jnp.bfloat16).reshape(2, 4, 4, 32, 512)

    def back_attn_norm():
        gain = r_attn_gain[...]
        mine = columns(me)

        def block(b, total):
            at = pl.ds(pl.multiple_of(b * 16, 16), 16)
            resid = r_x[at, :].astype(jnp.float32)
            inverse = lax.rsqrt(jnp.mean(resid * resid, axis=-1, keepdims=True) + EPS)
            plain = resid * inverse
            d_one = r_d_one[at, :].astype(jnp.float32)
            u = d_one * gain
            r_d_hidden[at, :] = r_d_hidden[at, :] + inverse * (
                u - plain * jnp.mean(u * plain, axis=-1, keepdims=True))
            return total + jnp.sum(d_one * plain, axis=0, keepdims=True)

        total = lax.fori_loop(0, rows // 16, block, jnp.zeros((1, 1024), jnp.float32))
        r_vec[0:1, :] = total
        r_vec[2:3, 0:128] = r_gains_sum[0:1, :]
        r_input_grad[...] = r_d_hidden[:, mine].astype(jnp.bfloat16)

    for step in (
        gather_start, tables, lambda: gather_pass(0), lambda: gather_pass(1), lambda: gather_end(0),
        attn_norm, attention, attended[0], lambda: gather_end(1), attended[1], attended[2], swap_cot, attended[3],
        mlp_norm, mlp_units, swap_act, gate_grad, c1.start1, mlp_back, two[0], up_grad, two[1], c2.start1, down_grad, c0.start1,
        mlp_out, two[2], own[0], two[3], own[1], c1.mid1, own[2], c0.mid1, own[3], back_mlp_norm,
        back_output, c2.mid1, c1.fin1, back_scores, c0.fin1, back_head_norm, back_project,
        one[0], gains[0], back_attn_weights, c3.start1, c0.mid2, c1.mid2, one[1], gains[1], c0.fin2, c2.fin1, one[2], gains[2], c0.ag2, c1.fin2, one[3],
        back_attn_norm, small.one, c0.ag1s, c3.mid1, c2.mid2, c1.finy, small.two, c0.ag1, c2.fin2, c3.fin1, c1.ag2, c0.last, c2.finy,
        c3.mid2, small.three, c1.ag1s, c3.fin2, c2.ag2, c3.finy, c2.ag1s, c1.ag1, c3.ag2, small.four,
        c3.ag1s, c2.ag1, leave(1, c1), c3.ag1, leave(0, c0), leave(2, c2), leave(3, c3),
    ):
        step()
    for out in stores:
        out.wait()


def big(arrays):
    V, A = pl.BlockSpec(memory_space=pltpu.VMEM), pl.BlockSpec(memory_space=pl.ANY)
    f32, bf = jnp.float32, jnp.bfloat16
    S = jax.ShapeDtypeStruct
    out_shape = [S(s, bf) for s in SUM_SHAPES] + [S((8, 1024), f32), S((144, 256), bf), S((144, 256), bf)]
    B = lambda *shape: pltpu.VMEM(shape, bf)
    F = lambda *shape: pltpu.VMEM(shape, f32)
    D = lambda n: pltpu.SemaphoreType.DMA((n,))
    scratch = sum([scratch_for(s) for s in CHUNK_SHAPES], [])
    scratch += [F(3, 4, 8, 1024), F(3, 8, 1024), D(9), D(9)]
    scratch += [B(*s) for s in CHUNK_SHAPES] + [B(*s) for s in SUM_SHAPES]
    scratch += [F(8, 1024), B(144, 1024), F(144, 256), B(144, 1024), F(8, 128), F(8, 128), F(144, 1024), F(144, 1024), B(144, 1024), B(144, 512)]
    scratch += [B(144, 1024), B(144, 1024), B(144, 1024), B(144, 1024), B(144, 1024), F(144, 1024), F(144, 1024), F(144, 1024)]
    scratch += [B(144, 256), B(144, 128), B(144, 128), F(144, 256), F(144, 128), F(144, 256), F(144, 128), F(144, 256), F(144, 256), F(4, 144, 144), B(144, 256)]
    scratch += [B(288, 1152), B(144, 1152), B(144, 1152), B(1024, 1152), B(1024, 1152), B(1152, 1024), B(288, 512)]
    scratch += ([B(144, 1024)] + [B(2, 144, 256)] * 3) * 4 + [F(8, 128)] * 3
    scratch += [D(34), D(34), D(3), D(4)]
    return pl.pallas_call(
        big_kernel, out_shape=out_shape, in_specs=[V] * 11 + [A] * 3, out_specs=[A] * 4 + [V] * 3, scratch_shapes=scratch,
        compiler_params=pltpu.CompilerParams(collective_id=0, has_side_effects=True, vmem_limit_bytes=61 * 1024 * 1024),
        name="block",
    )(*arrays)


def widen_kernel(gate, up, down, attn, vec, block, grad, o_gate, o_up, o_down, o_q, o_k, o_v, o_out, o_attn, o_mlp, o_qg, o_kg, o_block, o_grad):
    o_gate[...] = gate[...].astype(jnp.float32)
    o_up[...] = up[...].astype(jnp.float32)
    o_down[...] = down[...].astype(jnp.float32).T
    wide = attn[...].astype(jnp.float32)
    o_q[...] = wide[:, :256]
    o_k[...] = wide[:, 256:384]
    o_v[...] = wide[:, 384:512]
    o_out[...] = wide[:, 512:768].T

    @pl.when(pl.program_id(0) == 0)
    def _():
        o_attn[...] = vec[0, :]
        o_mlp[...] = vec[1, :]
        o_qg[...] = vec[2, 0:64]
        o_kg[...] = vec[2, 64:128]
        o_block[...] = block[...]
        o_grad[...] = grad[...]


def widen(gate, up, down, attn, vec, block, grad):
    S = lambda *s: jax.ShapeDtypeStruct(s, jnp.float32)
    row = lambda w: pl.BlockSpec((128, w), lambda b: (b, 0))
    col = lambda h: pl.BlockSpec((h, 128), lambda b: (0, b))
    all_of = lambda *s: pl.BlockSpec(s, lambda b: (0,) * len(s))
    own = jax.ShapeDtypeStruct(block.shape, block.dtype)
    return pl.pallas_call(
        widen_kernel, grid=(8,),
        in_specs=[row(1152), row(1152), row(1152), row(768), all_of(8, 1024), all_of(144, 256), all_of(144, 256)],
        out_specs=[row(1152), row(1152), col(1152), row(256), row(128), row(128), col(256),
                   all_of(1024), all_of(1024), all_of(64), all_of(64), all_of(144, 256), all_of(144, 256)],
        out_shape=[S(1024, 1152), S(1024, 1152), S(1152, 1024), S(1024, 256), S(1024, 128), S(1024, 128), S(256, 1024),
                   S(1024), S(1024), S(64), S(64), own, own],
        compiler_params=pltpu.CompilerParams(vmem_limit_bytes=60 * 1024 * 1024),
        name="widen",
    )(gate, up, down, attn, vec, block, grad)


EPS = 1e-05
THETA = 1000000.0


def dot_rows(left_side, right_side):
    return lax.dot_general(
        left_side, right_side, (((0,), (0,)), ((), ())), preferred_element_type=jnp.float32
    )


def dot_last(left_side, right_side):
    return lax.dot_general(
        left_side, right_side, (((1,), (1,)), ((), ())), preferred_element_type=jnp.float32
    )


def body(
    tokens,
    lengths,
    attn_gain,
    w_query,
    key_weight,
    value_weight,
    query_gain,
    key_gain,
    w_output,
    mlp_gain,
    w_gate,
    w_up,
    w_down,
    cotangent,
):
    down, gate, up, attn, vec, block_out, input_grad = big(
        (
            tokens,
            cotangent,
            lengths,
            attn_gain[None],
            mlp_gain[None],
            query_gain[None],
            key_gain[None],
            w_query,
            key_weight,
            value_weight,
            w_output,
            w_gate,
            w_up,
            w_down,
        )
    )
    gate, up, down, w_q, w_k, w_v, w_o, attn_g, mlp_g, query_g, key_g, block_out, input_grad = widen(
        gate.reshape(1024, 1152), up.reshape(1024, 1152), down.reshape(1024, 1152), attn.reshape(1024, 768), vec, block_out, input_grad
    )
    return (block_out, input_grad, attn_g, w_q, w_k, w_v, query_g, key_g, w_o, mlp_g, gate, up, down)


def solution(mesh):
    in_specs = (
        P("dp", "tensor"),
        P("dp", None),
        P(),
        P(None, "tensor"),
        P(None, "tensor"),
        P(None, "tensor"),
        P(),
        P(),
        P("tensor", None),
        P(),
        P(None, "tensor"),
        P(None, "tensor"),
        P("tensor", None),
        P("dp", "tensor"),
    )
    out_specs = (
        P("dp", "tensor"),
        P("dp", "tensor"),
        P(),
        P(None, "tensor"),
        P(None, "tensor"),
        P(None, "tensor"),
        P(),
        P(),
        P("tensor", None),
        P(),
        P(None, "tensor"),
        P(None, "tensor"),
        P("tensor", None),
    )
    return jax.shard_map(body, mesh=mesh, in_specs=in_specs, out_specs=out_specs, check_vma=False)
```

```python
import math
import functools
import jax
import jax.numpy as jnp
from jax import lax
from jax.experimental import pallas as pl
from jax.experimental.pallas import tpu as pltpu
from jax.sharding import PartitionSpec as P

HEAD_SIZE = 64
MESH = pl.DeviceIdType.MESH


def add_into(out, parts, step):
    lead = out.shape[0]
    rows = out.shape[1]
    per = rows // step

    def add_step(i, _):
        b = i // per
        r = pl.multiple_of((i % per) * step, 16)
        total = parts[0][b, pl.ds(r, step), :].astype(jnp.float32)
        for part in parts[1:]:
            total = total + part[b, pl.ds(r, step), :].astype(jnp.float32)
        out[b, pl.ds(r, step), :] = total.astype(jnp.bfloat16)
        return 0

    lax.fori_loop(0, lead * per, add_step, 0)


(T1P, T1M, I1P, I1M, M1P, M1M, T2P, T2M, I2P, I2M, M2P, M2M, Y, A2P, A2M, F2P, F2M, A1P, A1M, F1P, F1M, YA, YB, YC, YD) = range(25)
KEYS = 25


class Chunk:
    def __init__(self, src, dst, t1, r1, m1, s1, t2, r2, m2, s2, yb, send, recv, step, where):
        self.src, self.dst = src, dst
        self.t1, self.r1, self.m1, self.s1 = t1, r1, m1, s1
        self.t2, self.r2, self.m2, self.s2, self.yb = t2, r2, m2, s2, yb
        self.send, self.recv, self.step = send, recv, step
        y, z, x = where
        self.where = where

        def dev(yy, zz, xx):
            return {"dp": (yy * 4 + zz) * 4 + xx}

        up = lambda v: lax.rem(v + 1, 4)
        down = lambda v: lax.rem(v + 3, 4)
        xp, xm = dev(y, z, up(x)), dev(y, z, down(x))
        zp, zm = dev(y, up(z), x), dev(y, down(z), x)
        self.ynb = dev(1 - y, z, x)
        self.first = ((x, xp, xm), (z, zp, zm))
        self.second = ((z, zp, zm), (x, xp, xm))
        self.live = {}
        R, C = src.shape[3:]
        self.lo = (pl.ds(0, R // 2), pl.ds(0, C))
        self.hi = (pl.ds(R // 2, R // 2), pl.ds(0, C))

    def go(self, h, name, src, dst, device):
        k = h * KEYS + name
        c = pltpu.make_async_remote_copy(
            src_ref=src, dst_ref=dst, send_sem=self.send.at[k], recv_sem=self.recv.at[k],
            device_id=device, device_id_type=MESH)
        c.start()
        self.live[h, name] = c

    def got(self, h, *names):
        for n in names:
            self.live[h, n].wait_recv()

    def start1(self):
        for h in range(2):
            p, plus, minus = self.first[h]
            k2, kp, km = lax.rem(p + 2, 4), lax.rem(p + 1, 4), lax.rem(p + 3, 4)
            H, T, R = self.src.at[h], self.t1.at[h], self.r1.at[h]
            self.go(h, T1P, H.at[k2, pl.ds(0, 2)], T.at[0], plus)
            self.go(h, T1M, H.at[k2, pl.ds(2, 2)], T.at[1], minus)
            self.go(h, I1P, H.at[kp, pl.ds(2, 2)], R.at[0, pl.ds(2, 2)], plus)
            self.go(h, I1M, H.at[km, pl.ds(0, 2)], R.at[1, pl.ds(0, 2)], minus)

    def mid1(self):
        for h in range(2):
            p, plus, minus = self.first[h]
            kp, km = lax.rem(p + 1, 4), lax.rem(p + 3, 4)
            H, T, R, M = self.src.at[h], self.t1.at[h], self.r1.at[h], self.m1.at[h]
            self.got(h, T1P)
            add_into(M.at[0], (H.at[kp, pl.ds(0, 2)], T.at[0]), self.step)
            self.go(h, M1P, M.at[0], R.at[0, pl.ds(0, 2)], plus)
            self.got(h, T1M)
            add_into(M.at[1], (H.at[km, pl.ds(2, 2)], T.at[1]), self.step)
            self.go(h, M1M, M.at[1], R.at[1, pl.ds(2, 2)], minus)

    def fin1(self):
        for h in range(2):
            p = self.first[h][0]
            R = self.r1.at[h]
            self.got(h, I1P, I1M, M1P, M1M)
            add_into(self.s1.at[h], (self.src.at[h, p], R.at[0], R.at[1]), self.step)
            p, plus, minus = self.second[h]
            k2, kp, km = lax.rem(p + 2, 4), lax.rem(p + 1, 4), lax.rem(p + 3, 4)
            H, T, R, lo, hi = self.s1.at[h], self.t2.at[h], self.r2.at[h], self.lo, self.hi
            self.go(h, T2P, H.at[(k2,) + lo], T.at[lo], plus)
            self.go(h, T2M, H.at[(k2,) + hi], T.at[hi], minus)
            self.go(h, I2P, H.at[(kp,) + hi], R.at[(0,) + hi], plus)
            self.go(h, I2M, H.at[(km,) + lo], R.at[(1,) + lo], minus)

    def mid2(self):
        for h in range(2):
            p, plus, minus = self.second[h]
            kp, km = lax.rem(p + 1, 4), lax.rem(p + 3, 4)
            R, own = self.r2.at[h], (pl.ds(h, 1),)
            for name, arrived, k, part, slot, to in ((M2P, T2P, kp, self.lo, 0, plus), (M2M, T2M, km, self.hi, 1, minus)):
                self.got(h, arrived)
                add_into(self.m2.at[own + part], (self.s1.at[(h, pl.ds(k, 1)) + part], self.t2.at[own + part]), 16)
                self.go(h, name, self.m2.at[(h,) + part], R.at[(slot,) + part], to)

    def fin2(self):
        for h in range(2):
            p = self.second[h][0]
            R = self.r2.at[h]
            self.got(h, I2P, I2M, M2P, M2M)
            add_into(self.s2.at[pl.ds(h, 1)], (self.s1.at[h, pl.ds(p, 1)], R.at[pl.ds(0, 1)], R.at[pl.ds(1, 1)]), self.step)
            self.go(h, Y, self.s2.at[h], self.yb.at[h], self.ynb)

    def finy(self):
        for h in range(2):
            a = self.first[h][0]
            p, plus, minus = self.second[h]
            self.got(h, Y)
            add_into(self.dst.at[h, a, pl.ds(p, 1)], (self.s2.at[pl.ds(h, 1)], self.yb.at[pl.ds(h, 1)]), self.step)
            blk = self.dst.at[h, a, p]
            self.go(h, A2P, blk, blk, plus)
            self.go(h, A2M, blk, blk, minus)

    def ag2(self):
        for h in range(2):
            a = self.first[h][0]
            p, plus, minus = self.second[h]
            kp, km = lax.rem(p + 1, 4), lax.rem(p + 3, 4)
            self.got(h, A2P)
            blk = self.dst.at[(h, a, km) + self.lo]
            self.go(h, F2P, blk, blk, plus)
            self.got(h, A2M)
            blk = self.dst.at[(h, a, kp) + self.hi]
            self.go(h, F2M, blk, blk, minus)

    def ag1s(self):
        for h in range(2):
            p, plus, minus = self.first[h]
            self.got(h, F2P, F2M)
            blk = self.dst.at[h, p]
            self.go(h, A1P, blk, blk, plus)
            self.go(h, A1M, blk, blk, minus)

    def ag1(self):
        for h in range(2):
            p, plus, minus = self.first[h]
            kp, km = lax.rem(p + 1, 4), lax.rem(p + 3, 4)
            self.got(h, A1P)
            blk = self.dst.at[h, km, pl.ds(0, 2)]
            self.go(h, F1P, blk, blk, plus)
            self.got(h, A1M)
            blk = self.dst.at[h, kp, pl.ds(2, 2)]
            self.go(h, F1M, blk, blk, minus)

    def end(self):
        for h in range(2):
            self.got(h, F1P, F1M)
        for c in self.live.values():
            c.wait_send()

    def stages(self):
        return [self.start1, self.mid1, self.fin1, self.mid2, self.fin2, self.finy, self.ag2, self.ag1s, self.ag1, self.end]


class HalfChunk(Chunk):
    def __init__(self, src, whole, *rest):
        *_, where = rest
        super().__init__(src, whole.at[where[0]], *rest)
        R, C = src.shape[3:]
        self.lo = (pl.ds(0, R), pl.ds(0, 640))
        self.hi = (pl.ds(0, R), pl.ds(640, C - 640))

    def fin2(self):
        for h in range(2):
            a = self.first[h][0]
            p, plus, minus = self.second[h]
            R = self.r2.at[h]
            self.got(h, I2P, I2M, M2P, M2M)
            add_into(self.dst.at[h, a, pl.ds(p, 1)], (self.s1.at[h, pl.ds(p, 1)], R.at[pl.ds(0, 1)], R.at[pl.ds(1, 1)]), self.step)
            blk = self.dst.at[h, a, p]
            self.go(h, A2P, blk, blk, plus)
            self.go(h, A2M, blk, blk, minus)

    def across(self, h, name, k):
        blk = self.dst.at[h, k]
        self.go(h, name, blk, blk, self.ynb)

    def ya(self):
        for h in range(2):
            self.across(h, YA, self.first[h][0])

    def ybc(self):
        for h in range(2):
            p = self.first[h][0]
            self.across(h, YB, lax.rem(p + 3, 4))
            self.across(h, YC, lax.rem(p + 1, 4))

    def last(self):
        for h in range(2):
            self.got(h, F1P, F1M)

    def yd(self):
        for h in range(2):
            self.across(h, YD, lax.rem(self.first[h][0] + 2, 4))

    def end(self):
        for h in range(2):
            self.got(h, YA, YB, YC, YD)
        for c in self.live.values():
            c.wait_send()


def coords():
    d = lax.axis_index("dp")
    return d // 16, (d // 4) % 4, d % 4


def scratch_for(shape):
    _, _, _, R, C = shape
    bf = jnp.bfloat16
    return [
        pltpu.VMEM((2, 2, 2, R, C), bf), pltpu.VMEM((2, 2, 4, R, C), bf), pltpu.VMEM((2, 2, 2, R, C), bf), pltpu.VMEM((2, 4, R, C), bf),
        pltpu.VMEM((2, R, C), bf), pltpu.VMEM((2, 2, R, C), bf), pltpu.VMEM((2, R, C), bf), pltpu.VMEM((2, R, C), bf), pltpu.VMEM((2, R, C), bf),
        pltpu.SemaphoreType.DMA((2 * KEYS,)), pltpu.SemaphoreType.DMA((2 * KEYS,)),
    ]

NS = 11

def tensor_place():
    t = lax.axis_index("tensor")
    core, side = lax.rem(t, 2), t // 2
    return side, core, side * 2 + (1 - core), (1 - side) * 2 + core


def send(src, dst, sems, k, peer):
    c = pltpu.make_async_remote_copy(
        src_ref=src, dst_ref=dst, send_sem=sems[0].at[k], recv_sem=sems[1].at[k],
        device_id={"tensor": peer}, device_id_type=MESH)
    c.start()
    return c


def greet(sib, far):
    barrier = pltpu.get_barrier_semaphore()
    for peer in (sib, far):
        pl.semaphore_signal(barrier, inc=1, device_id={"tensor": peer}, device_id_type=MESH)
    pl.semaphore_wait(barrier, 2)


def columns(block):
    return pl.ds(pl.multiple_of(block * 256, 256), 256)


def sum_steps(part, out, low, near, mid, away, sems, base, place, scatter):
    side, core, sib, far = place
    live = []

    def one():
        low[...] = part[...].astype(jnp.bfloat16)
        for s in range(2):
            live.append(send(low.at[:, columns(s * 2 + 1 - core)], near.at[s], sems, base + s, sib))

    def two():
        order = (1 - side, side)
        for s in range(2):
            live[s].wait_recv()
        for i, s in enumerate(order):
            mid[s] = (low[:, columns(s * 2 + core)].astype(jnp.float32) + near[s].astype(jnp.float32)).astype(jnp.bfloat16)
            if i == 0 or not scatter:
                live.append(send(mid.at[s], away.at[s], sems, base + 2 + i, far))

    def three():
        if scatter:
            live[2].wait_recv()
            out[...] = mid[side].astype(jnp.float32) + away[side].astype(jnp.float32)
            return
        for i, s in enumerate((1 - side, side)):
            live[2 + i].wait_recv()
        for i, s in enumerate((1 - side, side)):
            there = out.at[:, columns(s * 2 + core)]
            out[:, columns(s * 2 + core)] = (mid[s].astype(jnp.float32) + away[s].astype(jnp.float32)).astype(jnp.bfloat16)
            live.append(send(there, there, sems, base + 4 + i, sib))

    def four():
        for c in live[4:]:
            c.wait_recv()
        for c in live:
            c.wait_send()

    return [one, two, three, four]


class SmallSum:
    def __init__(self, where, vec, out, slots, mine, send_sem, recv_sem):
        y, z, x = where
        self.vec, self.out, self.slots, self.mine = vec, out, slots, mine
        self.sems = (send_sem, recv_sem)
        self.axes = (
            (x, 4, lambda v: (y * 4 + z) * 4 + v),
            (z, 4, lambda v: (y * 4 + v) * 4 + x),
            (y, 2, lambda v: (v * 4 + z) * 4 + x),
        )
        self.live = []

    def begin(self, s, value):
        p, n, dev = self.axes[s]
        self.mine[s] = value
        self.slots[s, p] = value
        self.live = []
        for i in range(1, n):
            k = s * 3 + i - 1
            c = pltpu.make_async_remote_copy(
                src_ref=self.mine.at[s], dst_ref=self.slots.at[s, p], send_sem=self.sems[0].at[k], recv_sem=self.sems[1].at[k],
                device_id={"dp": dev(lax.rem(p + i, n))}, device_id_type=MESH)
            c.start()
            self.live.append(c)

    def close(self, s):
        for c in self.live:
            c.wait()
        value = self.slots[s, 0]
        for i in range(1, self.axes[s][1]):
            value = value + self.slots[s, i]
        return value

    def one(self):
        self.begin(0, self.vec[...])

    def two(self):
        self.begin(1, self.close(0))

    def three(self):
        self.begin(2, self.close(1))

    def four(self):
        self.out[...] = self.close(2)


def small_steps(v, out, near, mid, away, sems, base, place):
    side, core, sib, far = place
    live = []

    def one():
        live.append(send(v, near, sems, base, sib))

    def two():
        live[0].wait()
        mid[...] = v[...] + near[...]
        live.append(send(mid, away, sems, base + 1, far))

    def three():
        live[1].wait()
        out[...] = mid[...] + away[...]

    return [one, two, three]


def swap_halves(v):
    n = v.shape[1]
    lane = lax.broadcasted_iota(jnp.int32, v.shape, 1) % 64
    return jnp.where(lane < 32, pltpu.roll(v, n - 32, 1), pltpu.roll(v, 32, 1))


def head_means(v, heads):
    return [jnp.mean(v[:, 64 * h:64 * h + 64], axis=-1, keepdims=True) for h in range(heads)]


def spread(cols, heads):
    return jnp.concatenate([jnp.broadcast_to(c, (c.shape[0], 64)) for c in cols], axis=1)


CHUNK_SHAPES = ((2, 4, 4, 16, 1152), (2, 4, 4, 32, 1152), (2, 4, 4, 32, 1152), (2, 4, 4, 32, 768))
SUM_SHAPES = ((2,) + CHUNK_SHAPES[0],) + CHUNK_SHAPES[1:]


def big_kernel(*refs):
    (
        r_tokens, r_cotangent, r_lengths, r_attn_gain, r_mlp_gain, r_q_gain, r_k_gain,
        r_w_query, r_w_key, r_w_value, r_w_output, h_gate, h_up, h_down,
    ) = refs[:14]
    h_sums, (r_vec_sum, r_block_out, r_input_grad) = refs[14:18], refs[18:21]
    rest = refs[21:]
    groups = [rest[NS * c:NS * c + NS] for c in range(4)]
    rest = rest[NS * 4:]
    small_refs, grads, sums, rest = rest[:4], rest[4:8], rest[8:12], rest[12:]
    (r_vec, r_d_two, r_own, r_d_one, r_gains, r_gains_sum, r_part, r_d_hidden, r_d_low, r_d_qkv) = rest[:10]
    (r_x, r_cot, r_normed_one, r_normed_two, r_attended, r_hidden, r_d_two_part, r_mlp_part) = rest[10:18]
    (r_q_low, r_k_low, r_v_low, r_q_plain, r_k_plain, r_q_inv, r_k_inv, r_cosine, r_sine, r_p, r_heads_out) = rest[18:29]
    (r_acts, r_d_gate, r_d_up, w_gate, w_up, w_down, r_cots) = rest[29:36]
    rest = rest[36:]
    r_act = r_acts.at[pl.ds(0, 144)]
    ts, tb, tc, ta, td = rest[:4], rest[4:8], rest[8:12], rest[12:16], rest[16:19]
    sems, load_sem, store_sem = rest[19:21], rest[21], rest[22]
    where, place = coords(), tensor_place()
    side, core, sib, far = place
    me = side * 2 + core
    y, z, x = where
    f32, bf = jnp.float32, jnp.bfloat16
    loads = []
    for k, (there, here) in enumerate(((h_gate, w_gate), (h_up, w_up), (h_down, w_down))):
        loads.append(pltpu.make_async_copy(there, here, load_sem.at[k]))
        loads[k].start()
    barrier = pltpu.get_barrier_semaphore()
    peers = [(y, z, lax.rem(x + k, 4)) for k in (1, 2, 3)] + [(y, lax.rem(z + k, 4), x) for k in (1, 2, 3)] + [(1 - y, z, x)]
    for a, b, c in peers:
        pl.semaphore_signal(barrier, inc=1, device_id={"dp": (a * 4 + b) * 4 + c}, device_id_type=MESH)
    for peer in (sib, far):
        pl.semaphore_signal(barrier, inc=1, device_id={"tensor": peer}, device_id_type=MESH)
    pl.semaphore_wait(barrier, len(peers) + 2)

    c0 = HalfChunk(grads[0], sums[0], *groups[0], 16, where)
    c1, c2, c3 = [Chunk(grads[c], sums[c], *groups[c], 16, where) for c in range(1, 4)]
    r_attn = grads[3]
    small = SmallSum(where, r_vec, r_vec_sum, *small_refs)
    attended = sum_steps(r_part, r_attended, *ts, sems, 0, place, False)
    two = sum_steps(r_d_two_part, r_d_two, *ta, sems, 6, place, False)
    own = sum_steps(r_mlp_part, r_own, *tb, sems, 12, place, True)
    one = sum_steps(r_part, r_d_one, *tc, sems, 18, place, False)
    gains = small_steps(r_gains, r_gains_sum, *td, sems, 24, place)
    rows = r_x.shape[0]
    stores = []

    def leave(c, chunk):
        def finish():
            chunk.end()
            out = pltpu.make_async_copy(sums[c], h_sums[c], store_sem.at[c])
            out.start()
            stores.append(out)

        return finish

    def row_blocks(step, start):
        return lax.fori_loop(0, rows // 16, lambda b, v: step(pl.ds(pl.multiple_of(b * 16, 16), 16), v), start)

    pairs = ((r_tokens, r_x), (r_cotangent, r_cot))
    moves = {}

    def gather_start():
        for k, (v, o) in enumerate(pairs):
            there = o.at[:, columns(me)]
            moves[k] = (send(v, there, sems, 26 + 3 * k, far), send(v, there, sems, 27 + 3 * k, sib))
        for v, o in pairs:
            o[:, columns(me)] = v[...]

    def gather_pass(k):
        moves[k][0].wait_recv()
        there = pairs[k][1].at[:, columns(far)]
        moves[k + 2] = (send(there, there, sems, 28 + 3 * k, sib),)

    def gather_end(k):
        moves[k][0].wait_send()
        moves[k][1].wait()
        moves[k + 2][0].wait()

    def tables():
        lengths = r_lengths[...]
        one_length = [lengths[:, k:k + 1] for k in range(4)]
        ends = [one_length[0]]
        for k in range(1, 4):
            ends.append(ends[-1] + one_length[k])

        def segment(row):
            total = jnp.zeros(row.shape, jnp.int32)
            for end in ends:
                total = total + jnp.where(row >= end, 1, 0)
            return total

        row = lax.broadcasted_iota(jnp.int32, (rows, 128), 0)
        start = jnp.zeros(row.shape, jnp.int32)
        for end, length in zip(ends, one_length):
            start = start + jnp.where(row >= end, length, 0)
        lane = lax.broadcasted_iota(jnp.int32, (rows, 128), 1) % 64
        power = (lane % 32).astype(f32) * (-2.0 / HEAD_SIZE)
        angles = (row - start).astype(f32) * jnp.exp(power * math.log(THETA))
        cosine, sine = jnp.cos(angles), jnp.sin(angles)
        sine = jnp.where(lane < 32, -sine, sine)
        for k in (0, 128):
            r_cosine[:, k:k + 128] = cosine
            r_sine[:, k:k + 128] = sine
        query_row = lax.broadcasted_iota(jnp.int32, (rows, rows), 0)
        key_row = lax.broadcasted_iota(jnp.int32, (rows, rows), 1)
        moves[9] = (segment(query_row) == segment(key_row)) & (query_row >= key_row)

    def attn_norm():
        gain = r_attn_gain[...]

        def block(at, v):
            resid = r_x[at, :].astype(f32)
            inverse = lax.rsqrt(jnp.mean(resid * resid, axis=-1, keepdims=True) + EPS)
            r_normed_one[at, :] = (resid * inverse * gain).astype(bf)
            return v

        row_blocks(block, 0)

    def attention():
        normed = r_normed_one[...]
        r_v_low[...] = jnp.dot(normed, r_w_value[...], preferred_element_type=f32).astype(bf)
        for weight, gain, low, plain_ref, inv_ref, heads in (
            (r_w_query, r_q_gain, r_q_low, r_q_plain, r_q_inv, 4), (r_w_key, r_k_gain, r_k_low, r_k_plain, r_k_inv, 2)):
            width = 64 * heads
            raw = jnp.dot(normed, weight[...], preferred_element_type=f32)
            inv = spread([lax.rsqrt(m + EPS) for m in head_means(raw * raw, heads)], heads)
            plain = raw * inv
            inv_ref[...] = inv
            plain_ref[...] = plain
            scaled = plain * jnp.concatenate([gain[...]] * heads, axis=1)
            low[...] = (scaled * r_cosine[:, :width] + swap_halves(scaled) * r_sine[:, :width]).astype(bf)
        out = []
        for h in range(4):
            at = slice(64 * (h // 2), 64 * (h // 2) + 64)
            scores = dot_last(r_q_low[:, 64 * h:64 * h + 64], r_k_low[:, at]) * HEAD_SIZE ** (-0.5)
            scores = jnp.where(moves[9], scores, -1e30)
            weights = jnp.exp(scores - jnp.max(scores, axis=-1, keepdims=True))
            p = weights / jnp.sum(weights, axis=-1, keepdims=True)
            r_p[h] = p
            out.append(jnp.dot(p.astype(bf), r_v_low[:, at], preferred_element_type=f32))
        heads_out = jnp.concatenate(out, axis=1).astype(bf)
        r_heads_out[...] = heads_out
        r_part[...] = jnp.dot(heads_out, r_w_output[...], preferred_element_type=f32)

    def mlp_norm():
        gain = r_mlp_gain[...]

        def block(at, v):
            hidden = r_x[at, :].astype(f32) + r_attended[at, :].astype(f32)
            r_hidden[at, :] = hidden
            inverse = lax.rsqrt(jnp.mean(hidden * hidden, axis=-1, keepdims=True) + EPS)
            r_normed_two[at, :] = (hidden * inverse * gain).astype(bf)
            return v

        row_blocks(block, 0)

    def mlp_units():
        for load in loads:
            load.wait()

        def tile(j, v):
            at = pl.ds(pl.multiple_of(j * 384, 128), 384)
            gate = jnp.dot(r_normed_two[...], w_gate[:, at], preferred_element_type=f32)
            up = jnp.dot(r_normed_two[...], w_up[:, at], preferred_element_type=f32)
            s = jax.nn.sigmoid(gate)
            silu = gate * s
            r_act[:, at] = (silu * up).astype(bf)
            d_act = dot_last(r_cot[...], w_down[at, :])
            r_d_gate[:, at] = (d_act * up * s * (1.0 + gate * (1.0 - s))).astype(bf)
            r_d_up[:, at] = (d_act * silu).astype(bf)
            return v

        lax.fori_loop(0, 3, tile, 0)

    def weight_grad(left, right, out):
        def tile(j, v):
            part = dot_rows(left[:, columns(j)], right[...]).astype(bf)
            out[j // 2, pl.ds((j % 2) * 2, 2)] = part.reshape(2, 4, 32, right.shape[1])
            return v

        return lambda: lax.fori_loop(0, 4, tile, 0)

    def swap_y(k, src, dst):
        c = pltpu.make_async_remote_copy(
            src_ref=src, dst_ref=dst, send_sem=sems[0].at[32 + k], recv_sem=sems[1].at[32 + k],
            device_id={"dp": c0.ynb["dp"]}, device_id_type=MESH)
        c.start()
        moves[20 + k] = c

    def swap_cot():
        half = lambda v: pl.ds(pl.multiple_of(v * 512, 512), 512)
        swap_y(0, r_cot.at[:, half(1 - y)], r_cots.at[pl.ds(144, 144)])
        r_cots[0:144, :] = r_cot[:, half(y)]

    def swap_act():
        swap_y(1, r_act, r_acts.at[pl.ds(144, 144)])

    def down_grad():
        moves[20].wait()
        moves[21].wait()

        def tile(j, v):
            grads[0][j] = dot_rows(r_cots[:, columns(j)], r_acts[...]).astype(bf).reshape(4, 4, 16, 1152)
            return v

        lax.fori_loop(0, 2, tile, 0)

    gate_grad = weight_grad(r_normed_two, r_d_gate, grads[1])
    up_grad = weight_grad(r_normed_two, r_d_up, grads[2])

    def mlp_back():
        def tile(j, v):
            at = columns(j)
            r_d_two_part[:, at] = dot_last(r_d_gate[...], w_gate[at, :]) + dot_last(r_d_up[...], w_up[at, :])
            return v

        lax.fori_loop(0, 4, tile, 0)

    def mlp_out():
        def tile(j, v):
            at = columns(j)
            r_mlp_part[:, at] = jnp.dot(r_act[...], w_down[:, at], preferred_element_type=f32)
            return v

        lax.fori_loop(0, 4, tile, 0)

    def back_mlp_norm():
        gain = r_mlp_gain[...]

        def block(b, total):
            at = pl.ds(pl.multiple_of(b * 16, 16), 16)
            hidden = r_hidden[at, :]
            inverse = lax.rsqrt(jnp.mean(hidden * hidden, axis=-1, keepdims=True) + EPS)
            plain = hidden * inverse
            d_two = r_d_two[at, :].astype(jnp.float32)
            u = d_two * gain
            d_hidden = r_cot[at, :].astype(jnp.float32) + inverse * (
                u - plain * jnp.mean(u * plain, axis=-1, keepdims=True))
            r_d_hidden[at, :] = d_hidden
            r_d_low[at, :] = d_hidden.astype(jnp.bfloat16)
            return total + jnp.sum(d_two * plain, axis=0, keepdims=True)

        total = lax.fori_loop(0, rows // 16, block, jnp.zeros((1, 1024), jnp.float32))
        r_vec[...] = jnp.zeros((8, 1024), jnp.float32)
        r_vec[1:2, :] = total
        mine = columns(me)
        r_block_out[...] = (r_hidden[:, mine] + r_own[...]).astype(jnp.bfloat16)

    hold = {}

    def back_output():
        d_low = r_d_low[...]
        hold[0] = dot_last(d_low, r_w_output[...]).astype(jnp.bfloat16)
        r_attn[:, :, :, :, 512:768] = dot_rows(d_low, r_heads_out[...]).astype(jnp.bfloat16).reshape(2, 4, 4, 32, 256)

    def back_scores():
        d_heads = hold[0]
        scale = HEAD_SIZE ** (-0.5)
        d_query, d_key, d_value = [], [], []
        for j in range(2):
            at = slice(64 * j, 64 * j + 64)
            key, value = r_k_low[:, at], r_v_low[:, at]
            dk, dv = 0.0, 0.0
            for h in (2 * j, 2 * j + 1):
                p = r_p[h]
                dh = d_heads[:, 64 * h:64 * h + 64]
                d_probs = dot_last(dh, value)
                ds = (p * (d_probs - jnp.sum(d_probs * p, axis=-1, keepdims=True))).astype(jnp.bfloat16)
                d_query.append(jnp.dot(ds, key, preferred_element_type=jnp.float32) * scale)
                dk = dk + dot_rows(ds, r_q_low[:, 64 * h:64 * h + 64])
                dv = dv + dot_rows(p.astype(jnp.bfloat16), dh)
            d_key.append(dk * scale)
            d_value.append(dv)
        r_d_qkv[:, 384:512] = jnp.concatenate(d_value, axis=1).astype(jnp.bfloat16)
        hold[1] = jnp.concatenate(d_query, axis=1)
        hold[2] = jnp.concatenate(d_key, axis=1)

    def back_head_norm():
        r_gains[...] = jnp.zeros((8, 128), jnp.float32)
        for d, plain_ref, gain_ref, inv_ref, heads, put, place_at in (
            (hold[1], r_q_plain, r_q_gain, r_q_inv, 4, 0, 0), (hold[2], r_k_plain, r_k_gain, r_k_inv, 2, 256, 64)):
            width = 64 * heads
            turned = d * r_cosine[:, :width] - swap_halves(d) * r_sine[:, :width]
            plain = plain_ref[...]
            sums = jnp.sum(turned * plain, axis=0, keepdims=True)
            total = sums[:, :64]
            for h in range(1, heads):
                total = total + sums[:, 64 * h:64 * h + 64]
            r_gains[0:1, place_at:place_at + 64] = total
            u = turned * jnp.concatenate([gain_ref[...]] * heads, axis=1)
            inv = inv_ref[...]
            back = inv * (u - plain * spread(head_means(u * plain, heads), heads))
            r_d_qkv[:, put:put + width] = back.astype(jnp.bfloat16)

    def back_project():
        dq, dk, dv = r_d_qkv[:, :256], r_d_qkv[:, 256:384], r_d_qkv[:, 384:512]
        r_part[...] = (
            dot_last(dq, r_w_query[...]) + dot_last(dk, r_w_key[...]) + dot_last(dv, r_w_value[...]))

    def back_attn_weights():
        r_attn[:, :, :, :, 0:512] = dot_rows(r_normed_one[...], r_d_qkv[...]).astype(jnp.bfloat16).reshape(2, 4, 4, 32, 512)

    def back_attn_norm():
        gain = r_attn_gain[...]
        mine = columns(me)

        def block(b, total):
            at = pl.ds(pl.multiple_of(b * 16, 16), 16)
            resid = r_x[at, :].astype(jnp.float32)
            inverse = lax.rsqrt(jnp.mean(resid * resid, axis=-1, keepdims=True) + EPS)
            plain = resid * inverse
            d_one = r_d_one[at, :].astype(jnp.float32)
            u = d_one * gain
            r_d_hidden[at, :] = r_d_hidden[at, :] + inverse * (
                u - plain * jnp.mean(u * plain, axis=-1, keepdims=True))
            return total + jnp.sum(d_one * plain, axis=0, keepdims=True)

        total = lax.fori_loop(0, rows // 16, block, jnp.zeros((1, 1024), jnp.float32))
        r_vec[0:1, :] = total
        r_vec[2:3, 0:128] = r_gains_sum[0:1, :]
        r_input_grad[...] = r_d_hidden[:, mine].astype(jnp.bfloat16)

    for step in (
        gather_start, tables, lambda: gather_pass(0), lambda: gather_pass(1), lambda: gather_end(0), attn_norm, attention, attended[0],
        lambda: gather_end(1), attended[1], attended[2], swap_cot, attended[3], mlp_norm, mlp_units, swap_act, gate_grad, c1.start1,
        mlp_back, two[0], up_grad, two[1], c2.start1, down_grad, c0.start1, mlp_out, two[2], own[0], two[3], own[1], c1.mid1, own[2],
        c0.mid1, own[3], back_mlp_norm, back_output, c2.mid1, c1.fin1, back_scores, c0.fin1, back_head_norm, back_project, one[0],
        gains[0], back_attn_weights, c3.start1, c0.mid2, c1.mid2, one[1], gains[1], c0.fin2, c2.fin1, one[2], gains[2], c0.ag2, c1.fin2,
        one[3], back_attn_norm, small.one, c0.ag1s, c3.mid1, c2.mid2, c1.finy, small.two, c0.ag1, c2.fin2, c0.ya, c3.fin1, c1.ag2,
        c2.finy, c3.mid2, small.three, c1.ag1s, c3.fin2, c0.ybc, c0.last, c0.yd, c2.ag2, c3.finy, c2.ag1s, c1.ag1, c3.ag2, small.four,
        c3.ag1s, c2.ag1, leave(1, c1), c3.ag1, leave(0, c0), leave(2, c2), leave(3, c3),
    ):
        step()
    for out in stores:
        out.wait()


def big(arrays):
    V, A = pl.BlockSpec(memory_space=pltpu.VMEM), pl.BlockSpec(memory_space=pl.ANY)
    f32, bf = jnp.float32, jnp.bfloat16
    S = jax.ShapeDtypeStruct
    out_shape = [S(s, bf) for s in SUM_SHAPES] + [S((8, 1024), f32), S((144, 256), bf), S((144, 256), bf)]
    B = lambda *shape: pltpu.VMEM(shape, bf)
    F = lambda *shape: pltpu.VMEM(shape, f32)
    D = lambda n: pltpu.SemaphoreType.DMA((n,))
    scratch = sum([scratch_for(s) for s in CHUNK_SHAPES], [])
    scratch += [F(3, 4, 8, 1024), F(3, 8, 1024), D(9), D(9)]
    scratch += [B(*s) for s in CHUNK_SHAPES] + [B(*s) for s in SUM_SHAPES]
    scratch += [F(8, 1024), B(144, 1024), F(144, 256), B(144, 1024), F(8, 128), F(8, 128), F(144, 1024), F(144, 1024), B(144, 1024), B(144, 512)]
    scratch += [B(144, 1024), B(144, 1024), B(144, 1024), B(144, 1024), B(144, 1024), F(144, 1024), F(144, 1024), F(144, 1024)]
    scratch += [B(144, 256), B(144, 128), B(144, 128), F(144, 256), F(144, 128), F(144, 256), F(144, 128), F(144, 256), F(144, 256), F(4, 144, 144), B(144, 256)]
    scratch += [B(288, 1152), B(144, 1152), B(144, 1152), B(1024, 1152), B(1024, 1152), B(1152, 1024), B(288, 512)]
    scratch += ([B(144, 1024)] + [B(2, 144, 256)] * 3) * 4 + [F(8, 128)] * 3
    scratch += [D(34), D(34), D(3), D(4)]
    return pl.pallas_call(
        big_kernel, out_shape=out_shape, in_specs=[V] * 11 + [A] * 3, out_specs=[A] * 4 + [V] * 3, scratch_shapes=scratch,
        compiler_params=pltpu.CompilerParams(collective_id=0, has_side_effects=True, vmem_limit_bytes=61 * 1024 * 1024),
        name="block",
    )(*arrays)


def widen_kernel(gate, up, down, attn, vec, block, grad, o_gate, o_up, o_down, o_q, o_k, o_v, o_out, o_attn, o_mlp, o_qg, o_kg, o_block, o_grad):
    o_gate[...] = gate[...].astype(jnp.float32)
    o_up[...] = up[...].astype(jnp.float32)
    o_down[...] = down[...].astype(jnp.float32).T
    wide = attn[...].astype(jnp.float32)
    o_q[...] = wide[:, :256]
    o_k[...] = wide[:, 256:384]
    o_v[...] = wide[:, 384:512]
    o_out[...] = wide[:, 512:768].T

    @pl.when(pl.program_id(0) == 0)
    def _():
        o_attn[...] = vec[0, :]
        o_mlp[...] = vec[1, :]
        o_qg[...] = vec[2, 0:64]
        o_kg[...] = vec[2, 64:128]
        o_block[...] = block[...]
        o_grad[...] = grad[...]


def widen(gate, up, down, attn, vec, block, grad):
    S = lambda *s: jax.ShapeDtypeStruct(s, jnp.float32)
    row = lambda w: pl.BlockSpec((128, w), lambda b: (b, 0))
    col = lambda h: pl.BlockSpec((h, 128), lambda b: (0, b))
    all_of = lambda *s: pl.BlockSpec(s, lambda b: (0,) * len(s))
    own = jax.ShapeDtypeStruct(block.shape, block.dtype)
    return pl.pallas_call(
        widen_kernel, grid=(8,),
        in_specs=[row(1152), row(1152), row(1152), row(768), all_of(8, 1024), all_of(144, 256), all_of(144, 256)],
        out_specs=[row(1152), row(1152), col(1152), row(256), row(128), row(128), col(256),
                   all_of(1024), all_of(1024), all_of(64), all_of(64), all_of(144, 256), all_of(144, 256)],
        out_shape=[S(1024, 1152), S(1024, 1152), S(1152, 1024), S(1024, 256), S(1024, 128), S(1024, 128), S(256, 1024),
                   S(1024), S(1024), S(64), S(64), own, own],
        compiler_params=pltpu.CompilerParams(vmem_limit_bytes=60 * 1024 * 1024),
        name="widen",
    )(gate, up, down, attn, vec, block, grad)


EPS = 1e-05
THETA = 1000000.0


def dot_rows(left_side, right_side):
    return lax.dot_general(
        left_side, right_side, (((0,), (0,)), ((), ())), preferred_element_type=jnp.float32
    )


def dot_last(left_side, right_side):
    return lax.dot_general(
        left_side, right_side, (((1,), (1,)), ((), ())), preferred_element_type=jnp.float32
    )


def body(
    tokens,
    lengths,
    attn_gain,
    w_query,
    key_weight,
    value_weight,
    query_gain,
    key_gain,
    w_output,
    mlp_gain,
    w_gate,
    w_up,
    w_down,
    cotangent,
):
    down, gate, up, attn, vec, block_out, input_grad = big(
        (
            tokens,
            cotangent,
            lengths,
            attn_gain[None],
            mlp_gain[None],
            query_gain[None],
            key_gain[None],
            w_query,
            key_weight,
            value_weight,
            w_output,
            w_gate,
            w_up,
            w_down,
        )
    )
    gate, up, down, w_q, w_k, w_v, w_o, attn_g, mlp_g, query_g, key_g, block_out, input_grad = widen(
        gate.reshape(1024, 1152), up.reshape(1024, 1152), down.reshape(1024, 1152), attn.reshape(1024, 768), vec, block_out, input_grad
    )
    return (block_out, input_grad, attn_g, w_q, w_k, w_v, query_g, key_g, w_o, mlp_g, gate, up, down)


def solution(mesh):
    in_specs = (
        P("dp", "tensor"),
        P("dp", None),
        P(),
        P(None, "tensor"),
        P(None, "tensor"),
        P(None, "tensor"),
        P(),
        P(),
        P("tensor", None),
        P(),
        P(None, "tensor"),
        P(None, "tensor"),
        P("tensor", None),
        P("dp", "tensor"),
    )
    out_specs = (
        P("dp", "tensor"),
        P("dp", "tensor"),
        P(),
        P(None, "tensor"),
        P(None, "tensor"),
        P(None, "tensor"),
        P(),
        P(),
        P("tensor", None),
        P(),
        P(None, "tensor"),
        P(None, "tensor"),
        P("tensor", None),
    )
    return jax.shard_map(body, mesh=mesh, in_specs=in_specs, out_specs=out_specs, check_vma=False)
```

```python
import math
import functools
import jax
import jax.numpy as jnp
from jax import lax
from jax.experimental import pallas as pl
from jax.experimental.pallas import tpu as pltpu
from jax.sharding import PartitionSpec as P

HEAD_SIZE = 64
MESH = pl.DeviceIdType.MESH


def add_into(out, parts, step):
    lead = out.shape[0]
    rows = out.shape[1]
    per = rows // step

    def add_step(i, _):
        b = i // per
        r = pl.multiple_of((i % per) * step, 16)
        total = parts[0][b, pl.ds(r, step), :].astype(jnp.float32)
        for part in parts[1:]:
            total = total + part[b, pl.ds(r, step), :].astype(jnp.float32)
        out[b, pl.ds(r, step), :] = total.astype(jnp.bfloat16)
        return 0

    lax.fori_loop(0, lead * per, add_step, 0)


(T1P, T1M, I1P, I1M, M1P, M1M, T2P, T2M, I2P, I2M, M2P, M2M, Y, A2P, A2M, F2P, F2M, A1P, A1M, F1P, F1M, YA, YB, YC, YD) = range(25)
KEYS = 25


class Chunk:
    def __init__(self, src, dst, t1, r1, m1, s1, t2, r2, m2, s2, yb, send, recv, step, where):
        self.src, self.dst = src, dst
        self.t1, self.r1, self.m1, self.s1 = t1, r1, m1, s1
        self.t2, self.r2, self.m2, self.s2, self.yb = t2, r2, m2, s2, yb
        self.send, self.recv, self.step = send, recv, step
        y, z, x = where
        self.where = where

        def dev(yy, zz, xx):
            return {"dp": (yy * 4 + zz) * 4 + xx}

        up = lambda v: lax.rem(v + 1, 4)
        down = lambda v: lax.rem(v + 3, 4)
        xp, xm = dev(y, z, up(x)), dev(y, z, down(x))
        zp, zm = dev(y, up(z), x), dev(y, down(z), x)
        self.ynb = dev(1 - y, z, x)
        self.first = ((x, xp, xm), (z, zp, zm))
        self.second = ((z, zp, zm), (x, xp, xm))
        self.live = {}
        R, C = src.shape[3:]
        self.lo = (pl.ds(0, R // 2), pl.ds(0, C))
        self.hi = (pl.ds(R // 2, R // 2), pl.ds(0, C))

    def go(self, h, name, src, dst, device):
        k = h * KEYS + name
        c = pltpu.make_async_remote_copy(
            src_ref=src, dst_ref=dst, send_sem=self.send.at[k], recv_sem=self.recv.at[k],
            device_id=device, device_id_type=MESH)
        c.start()
        self.live[h, name] = c

    def got(self, h, *names):
        for n in names:
            self.live[h, n].wait_recv()

    def start1(self):
        for h in range(2):
            self.begin(h)

    def begin(self, h):
        p, plus, minus = self.first[h]
        k2, kp, km = lax.rem(p + 2, 4), lax.rem(p + 1, 4), lax.rem(p + 3, 4)
        H, T, R = self.src.at[h], self.t1.at[h], self.r1.at[h]
        self.go(h, T1P, H.at[k2, pl.ds(0, 2)], T.at[0], plus)
        self.go(h, T1M, H.at[k2, pl.ds(2, 2)], T.at[1], minus)
        self.go(h, I1P, H.at[kp, pl.ds(2, 2)], R.at[0, pl.ds(2, 2)], plus)
        self.go(h, I1M, H.at[km, pl.ds(0, 2)], R.at[1, pl.ds(0, 2)], minus)

    def mid1(self):
        for h in range(2):
            p, plus, minus = self.first[h]
            kp, km = lax.rem(p + 1, 4), lax.rem(p + 3, 4)
            H, T, R, M = self.src.at[h], self.t1.at[h], self.r1.at[h], self.m1.at[h]
            self.got(h, T1P)
            add_into(M.at[0], (H.at[kp, pl.ds(0, 2)], T.at[0]), self.step)
            self.go(h, M1P, M.at[0], R.at[0, pl.ds(0, 2)], plus)
            self.got(h, T1M)
            add_into(M.at[1], (H.at[km, pl.ds(2, 2)], T.at[1]), self.step)
            self.go(h, M1M, M.at[1], R.at[1, pl.ds(2, 2)], minus)

    def fin1(self):
        for h in range(2):
            p = self.first[h][0]
            R = self.r1.at[h]
            self.got(h, I1P, I1M, M1P, M1M)
            add_into(self.s1.at[h], (self.src.at[h, p], R.at[0], R.at[1]), self.step)
            p, plus, minus = self.second[h]
            k2, kp, km = lax.rem(p + 2, 4), lax.rem(p + 1, 4), lax.rem(p + 3, 4)
            H, T, R, lo, hi = self.s1.at[h], self.t2.at[h], self.r2.at[h], self.lo, self.hi
            self.go(h, T2P, H.at[(k2,) + lo], T.at[lo], plus)
            self.go(h, T2M, H.at[(k2,) + hi], T.at[hi], minus)
            self.go(h, I2P, H.at[(kp,) + hi], R.at[(0,) + hi], plus)
            self.go(h, I2M, H.at[(km,) + lo], R.at[(1,) + lo], minus)

    def mid2(self):
        for h in range(2):
            p, plus, minus = self.second[h]
            kp, km = lax.rem(p + 1, 4), lax.rem(p + 3, 4)
            R, own = self.r2.at[h], (pl.ds(h, 1),)
            for name, arrived, k, part, slot, to in ((M2P, T2P, kp, self.lo, 0, plus), (M2M, T2M, km, self.hi, 1, minus)):
                self.got(h, arrived)
                add_into(self.m2.at[own + part], (self.s1.at[(h, pl.ds(k, 1)) + part], self.t2.at[own + part]), 16)
                self.go(h, name, self.m2.at[(h,) + part], R.at[(slot,) + part], to)

    def fin2(self):
        for h in range(2):
            p = self.second[h][0]
            R = self.r2.at[h]
            self.got(h, I2P, I2M, M2P, M2M)
            add_into(self.s2.at[pl.ds(h, 1)], (self.s1.at[h, pl.ds(p, 1)], R.at[pl.ds(0, 1)], R.at[pl.ds(1, 1)]), self.step)
            self.go(h, Y, self.s2.at[h], self.yb.at[h], self.ynb)

    def finy(self):
        for h in range(2):
            a = self.first[h][0]
            p, plus, minus = self.second[h]
            self.got(h, Y)
            add_into(self.dst.at[h, a, pl.ds(p, 1)], (self.s2.at[pl.ds(h, 1)], self.yb.at[pl.ds(h, 1)]), self.step)
            blk = self.dst.at[h, a, p]
            self.go(h, A2P, blk, blk, plus)
            self.go(h, A2M, blk, blk, minus)

    def ag2(self):
        for h in range(2):
            a = self.first[h][0]
            p, plus, minus = self.second[h]
            kp, km = lax.rem(p + 1, 4), lax.rem(p + 3, 4)
            self.got(h, A2P)
            blk = self.dst.at[(h, a, km) + self.lo]
            self.go(h, F2P, blk, blk, plus)
            self.got(h, A2M)
            blk = self.dst.at[(h, a, kp) + self.hi]
            self.go(h, F2M, blk, blk, minus)

    def ag1s(self):
        for h in range(2):
            p, plus, minus = self.first[h]
            self.got(h, F2P, F2M)
            blk = self.dst.at[h, p]
            self.go(h, A1P, blk, blk, plus)
            self.go(h, A1M, blk, blk, minus)

    def ag1(self):
        for h in range(2):
            p, plus, minus = self.first[h]
            kp, km = lax.rem(p + 1, 4), lax.rem(p + 3, 4)
            self.got(h, A1P)
            blk = self.dst.at[h, km, pl.ds(0, 2)]
            self.go(h, F1P, blk, blk, plus)
            self.got(h, A1M)
            blk = self.dst.at[h, kp, pl.ds(2, 2)]
            self.go(h, F1M, blk, blk, minus)

    def end(self):
        for h in range(2):
            self.got(h, F1P, F1M)
        for c in self.live.values():
            c.wait_send()

    def stages(self):
        return [self.start1, self.mid1, self.fin1, self.mid2, self.fin2, self.finy, self.ag2, self.ag1s, self.ag1, self.end]


class HalfChunk(Chunk):
    def __init__(self, src, whole, *rest):
        *_, where = rest
        super().__init__(src, whole.at[where[0]], *rest)
        R, C = src.shape[3:]
        self.lo = (pl.ds(0, R), pl.ds(0, 640))
        self.hi = (pl.ds(0, R), pl.ds(640, C - 640))

    def fin2(self):
        for h in range(2):
            a = self.first[h][0]
            p, plus, minus = self.second[h]
            R = self.r2.at[h]
            self.got(h, I2P, I2M, M2P, M2M)
            add_into(self.dst.at[h, a, pl.ds(p, 1)], (self.s1.at[h, pl.ds(p, 1)], R.at[pl.ds(0, 1)], R.at[pl.ds(1, 1)]), self.step)
            blk = self.dst.at[h, a, p]
            self.go(h, A2P, blk, blk, plus)
            self.go(h, A2M, blk, blk, minus)

    def across(self, h, name, k):
        blk = self.dst.at[h, k]
        self.go(h, name, blk, blk, self.ynb)

    def ya(self):
        for h in range(2):
            self.across(h, YA, self.first[h][0])

    def ybc(self):
        for h in range(2):
            p = self.first[h][0]
            self.across(h, YB, lax.rem(p + 3, 4))
            self.across(h, YC, lax.rem(p + 1, 4))

    def last(self):
        for h in range(2):
            self.got(h, F1P, F1M)

    def yd(self):
        for h in range(2):
            self.across(h, YD, lax.rem(self.first[h][0] + 2, 4))

    def end(self):
        for h in range(2):
            self.got(h, YA, YB, YC, YD)
        for c in self.live.values():
            c.wait_send()


def coords():
    d = lax.axis_index("dp")
    return d // 16, (d // 4) % 4, d % 4


def scratch_for(shape):
    _, _, _, R, C = shape
    bf = jnp.bfloat16
    return [
        pltpu.VMEM((2, 2, 2, R, C), bf), pltpu.VMEM((2, 2, 4, R, C), bf), pltpu.VMEM((2, 2, 2, R, C), bf), pltpu.VMEM((2, 4, R, C), bf),
        pltpu.VMEM((2, R, C), bf), pltpu.VMEM((2, 2, R, C), bf), pltpu.VMEM((2, R, C), bf), pltpu.VMEM((2, R, C), bf), pltpu.VMEM((2, R, C), bf),
        pltpu.SemaphoreType.DMA((2 * KEYS,)), pltpu.SemaphoreType.DMA((2 * KEYS,)),
    ]

NS = 11

def tensor_place():
    t = lax.axis_index("tensor")
    core, side = lax.rem(t, 2), t // 2
    return side, core, side * 2 + (1 - core), (1 - side) * 2 + core


def send(src, dst, sems, k, peer):
    c = pltpu.make_async_remote_copy(
        src_ref=src, dst_ref=dst, send_sem=sems[0].at[k], recv_sem=sems[1].at[k],
        device_id={"tensor": peer}, device_id_type=MESH)
    c.start()
    return c


def greet(sib, far):
    barrier = pltpu.get_barrier_semaphore()
    for peer in (sib, far):
        pl.semaphore_signal(barrier, inc=1, device_id={"tensor": peer}, device_id_type=MESH)
    pl.semaphore_wait(barrier, 2)


def columns(block):
    return pl.ds(pl.multiple_of(block * 256, 256), 256)


def sum_steps(part, out, low, near, mid, away, sems, base, place, scatter):
    side, core, sib, far = place
    live = []

    def one():
        low[...] = part[...].astype(jnp.bfloat16)
        for s in range(2):
            live.append(send(low.at[:, columns(s * 2 + 1 - core)], near.at[s], sems, base + s, sib))

    def fold(s):
        mid[s] = (low[:, columns(s * 2 + core)].astype(jnp.float32) + near[s].astype(jnp.float32)).astype(jnp.bfloat16)

    def two():
        if scatter:
            for s in range(2):
                live[s].wait_recv()
            fold(1 - side)
            live.append(send(mid.at[1 - side], away.at[1 - side], sems, base + 2, far))
            fold(side)
            return
        for s in range(2):
            live[s].wait_recv()
            fold(s)
            live.append(send(mid.at[s], away.at[s], sems, base + 2 + s, far))

    def three():
        if scatter:
            live[2].wait_recv()
            out[...] = mid[side].astype(jnp.float32) + away[side].astype(jnp.float32)
            return
        for s in range(2):
            live[2 + s].wait_recv()
            there = out.at[:, columns(s * 2 + core)]
            out[:, columns(s * 2 + core)] = (mid[s].astype(jnp.float32) + away[s].astype(jnp.float32)).astype(jnp.bfloat16)
            live.append(send(there, there, sems, base + 4 + s, sib))

    def four():
        for c in live[4:]:
            c.wait_recv()
        for c in live:
            c.wait_send()

    return [one, two, three, four]


class SmallSum:
    def __init__(self, where, vec, out, slots, mine, send_sem, recv_sem):
        y, z, x = where
        self.vec, self.out, self.slots, self.mine = vec, out, slots, mine
        self.sems = (send_sem, recv_sem)
        self.axes = (
            (x, 4, lambda v: (y * 4 + z) * 4 + v),
            (z, 4, lambda v: (y * 4 + v) * 4 + x),
            (y, 2, lambda v: (v * 4 + z) * 4 + x),
        )
        self.live = []

    def begin(self, s, value):
        p, n, dev = self.axes[s]
        self.mine[s] = value
        self.slots[s, p] = value
        self.live = []
        for i in range(1, n):
            k = s * 3 + i - 1
            c = pltpu.make_async_remote_copy(
                src_ref=self.mine.at[s], dst_ref=self.slots.at[s, p], send_sem=self.sems[0].at[k], recv_sem=self.sems[1].at[k],
                device_id={"dp": dev(lax.rem(p + i, n))}, device_id_type=MESH)
            c.start()
            self.live.append(c)

    def close(self, s):
        for c in self.live:
            c.wait()
        value = self.slots[s, 0]
        for i in range(1, self.axes[s][1]):
            value = value + self.slots[s, i]
        return value

    def one(self):
        self.begin(0, self.vec[...])

    def two(self):
        self.begin(1, self.close(0))

    def three(self):
        self.begin(2, self.close(1))

    def four(self):
        self.out[...] = self.close(2)


def small_steps(v, out, near, mid, away, sems, base, place):
    side, core, sib, far = place
    live = []

    def one():
        live.append(send(v, near, sems, base, sib))

    def two():
        live[0].wait()
        mid[...] = v[...] + near[...]
        live.append(send(mid, away, sems, base + 1, far))

    def three():
        live[1].wait()
        out[...] = mid[...] + away[...]

    return [one, two, three]


def swap_halves(v):
    n = v.shape[1]
    lane = lax.broadcasted_iota(jnp.int32, v.shape, 1) % 64
    return jnp.where(lane < 32, pltpu.roll(v, n - 32, 1), pltpu.roll(v, 32, 1))


def head_means(v, heads):
    return [jnp.mean(v[:, 64 * h:64 * h + 64], axis=-1, keepdims=True) for h in range(heads)]


def spread(cols, heads):
    return jnp.concatenate([jnp.broadcast_to(c, (c.shape[0], 64)) for c in cols], axis=1)


CHUNK_SHAPES = ((2, 4, 4, 16, 1152), (2, 4, 4, 32, 1152), (2, 4, 4, 32, 1152), (2, 4, 4, 32, 768))
SUM_SHAPES = ((2,) + CHUNK_SHAPES[0],) + CHUNK_SHAPES[1:]


def big_kernel(*refs):
    (
        r_tokens, r_cotangent, r_lengths, r_attn_gain, r_mlp_gain, r_q_gain, r_k_gain,
        r_w_query, r_w_key, r_w_value, r_w_output, h_gate, h_up, h_down,
    ) = refs[:14]
    h_sums, (r_vec_sum, r_block_out, r_input_grad) = refs[14:18], refs[18:21]
    rest = refs[21:]
    groups = [rest[NS * c:NS * c + NS] for c in range(4)]
    rest = rest[NS * 4:]
    small_refs, grads, sums, rest = rest[:4], rest[4:8], rest[8:12], rest[12:]
    (r_vec, r_d_two, r_own, r_d_one, r_gains, r_gains_sum, r_part, r_d_hidden, r_d_low, r_d_qkv) = rest[:10]
    (r_x, r_cot, r_normed_one, r_normed_two, r_attended, r_hidden, r_d_two_part, r_mlp_part) = rest[10:18]
    (r_q_low, r_k_low, r_v_low, r_q_plain, r_k_plain, r_q_inv, r_k_inv, r_cosine, r_sine, r_p, r_heads_out) = rest[18:29]
    (r_acts, r_d_gate, r_d_up, w_gate, w_up, w_down, r_cots, r_d_act) = rest[29:37]
    rest = rest[37:]
    r_act = r_acts.at[pl.ds(0, 144)]
    ts, tb, tc, ta, td = rest[:4], rest[4:8], rest[8:12], rest[12:16], rest[16:19]
    sems, load_sem, store_sem = rest[19:21], rest[21], rest[22]
    where, place = coords(), tensor_place()
    side, core, sib, far = place
    me = side * 2 + core
    y, z, x = where
    f32, bf = jnp.float32, jnp.bfloat16
    loads = []
    for k, (there, here) in enumerate(((h_gate, w_gate), (h_up, w_up), (h_down, w_down))):
        loads.append(pltpu.make_async_copy(there, here, load_sem.at[k]))
        loads[k].start()
    barrier = pltpu.get_barrier_semaphore()
    peers = [(y, z, lax.rem(x + k, 4)) for k in (1, 2, 3)] + [(y, lax.rem(z + k, 4), x) for k in (1, 2, 3)] + [(1 - y, z, x)]
    for a, b, c in peers:
        pl.semaphore_signal(barrier, inc=1, device_id={"dp": (a * 4 + b) * 4 + c}, device_id_type=MESH)
    for peer in (sib, far):
        pl.semaphore_signal(barrier, inc=1, device_id={"tensor": peer}, device_id_type=MESH)
    pl.semaphore_wait(barrier, len(peers) + 2)

    c0 = HalfChunk(grads[0], sums[0], *groups[0], 16, where)
    c1, c2, c3 = [Chunk(grads[c], sums[c], *groups[c], 16, where) for c in range(1, 4)]
    r_attn = grads[3]
    small = SmallSum(where, r_vec, r_vec_sum, *small_refs)
    attended = sum_steps(r_part, r_attended, *ts, sems, 0, place, False)
    two = sum_steps(r_d_two_part, r_d_two, *ta, sems, 6, place, False)
    own = sum_steps(r_mlp_part, r_own, *tb, sems, 12, place, True)
    one = sum_steps(r_part, r_d_one, *tc, sems, 18, place, False)
    gains = small_steps(r_gains, r_gains_sum, *td, sems, 24, place)
    rows = r_x.shape[0]
    stores = []

    def leave(c, chunk):
        def finish():
            chunk.end()
            out = pltpu.make_async_copy(sums[c], h_sums[c], store_sem.at[c])
            out.start()
            stores.append(out)

        return finish

    def row_blocks(step, start):
        return lax.fori_loop(0, rows // 16, lambda b, v: step(pl.ds(pl.multiple_of(b * 16, 16), 16), v), start)

    pairs = ((r_tokens, r_x), (r_cotangent, r_cot))
    moves = {}

    def gather_start():
        for k, (v, o) in enumerate(pairs):
            there = o.at[:, columns(me)]
            moves[k] = (send(v, there, sems, 26 + 3 * k, far), send(v, there, sems, 27 + 3 * k, sib))
        for v, o in pairs:
            o[:, columns(me)] = v[...]

    def gather_pass(k):
        moves[k][0].wait_recv()
        there = pairs[k][1].at[:, columns(far)]
        moves[k + 2] = (send(there, there, sems, 28 + 3 * k, sib),)

    def gather_end(k):
        moves[k][0].wait_send()
        moves[k][1].wait()
        moves[k + 2][0].wait()

    def tables():
        lengths = r_lengths[...]
        one_length = [lengths[:, k:k + 1] for k in range(4)]
        ends = [one_length[0]]
        for k in range(1, 4):
            ends.append(ends[-1] + one_length[k])

        def segment(row):
            total = jnp.zeros(row.shape, jnp.int32)
            for end in ends:
                total = total + jnp.where(row >= end, 1, 0)
            return total

        row = lax.broadcasted_iota(jnp.int32, (rows, 128), 0)
        start = jnp.zeros(row.shape, jnp.int32)
        for end, length in zip(ends, one_length):
            start = start + jnp.where(row >= end, length, 0)
        lane = lax.broadcasted_iota(jnp.int32, (rows, 128), 1) % 64
        power = (lane % 32).astype(f32) * (-2.0 / HEAD_SIZE)
        angles = (row - start).astype(f32) * jnp.exp(power * math.log(THETA))
        cosine, sine = jnp.cos(angles), jnp.sin(angles)
        sine = jnp.where(lane < 32, -sine, sine)
        for k in (0, 128):
            r_cosine[:, k:k + 128] = cosine
            r_sine[:, k:k + 128] = sine
        query_row = lax.broadcasted_iota(jnp.int32, (rows, rows), 0)
        key_row = lax.broadcasted_iota(jnp.int32, (rows, rows), 1)
        moves[9] = (segment(query_row) == segment(key_row)) & (query_row >= key_row)

    def attn_norm():
        gain = r_attn_gain[...]

        def block(at, v):
            resid = r_x[at, :].astype(f32)
            inverse = lax.rsqrt(jnp.mean(resid * resid, axis=-1, keepdims=True) + EPS)
            r_normed_one[at, :] = (resid * inverse * gain).astype(bf)
            return v

        row_blocks(block, 0)

    def attention():
        normed = r_normed_one[...]
        r_v_low[...] = jnp.dot(normed, r_w_value[...], preferred_element_type=f32).astype(bf)
        for weight, gain, low, plain_ref, inv_ref, heads in (
            (r_w_query, r_q_gain, r_q_low, r_q_plain, r_q_inv, 4), (r_w_key, r_k_gain, r_k_low, r_k_plain, r_k_inv, 2)):
            width = 64 * heads
            raw = jnp.dot(normed, weight[...], preferred_element_type=f32)
            inv = spread([lax.rsqrt(m + EPS) for m in head_means(raw * raw, heads)], heads)
            plain = raw * inv
            inv_ref[...] = inv
            plain_ref[...] = plain
            scaled = plain * jnp.concatenate([gain[...]] * heads, axis=1)
            low[...] = (scaled * r_cosine[:, :width] + swap_halves(scaled) * r_sine[:, :width]).astype(bf)
        out = []
        for h in range(4):
            at = slice(64 * (h // 2), 64 * (h // 2) + 64)
            scores = dot_last(r_q_low[:, 64 * h:64 * h + 64], r_k_low[:, at]) * HEAD_SIZE ** (-0.5)
            scores = jnp.where(moves[9], scores, -1e30)
            weights = jnp.exp(scores - jnp.max(scores, axis=-1, keepdims=True))
            p = weights / jnp.sum(weights, axis=-1, keepdims=True)
            r_p[h] = p
            out.append(jnp.dot(p.astype(bf), r_v_low[:, at], preferred_element_type=f32))
        heads_out = jnp.concatenate(out, axis=1).astype(bf)
        r_heads_out[...] = heads_out
        r_part[...] = jnp.dot(heads_out, r_w_output[...], preferred_element_type=f32)

    def mlp_norm():
        gain = r_mlp_gain[...]

        def block(at, v):
            hidden = r_x[at, :].astype(f32) + r_attended[at, :].astype(f32)
            r_hidden[at, :] = hidden
            inverse = lax.rsqrt(jnp.mean(hidden * hidden, axis=-1, keepdims=True) + EPS)
            r_normed_two[at, :] = (hidden * inverse * gain).astype(bf)
            return v

        row_blocks(block, 0)

    def back_down():
        loads[2].wait()

        def tile(j, v):
            at = pl.ds(pl.multiple_of(j * 384, 128), 384)
            r_d_act[:, at] = dot_last(r_cot[...], w_down[at, :])
            return v

        lax.fori_loop(0, 3, tile, 0)

    def mlp_units():
        for load in loads[:2]:
            load.wait()

        def tile(j, v):
            at = pl.ds(pl.multiple_of(j * 384, 128), 384)
            gate = jnp.dot(r_normed_two[...], w_gate[:, at], preferred_element_type=f32)
            up = jnp.dot(r_normed_two[...], w_up[:, at], preferred_element_type=f32)
            s = jax.nn.sigmoid(gate)
            silu = gate * s
            r_act[:, at] = (silu * up).astype(bf)
            d_act = r_d_act[:, at]
            r_d_gate[:, at] = (d_act * up * s * (1.0 + gate * (1.0 - s))).astype(bf)
            r_d_up[:, at] = (d_act * silu).astype(bf)
            return v

        lax.fori_loop(0, 3, tile, 0)

    def weight_grad(left, right, out, h=None):
        def tile(j, v):
            part = dot_rows(left[:, columns(j)], right[...]).astype(bf)
            out[j // 2, pl.ds((j % 2) * 2, 2)] = part.reshape(2, 4, 32, right.shape[1])
            return v

        first, last = (0, 4) if h is None else (2 * h, 2 * h + 2)
        return lambda: lax.fori_loop(first, last, tile, 0)

    def swap_y(k, src, dst):
        c = pltpu.make_async_remote_copy(
            src_ref=src, dst_ref=dst, send_sem=sems[0].at[32 + k], recv_sem=sems[1].at[32 + k],
            device_id={"dp": c0.ynb["dp"]}, device_id_type=MESH)
        c.start()
        moves[20 + k] = c

    def swap_cot():
        half = lambda v: pl.ds(pl.multiple_of(v * 512, 512), 512)
        swap_y(0, r_cot.at[:, half(1 - y)], r_cots.at[pl.ds(144, 144)])
        r_cots[0:144, :] = r_cot[:, half(y)]

    def swap_act():
        swap_y(1, r_act, r_acts.at[pl.ds(144, 144)])

    def down_grad():
        moves[20].wait()
        moves[21].wait()

        def tile(j, v):
            grads[0][j] = dot_rows(r_cots[:, columns(j)], r_acts[...]).astype(bf).reshape(4, 4, 16, 1152)
            return v

        lax.fori_loop(0, 2, tile, 0)

    gate_low, gate_high = [weight_grad(r_normed_two, r_d_gate, grads[1], h) for h in range(2)]
    up_grad = weight_grad(r_normed_two, r_d_up, grads[2])

    def mlp_back():
        def tile(j, v):
            at = columns(j)
            r_d_two_part[:, at] = dot_last(r_d_gate[...], w_gate[at, :]) + dot_last(r_d_up[...], w_up[at, :])
            return v

        lax.fori_loop(0, 4, tile, 0)

    def mlp_out():
        def tile(j, v):
            at = columns(j)
            r_mlp_part[:, at] = jnp.dot(r_act[...], w_down[:, at], preferred_element_type=f32)
            return v

        lax.fori_loop(0, 4, tile, 0)

    def back_mlp_norm():
        gain = r_mlp_gain[...]

        def block(b, total):
            at = pl.ds(pl.multiple_of(b * 16, 16), 16)
            hidden = r_hidden[at, :]
            inverse = lax.rsqrt(jnp.mean(hidden * hidden, axis=-1, keepdims=True) + EPS)
            plain = hidden * inverse
            d_two = r_d_two[at, :].astype(jnp.float32)
            u = d_two * gain
            d_hidden = r_cot[at, :].astype(jnp.float32) + inverse * (
                u - plain * jnp.mean(u * plain, axis=-1, keepdims=True))
            r_d_hidden[at, :] = d_hidden
            r_d_low[at, :] = d_hidden.astype(jnp.bfloat16)
            return total + jnp.sum(d_two * plain, axis=0, keepdims=True)

        total = lax.fori_loop(0, rows // 16, block, jnp.zeros((1, 1024), jnp.float32))
        r_vec[...] = jnp.zeros((8, 1024), jnp.float32)
        r_vec[1:2, :] = total
        mine = columns(me)
        r_block_out[...] = (r_hidden[:, mine] + r_own[...]).astype(jnp.bfloat16)

    hold = {}

    def back_output():
        d_low = r_d_low[...]
        hold[0] = dot_last(d_low, r_w_output[...]).astype(jnp.bfloat16)
        r_attn[:, :, :, :, 512:768] = dot_rows(d_low, r_heads_out[...]).astype(jnp.bfloat16).reshape(2, 4, 4, 32, 256)

    def back_scores():
        d_heads = hold[0]
        scale = HEAD_SIZE ** (-0.5)
        d_query, d_key, d_value = [], [], []
        for j in range(2):
            at = slice(64 * j, 64 * j + 64)
            key, value = r_k_low[:, at], r_v_low[:, at]
            dk, dv = 0.0, 0.0
            for h in (2 * j, 2 * j + 1):
                p = r_p[h]
                dh = d_heads[:, 64 * h:64 * h + 64]
                d_probs = dot_last(dh, value)
                ds = (p * (d_probs - jnp.sum(d_probs * p, axis=-1, keepdims=True))).astype(jnp.bfloat16)
                d_query.append(jnp.dot(ds, key, preferred_element_type=jnp.float32) * scale)
                dk = dk + dot_rows(ds, r_q_low[:, 64 * h:64 * h + 64])
                dv = dv + dot_rows(p.astype(jnp.bfloat16), dh)
            d_key.append(dk * scale)
            d_value.append(dv)
        r_d_qkv[:, 384:512] = jnp.concatenate(d_value, axis=1).astype(jnp.bfloat16)
        hold[1] = jnp.concatenate(d_query, axis=1)
        hold[2] = jnp.concatenate(d_key, axis=1)

    def back_head_norm():
        r_gains[...] = jnp.zeros((8, 128), jnp.float32)
        for d, plain_ref, gain_ref, inv_ref, heads, put, place_at in (
            (hold[1], r_q_plain, r_q_gain, r_q_inv, 4, 0, 0), (hold[2], r_k_plain, r_k_gain, r_k_inv, 2, 256, 64)):
            width = 64 * heads
            turned = d * r_cosine[:, :width] - swap_halves(d) * r_sine[:, :width]
            plain = plain_ref[...]
            sums = jnp.sum(turned * plain, axis=0, keepdims=True)
            total = sums[:, :64]
            for h in range(1, heads):
                total = total + sums[:, 64 * h:64 * h + 64]
            r_gains[0:1, place_at:place_at + 64] = total
            u = turned * jnp.concatenate([gain_ref[...]] * heads, axis=1)
            inv = inv_ref[...]
            back = inv * (u - plain * spread(head_means(u * plain, heads), heads))
            r_d_qkv[:, put:put + width] = back.astype(jnp.bfloat16)

    def back_project():
        dq, dk, dv = r_d_qkv[:, :256], r_d_qkv[:, 256:384], r_d_qkv[:, 384:512]
        r_part[...] = (
            dot_last(dq, r_w_query[...]) + dot_last(dk, r_w_key[...]) + dot_last(dv, r_w_value[...]))

    def back_attn_weights():
        r_attn[:, :, :, :, 0:512] = dot_rows(r_normed_one[...], r_d_qkv[...]).astype(jnp.bfloat16).reshape(2, 4, 4, 32, 512)

    def back_attn_norm():
        gain = r_attn_gain[...]
        mine = columns(me)

        def block(b, total):
            at = pl.ds(pl.multiple_of(b * 16, 16), 16)
            resid = r_x[at, :].astype(jnp.float32)
            inverse = lax.rsqrt(jnp.mean(resid * resid, axis=-1, keepdims=True) + EPS)
            plain = resid * inverse
            d_one = r_d_one[at, :].astype(jnp.float32)
            u = d_one * gain
            r_d_hidden[at, :] = r_d_hidden[at, :] + inverse * (
                u - plain * jnp.mean(u * plain, axis=-1, keepdims=True))
            return total + jnp.sum(d_one * plain, axis=0, keepdims=True)

        total = lax.fori_loop(0, rows // 16, block, jnp.zeros((1, 1024), jnp.float32))
        r_vec[0:1, :] = total
        r_vec[2:3, 0:128] = r_gains_sum[0:1, :]
        r_input_grad[...] = r_d_hidden[:, mine].astype(jnp.bfloat16)

    for step in (
        gather_start, tables, lambda: gather_pass(0), lambda: gather_pass(1), lambda: gather_end(0), attn_norm, attention, attended[0],
        lambda: gather_end(1), attended[1], back_down, attended[2], swap_cot, attended[3], mlp_norm, mlp_units, swap_act, gate_low,
        lambda: c1.begin(0), gate_high, lambda: c1.begin(1), mlp_back, two[0], up_grad, two[1], c2.start1, down_grad, c0.start1, mlp_out,
        two[2], own[0], two[3], own[1], c1.mid1, own[2], c0.mid1, own[3], back_mlp_norm, back_output, c2.mid1, c1.fin1, back_scores,
        c0.fin1, back_head_norm, back_project, one[0], gains[0], back_attn_weights, c3.start1, c0.mid2, c1.mid2, one[1], gains[1],
        c0.fin2, c2.fin1, one[2], gains[2], c0.ag2, c1.fin2, one[3], back_attn_norm, small.one, c0.ag1s, c3.mid1, c2.mid2, c1.finy,
        small.two, c0.ag1, c2.fin2, c0.ya, c3.fin1, c1.ag2, c2.finy, c3.mid2, small.three, c1.ag1s, c3.fin2, c0.ybc, c0.last, c0.yd,
        c2.ag2, c3.finy, c2.ag1s, c1.ag1, c3.ag2, small.four, c3.ag1s, c2.ag1, leave(1, c1), c3.ag1, leave(0, c0), leave(2, c2), leave(3,
        c3),
    ):
        step()
    for out in stores:
        out.wait()


def big(arrays):
    V, A = pl.BlockSpec(memory_space=pltpu.VMEM), pl.BlockSpec(memory_space=pl.ANY)
    f32, bf = jnp.float32, jnp.bfloat16
    S = jax.ShapeDtypeStruct
    out_shape = [S(s, bf) for s in SUM_SHAPES] + [S((8, 1024), f32), S((144, 256), bf), S((144, 256), bf)]
    B = lambda *shape: pltpu.VMEM(shape, bf)
    F = lambda *shape: pltpu.VMEM(shape, f32)
    D = lambda n: pltpu.SemaphoreType.DMA((n,))
    scratch = sum([scratch_for(s) for s in CHUNK_SHAPES], [])
    scratch += [F(3, 4, 8, 1024), F(3, 8, 1024), D(9), D(9)]
    scratch += [B(*s) for s in CHUNK_SHAPES] + [B(*s) for s in SUM_SHAPES]
    scratch += [F(8, 1024), B(144, 1024), F(144, 256), B(144, 1024), F(8, 128), F(8, 128), F(144, 1024), F(144, 1024), B(144, 1024), B(144, 512)]
    scratch += [B(144, 1024), B(144, 1024), B(144, 1024), B(144, 1024), B(144, 1024), F(144, 1024), F(144, 1024), F(144, 1024)]
    scratch += [B(144, 256), B(144, 128), B(144, 128), F(144, 256), F(144, 128), F(144, 256), F(144, 128), F(144, 256), F(144, 256), F(4, 144, 144), B(144, 256)]
    scratch += [B(288, 1152), B(144, 1152), B(144, 1152), B(1024, 1152), B(1024, 1152), B(1152, 1024), B(288, 512), F(144, 1152)]
    scratch += ([B(144, 1024)] + [B(2, 144, 256)] * 3) * 4 + [F(8, 128)] * 3
    scratch += [D(34), D(34), D(3), D(4)]
    return pl.pallas_call(
        big_kernel, out_shape=out_shape, in_specs=[V] * 11 + [A] * 3, out_specs=[A] * 4 + [V] * 3, scratch_shapes=scratch,
        compiler_params=pltpu.CompilerParams(collective_id=0, has_side_effects=True, vmem_limit_bytes=61 * 1024 * 1024),
        name="block",
    )(*arrays)


def widen_kernel(gate, up, down, attn, vec, block, grad, o_gate, o_up, o_down, o_q, o_k, o_v, o_out, o_attn, o_mlp, o_qg, o_kg, o_block, o_grad):
    o_gate[...] = gate[...].astype(jnp.float32)
    o_up[...] = up[...].astype(jnp.float32)
    o_down[...] = down[...].astype(jnp.float32).T
    wide = attn[...].astype(jnp.float32)
    o_q[...] = wide[:, :256]
    o_k[...] = wide[:, 256:384]
    o_v[...] = wide[:, 384:512]
    o_out[...] = wide[:, 512:768].T

    @pl.when(pl.program_id(0) == 0)
    def _():
        o_attn[...] = vec[0, :]
        o_mlp[...] = vec[1, :]
        o_qg[...] = vec[2, 0:64]
        o_kg[...] = vec[2, 64:128]
        o_block[...] = block[...]
        o_grad[...] = grad[...]


def widen(gate, up, down, attn, vec, block, grad):
    S = lambda *s: jax.ShapeDtypeStruct(s, jnp.float32)
    row = lambda w: pl.BlockSpec((256, w), lambda b: (b, 0))
    col = lambda h: pl.BlockSpec((h, 256), lambda b: (0, b))
    all_of = lambda *s: pl.BlockSpec(s, lambda b: (0,) * len(s))
    own = jax.ShapeDtypeStruct(block.shape, block.dtype)
    return pl.pallas_call(
        widen_kernel, grid=(4,),
        in_specs=[row(1152), row(1152), row(1152), row(768), all_of(8, 1024), all_of(144, 256), all_of(144, 256)],
        out_specs=[row(1152), row(1152), col(1152), row(256), row(128), row(128), col(256),
                   all_of(1024), all_of(1024), all_of(64), all_of(64), all_of(144, 256), all_of(144, 256)],
        out_shape=[S(1024, 1152), S(1024, 1152), S(1152, 1024), S(1024, 256), S(1024, 128), S(1024, 128), S(256, 1024),
                   S(1024), S(1024), S(64), S(64), own, own],
        compiler_params=pltpu.CompilerParams(vmem_limit_bytes=60 * 1024 * 1024),
        name="widen",
    )(gate, up, down, attn, vec, block, grad)


EPS = 1e-05
THETA = 1000000.0


def dot_rows(left_side, right_side):
    return lax.dot_general(
        left_side, right_side, (((0,), (0,)), ((), ())), preferred_element_type=jnp.float32
    )


def dot_last(left_side, right_side):
    return lax.dot_general(
        left_side, right_side, (((1,), (1,)), ((), ())), preferred_element_type=jnp.float32
    )


def body(
    tokens,
    lengths,
    attn_gain,
    w_query,
    key_weight,
    value_weight,
    query_gain,
    key_gain,
    w_output,
    mlp_gain,
    w_gate,
    w_up,
    w_down,
    cotangent,
):
    down, gate, up, attn, vec, block_out, input_grad = big(
        (
            tokens,
            cotangent,
            lengths,
            attn_gain[None],
            mlp_gain[None],
            query_gain[None],
            key_gain[None],
            w_query,
            key_weight,
            value_weight,
            w_output,
            w_gate,
            w_up,
            w_down,
        )
    )
    gate, up, down, w_q, w_k, w_v, w_o, attn_g, mlp_g, query_g, key_g, block_out, input_grad = widen(
        gate.reshape(1024, 1152), up.reshape(1024, 1152), down.reshape(1024, 1152), attn.reshape(1024, 768), vec, block_out, input_grad
    )
    return (block_out, input_grad, attn_g, w_q, w_k, w_v, query_g, key_g, w_o, mlp_g, gate, up, down)


def solution(mesh):
    in_specs = (
        P("dp", "tensor"),
        P("dp", None),
        P(),
        P(None, "tensor"),
        P(None, "tensor"),
        P(None, "tensor"),
        P(),
        P(),
        P("tensor", None),
        P(),
        P(None, "tensor"),
        P(None, "tensor"),
        P("tensor", None),
        P("dp", "tensor"),
    )
    out_specs = (
        P("dp", "tensor"),
        P("dp", "tensor"),
        P(),
        P(None, "tensor"),
        P(None, "tensor"),
        P(None, "tensor"),
        P(),
        P(),
        P("tensor", None),
        P(),
        P(None, "tensor"),
        P(None, "tensor"),
        P("tensor", None),
    )
    return jax.shard_map(body, mesh=mesh, in_specs=in_specs, out_specs=out_specs, check_vma=False)
```

```python
import math
import functools
import jax
import jax.numpy as jnp
from jax import lax
from jax.experimental import pallas as pl
from jax.experimental.pallas import tpu as pltpu
from jax.sharding import PartitionSpec as P

HEAD_SIZE = 64
MESH = pl.DeviceIdType.MESH


def add_into(out, parts, step):
    lead = out.shape[0]
    rows = out.shape[1]
    per = rows // step

    def add_step(i, _):
        b = i // per
        r = pl.multiple_of((i % per) * step, 16)
        total = parts[0][b, pl.ds(r, step), :].astype(jnp.float32)
        for part in parts[1:]:
            total = total + part[b, pl.ds(r, step), :].astype(jnp.float32)
        out[b, pl.ds(r, step), :] = total.astype(jnp.bfloat16)
        return 0

    lax.fori_loop(0, lead * per, add_step, 0)


(T1P, T1M, I1P, I1M, M1P, M1M, T2P, T2M, I2P, I2M, M2P, M2M, Y, A2P, A2M, F2P, F2M, A1P, A1M, F1P, F1M, YA, YB, YC, YD) = range(25)
KEYS = 25


class Chunk:
    def __init__(self, src, dst, t1, r1, m1, s1, t2, r2, m2, s2, yb, send, recv, step, where):
        self.src, self.dst = src, dst
        self.t1, self.r1, self.m1, self.s1 = t1, r1, m1, s1
        self.t2, self.r2, self.m2, self.s2, self.yb = t2, r2, m2, s2, yb
        self.send, self.recv, self.step = send, recv, step
        y, z, x = where
        self.where = where

        def dev(yy, zz, xx):
            return {"dp": (yy * 4 + zz) * 4 + xx}

        up = lambda v: lax.rem(v + 1, 4)
        down = lambda v: lax.rem(v + 3, 4)
        xp, xm = dev(y, z, up(x)), dev(y, z, down(x))
        zp, zm = dev(y, up(z), x), dev(y, down(z), x)
        self.ynb = dev(1 - y, z, x)
        self.first = ((x, xp, xm), (z, zp, zm))
        self.second = ((z, zp, zm), (x, xp, xm))
        self.live = {}
        R, C = src.shape[3:]
        self.lo = (pl.ds(0, R // 2), pl.ds(0, C))
        self.hi = (pl.ds(R // 2, R // 2), pl.ds(0, C))

    def go(self, h, name, src, dst, device):
        k = h * KEYS + name
        c = pltpu.make_async_remote_copy(
            src_ref=src, dst_ref=dst, send_sem=self.send.at[k], recv_sem=self.recv.at[k],
            device_id=device, device_id_type=MESH)
        c.start()
        self.live[h, name] = c

    def got(self, h, *names):
        for n in names:
            self.live[h, n].wait_recv()

    def start1(self):
        for h in range(2):
            self.begin(h)

    def begin(self, h):
        p, plus, minus = self.first[h]
        k2, kp, km = lax.rem(p + 2, 4), lax.rem(p + 1, 4), lax.rem(p + 3, 4)
        H, T, R = self.src.at[h], self.t1.at[h], self.r1.at[h]
        self.go(h, T1P, H.at[k2, pl.ds(0, 2)], T.at[0], plus)
        self.go(h, T1M, H.at[k2, pl.ds(2, 2)], T.at[1], minus)
        self.go(h, I1P, H.at[kp, pl.ds(2, 2)], R.at[0, pl.ds(2, 2)], plus)
        self.go(h, I1M, H.at[km, pl.ds(0, 2)], R.at[1, pl.ds(0, 2)], minus)

    def mid1(self):
        for h in range(2):
            p, plus, minus = self.first[h]
            kp, km = lax.rem(p + 1, 4), lax.rem(p + 3, 4)
            H, T, R, M = self.src.at[h], self.t1.at[h], self.r1.at[h], self.m1.at[h]
            self.got(h, T1P)
            add_into(M.at[0], (H.at[kp, pl.ds(0, 2)], T.at[0]), self.step)
            self.go(h, M1P, M.at[0], R.at[0, pl.ds(0, 2)], plus)
            self.got(h, T1M)
            add_into(M.at[1], (H.at[km, pl.ds(2, 2)], T.at[1]), self.step)
            self.go(h, M1M, M.at[1], R.at[1, pl.ds(2, 2)], minus)

    def fin1(self):
        for h in range(2):
            p = self.first[h][0]
            R = self.r1.at[h]
            self.got(h, I1P, I1M, M1P, M1M)
            add_into(self.s1.at[h], (self.src.at[h, p], R.at[0], R.at[1]), self.step)
            p, plus, minus = self.second[h]
            k2, kp, km = lax.rem(p + 2, 4), lax.rem(p + 1, 4), lax.rem(p + 3, 4)
            H, T, R, lo, hi = self.s1.at[h], self.t2.at[h], self.r2.at[h], self.lo, self.hi
            self.go(h, T2P, H.at[(k2,) + lo], T.at[lo], plus)
            self.go(h, T2M, H.at[(k2,) + hi], T.at[hi], minus)
            self.go(h, I2P, H.at[(kp,) + hi], R.at[(0,) + hi], plus)
            self.go(h, I2M, H.at[(km,) + lo], R.at[(1,) + lo], minus)

    def mid2(self):
        for h in range(2):
            p, plus, minus = self.second[h]
            kp, km = lax.rem(p + 1, 4), lax.rem(p + 3, 4)
            R, own = self.r2.at[h], (pl.ds(h, 1),)
            for name, arrived, k, part, slot, to in ((M2P, T2P, kp, self.lo, 0, plus), (M2M, T2M, km, self.hi, 1, minus)):
                self.got(h, arrived)
                add_into(self.m2.at[own + part], (self.s1.at[(h, pl.ds(k, 1)) + part], self.t2.at[own + part]), 16)
                self.go(h, name, self.m2.at[(h,) + part], R.at[(slot,) + part], to)

    def fin2(self):
        for h in range(2):
            p = self.second[h][0]
            R = self.r2.at[h]
            self.got(h, I2P, I2M, M2P, M2M)
            add_into(self.s2.at[pl.ds(h, 1)], (self.s1.at[h, pl.ds(p, 1)], R.at[pl.ds(0, 1)], R.at[pl.ds(1, 1)]), self.step)
            self.go(h, Y, self.s2.at[h], self.yb.at[h], self.ynb)

    def finy(self):
        for h in range(2):
            a = self.first[h][0]
            p, plus, minus = self.second[h]
            self.got(h, Y)
            add_into(self.dst.at[h, a, pl.ds(p, 1)], (self.s2.at[pl.ds(h, 1)], self.yb.at[pl.ds(h, 1)]), self.step)
            blk = self.dst.at[h, a, p]
            self.go(h, A2P, blk, blk, plus)
            self.go(h, A2M, blk, blk, minus)

    def ag2(self):
        for h in range(2):
            a = self.first[h][0]
            p, plus, minus = self.second[h]
            kp, km = lax.rem(p + 1, 4), lax.rem(p + 3, 4)
            self.got(h, A2P)
            blk = self.dst.at[(h, a, km) + self.lo]
            self.go(h, F2P, blk, blk, plus)
            self.got(h, A2M)
            blk = self.dst.at[(h, a, kp) + self.hi]
            self.go(h, F2M, blk, blk, minus)

    def ag1s(self):
        for h in range(2):
            p, plus, minus = self.first[h]
            self.got(h, F2P, F2M)
            blk = self.dst.at[h, p]
            self.go(h, A1P, blk, blk, plus)
            self.go(h, A1M, blk, blk, minus)

    def ag1(self):
        for h in range(2):
            p, plus, minus = self.first[h]
            kp, km = lax.rem(p + 1, 4), lax.rem(p + 3, 4)
            self.got(h, A1P)
            blk = self.dst.at[h, km, pl.ds(0, 2)]
            self.go(h, F1P, blk, blk, plus)
            self.got(h, A1M)
            blk = self.dst.at[h, kp, pl.ds(2, 2)]
            self.go(h, F1M, blk, blk, minus)

    def end(self):
        for h in range(2):
            self.got(h, F1P, F1M)
        for c in self.live.values():
            c.wait_send()

    def stages(self):
        return [self.start1, self.mid1, self.fin1, self.mid2, self.fin2, self.finy, self.ag2, self.ag1s, self.ag1, self.end]


class HalfChunk(Chunk):
    def __init__(self, src, whole, *rest):
        *_, where = rest
        super().__init__(src, whole.at[where[0]], *rest)
        R, C = src.shape[3:]
        self.lo = (pl.ds(0, R), pl.ds(0, 640))
        self.hi = (pl.ds(0, R), pl.ds(640, C - 640))

    def fin2(self):
        for h in range(2):
            a = self.first[h][0]
            p, plus, minus = self.second[h]
            R = self.r2.at[h]
            self.got(h, I2P, I2M, M2P, M2M)
            add_into(self.dst.at[h, a, pl.ds(p, 1)], (self.s1.at[h, pl.ds(p, 1)], R.at[pl.ds(0, 1)], R.at[pl.ds(1, 1)]), self.step)
            blk = self.dst.at[h, a, p]
            self.go(h, A2P, blk, blk, plus)
            self.go(h, A2M, blk, blk, minus)

    def across(self, h, name, k):
        blk = self.dst.at[h, k]
        self.go(h, name, blk, blk, self.ynb)

    def ya(self):
        for h in range(2):
            self.across(h, YA, self.first[h][0])

    def ybc(self):
        for h in range(2):
            p = self.first[h][0]
            self.across(h, YB, lax.rem(p + 3, 4))
            self.across(h, YC, lax.rem(p + 1, 4))

    def last(self):
        for h in range(2):
            self.got(h, F1P, F1M)

    def yd(self):
        for h in range(2):
            self.across(h, YD, lax.rem(self.first[h][0] + 2, 4))

    def end(self):
        for h in range(2):
            self.got(h, YA, YB, YC, YD)
        for c in self.live.values():
            c.wait_send()


def coords():
    d = lax.axis_index("dp")
    return d // 16, (d // 4) % 4, d % 4


def scratch_for(shape):
    _, _, _, R, C = shape
    bf = jnp.bfloat16
    return [
        pltpu.VMEM((2, 2, 2, R, C), bf), pltpu.VMEM((2, 2, 4, R, C), bf), pltpu.VMEM((2, 2, 2, R, C), bf), pltpu.VMEM((2, 4, R, C), bf),
        pltpu.VMEM((2, R, C), bf), pltpu.VMEM((2, 2, R, C), bf), pltpu.VMEM((2, R, C), bf), pltpu.VMEM((2, R, C), bf), pltpu.VMEM((2, R, C), bf),
        pltpu.SemaphoreType.DMA((2 * KEYS,)), pltpu.SemaphoreType.DMA((2 * KEYS,)),
    ]

NS = 11

def tensor_place():
    t = lax.axis_index("tensor")
    core, side = lax.rem(t, 2), t // 2
    return side, core, side * 2 + (1 - core), (1 - side) * 2 + core


def send(src, dst, sems, k, peer):
    c = pltpu.make_async_remote_copy(
        src_ref=src, dst_ref=dst, send_sem=sems[0].at[k], recv_sem=sems[1].at[k],
        device_id={"tensor": peer}, device_id_type=MESH)
    c.start()
    return c


def greet(sib, far):
    barrier = pltpu.get_barrier_semaphore()
    for peer in (sib, far):
        pl.semaphore_signal(barrier, inc=1, device_id={"tensor": peer}, device_id_type=MESH)
    pl.semaphore_wait(barrier, 2)


def columns(block):
    return pl.ds(pl.multiple_of(block * 256, 256), 256)


def sum_steps(part, out, low, near, mid, away, sems, base, place, scatter):
    side, core, sib, far = place
    live = []

    def one():
        low[...] = part[...].astype(jnp.bfloat16)
        for s in range(2):
            live.append(send(low.at[:, columns(s * 2 + 1 - core)], near.at[s], sems, base + s, sib))

    def fold(s):
        mid[s] = (low[:, columns(s * 2 + core)].astype(jnp.float32) + near[s].astype(jnp.float32)).astype(jnp.bfloat16)

    def two():
        if scatter:
            for s in range(2):
                live[s].wait_recv()
            fold(1 - side)
            live.append(send(mid.at[1 - side], away.at[1 - side], sems, base + 2, far))
            fold(side)
            return
        for s in range(2):
            live[s].wait_recv()
            fold(s)
            live.append(send(mid.at[s], away.at[s], sems, base + 2 + s, far))

    def three():
        if scatter:
            live[2].wait_recv()
            out[...] = mid[side].astype(jnp.float32) + away[side].astype(jnp.float32)
            return
        for s in range(2):
            live[2 + s].wait_recv()
            there = out.at[:, columns(s * 2 + core)]
            out[:, columns(s * 2 + core)] = (mid[s].astype(jnp.float32) + away[s].astype(jnp.float32)).astype(jnp.bfloat16)
            live.append(send(there, there, sems, base + 4 + s, sib))

    def four():
        for c in live[4:]:
            c.wait_recv()
        for c in live:
            c.wait_send()

    return [one, two, three, four]


class SmallSum:
    def __init__(self, where, vec, out, slots, mine, send_sem, recv_sem):
        y, z, x = where
        self.vec, self.out, self.slots, self.mine = vec, out, slots, mine
        self.sems = (send_sem, recv_sem)
        self.axes = (
            (x, 4, lambda v: (y * 4 + z) * 4 + v),
            (z, 4, lambda v: (y * 4 + v) * 4 + x),
            (y, 2, lambda v: (v * 4 + z) * 4 + x),
        )
        self.live = []

    def begin(self, s, value):
        p, n, dev = self.axes[s]
        self.mine[s] = value
        self.slots[s, p] = value
        self.live = []
        for i in range(1, n):
            k = s * 3 + i - 1
            c = pltpu.make_async_remote_copy(
                src_ref=self.mine.at[s], dst_ref=self.slots.at[s, p], send_sem=self.sems[0].at[k], recv_sem=self.sems[1].at[k],
                device_id={"dp": dev(lax.rem(p + i, n))}, device_id_type=MESH)
            c.start()
            self.live.append(c)

    def close(self, s):
        for c in self.live:
            c.wait()
        value = self.slots[s, 0]
        for i in range(1, self.axes[s][1]):
            value = value + self.slots[s, i]
        return value

    def one(self):
        self.begin(0, self.vec[...])

    def two(self):
        self.begin(1, self.close(0))

    def three(self):
        self.begin(2, self.close(1))

    def four(self):
        self.out[...] = self.close(2)


def small_steps(v, out, near, mid, away, sems, base, place):
    side, core, sib, far = place
    live = []

    def one():
        live.append(send(v, near, sems, base, sib))

    def two():
        live[0].wait()
        mid[...] = v[...] + near[...]
        live.append(send(mid, away, sems, base + 1, far))

    def three():
        live[1].wait()
        out[...] = mid[...] + away[...]

    return [one, two, three]


def swap_halves(v):
    n = v.shape[1]
    lane = lax.broadcasted_iota(jnp.int32, v.shape, 1) % 64
    return jnp.where(lane < 32, pltpu.roll(v, n - 32, 1), pltpu.roll(v, 32, 1))


def head_means(v, heads):
    return [jnp.mean(v[:, 64 * h:64 * h + 64], axis=-1, keepdims=True) for h in range(heads)]


def spread(cols, heads):
    return jnp.concatenate([jnp.broadcast_to(c, (c.shape[0], 64)) for c in cols], axis=1)


CHUNK_SHAPES = ((2, 4, 4, 16, 1152), (2, 4, 4, 32, 1152), (2, 4, 4, 32, 1152), (2, 4, 4, 32, 768))
SUM_SHAPES = ((2,) + CHUNK_SHAPES[0],) + CHUNK_SHAPES[1:]


def big_kernel(*refs):
    (
        r_tokens, r_cotangent, r_lengths, r_attn_gain, r_mlp_gain, r_q_gain, r_k_gain,
        r_w_query, r_w_key, r_w_value, r_w_output, h_gate, h_up, h_down,
    ) = refs[:14]
    h_sums, (r_vec_sum, r_block_out, r_input_grad) = refs[14:18], refs[18:21]
    rest = refs[21:]
    groups = [rest[NS * c:NS * c + NS] for c in range(4)]
    rest = rest[NS * 4:]
    small_refs, grads, sums, rest = rest[:4], rest[4:8], rest[8:12], rest[12:]
    (r_vec, r_d_two, r_own, r_d_one, r_gains, r_gains_sum, r_part, r_d_hidden, r_d_low, r_d_qkv) = rest[:10]
    (r_x, r_cot, r_normed_one, r_normed_two, r_attended, r_hidden, r_d_two_part, r_mlp_part) = rest[10:18]
    (r_q_low, r_k_low, r_v_low, r_q_plain, r_k_plain, r_q_inv, r_k_inv, r_cosine, r_sine, r_p, r_heads_out) = rest[18:29]
    (r_acts, r_d_gate, r_d_up, w_gate, w_up, w_down, r_cots, r_d_act) = rest[29:37]
    rest = rest[37:]
    r_act = r_acts.at[pl.ds(0, 144)]
    ts, tb, tc, ta, td = rest[:4], rest[4:8], rest[8:12], rest[12:16], rest[16:19]
    sems, load_sem, store_sem = rest[19:21], rest[21], rest[22]
    where, place = coords(), tensor_place()
    side, core, sib, far = place
    me = side * 2 + core
    y, z, x = where
    f32, bf = jnp.float32, jnp.bfloat16
    loads = []
    for k, (there, here) in enumerate(((h_gate, w_gate), (h_up, w_up), (h_down, w_down))):
        loads.append(pltpu.make_async_copy(there, here, load_sem.at[k]))
        loads[k].start()
    barrier = pltpu.get_barrier_semaphore()
    peers = [(y, z, lax.rem(x + k, 4)) for k in (1, 2, 3)] + [(y, lax.rem(z + k, 4), x) for k in (1, 2, 3)] + [(1 - y, z, x)]
    for a, b, c in peers:
        pl.semaphore_signal(barrier, inc=1, device_id={"dp": (a * 4 + b) * 4 + c}, device_id_type=MESH)
    for peer in (sib, far):
        pl.semaphore_signal(barrier, inc=1, device_id={"tensor": peer}, device_id_type=MESH)
    pl.semaphore_wait(barrier, len(peers) + 2)

    c0 = HalfChunk(grads[0], sums[0], *groups[0], 16, where)
    c1, c2, c3 = [Chunk(grads[c], sums[c], *groups[c], 16, where) for c in range(1, 4)]
    r_attn = grads[3]
    small = SmallSum(where, r_vec, r_vec_sum, *small_refs)
    attended = sum_steps(r_part, r_attended, *ts, sems, 0, place, False)
    two = sum_steps(r_d_two_part, r_d_two, *ta, sems, 6, place, False)
    own = sum_steps(r_mlp_part, r_own, *tb, sems, 12, place, True)
    one = sum_steps(r_part, r_d_one, *tc, sems, 18, place, False)
    gains = small_steps(r_gains, r_gains_sum, *td, sems, 24, place)
    rows = r_x.shape[0]
    stores = []

    def leave(c, chunk):
        def finish():
            chunk.end()
            out = pltpu.make_async_copy(sums[c], h_sums[c], store_sem.at[c])
            out.start()
            stores.append(out)

        return finish

    def row_blocks(step, start):
        return lax.fori_loop(0, rows // 16, lambda b, v: step(pl.ds(pl.multiple_of(b * 16, 16), 16), v), start)

    pairs = ((r_tokens, r_x), (r_cotangent, r_cot))
    moves = {}

    def gather_start():
        for k, (v, o) in enumerate(pairs):
            there = o.at[:, columns(me)]
            moves[k] = (send(v, there, sems, 26 + 3 * k, far), send(v, there, sems, 27 + 3 * k, sib))
        for v, o in pairs:
            o[:, columns(me)] = v[...]

    def gather_pass(k):
        moves[k][0].wait_recv()
        there = pairs[k][1].at[:, columns(far)]
        moves[k + 2] = (send(there, there, sems, 28 + 3 * k, sib),)

    def gather_end(k):
        moves[k][0].wait_send()
        moves[k][1].wait()
        moves[k + 2][0].wait()

    def tables():
        lengths = r_lengths[...]
        one_length = [lengths[:, k:k + 1] for k in range(4)]
        ends = [one_length[0]]
        for k in range(1, 4):
            ends.append(ends[-1] + one_length[k])

        def segment(row):
            total = jnp.zeros(row.shape, jnp.int32)
            for end in ends:
                total = total + jnp.where(row >= end, 1, 0)
            return total

        row = lax.broadcasted_iota(jnp.int32, (rows, 128), 0)
        start = jnp.zeros(row.shape, jnp.int32)
        for end, length in zip(ends, one_length):
            start = start + jnp.where(row >= end, length, 0)
        lane = lax.broadcasted_iota(jnp.int32, (rows, 128), 1) % 64
        power = (lane % 32).astype(f32) * (-2.0 / HEAD_SIZE)
        angles = (row - start).astype(f32) * jnp.exp(power * math.log(THETA))
        cosine, sine = jnp.cos(angles), jnp.sin(angles)
        sine = jnp.where(lane < 32, -sine, sine)
        for k in (0, 128):
            r_cosine[:, k:k + 128] = cosine
            r_sine[:, k:k + 128] = sine
        query_row = lax.broadcasted_iota(jnp.int32, (rows, rows), 0)
        key_row = lax.broadcasted_iota(jnp.int32, (rows, rows), 1)
        moves[9] = (segment(query_row) == segment(key_row)) & (query_row >= key_row)

    def attn_norm():
        gain = r_attn_gain[...]

        def block(at, v):
            resid = r_x[at, :].astype(f32)
            inverse = lax.rsqrt(jnp.mean(resid * resid, axis=-1, keepdims=True) + EPS)
            r_normed_one[at, :] = (resid * inverse * gain).astype(bf)
            return v

        row_blocks(block, 0)

    def attention():
        normed = r_normed_one[...]
        r_v_low[...] = jnp.dot(normed, r_w_value[...], preferred_element_type=f32).astype(bf)
        for weight, gain, low, plain_ref, inv_ref, heads in (
            (r_w_query, r_q_gain, r_q_low, r_q_plain, r_q_inv, 4), (r_w_key, r_k_gain, r_k_low, r_k_plain, r_k_inv, 2)):
            width = 64 * heads
            raw = jnp.dot(normed, weight[...], preferred_element_type=f32)
            inv = spread([lax.rsqrt(m + EPS) for m in head_means(raw * raw, heads)], heads)
            plain = raw * inv
            inv_ref[...] = inv
            plain_ref[...] = plain
            scaled = plain * jnp.concatenate([gain[...]] * heads, axis=1)
            low[...] = (scaled * r_cosine[:, :width] + swap_halves(scaled) * r_sine[:, :width]).astype(bf)
        out = []
        for h in range(4):
            at = slice(64 * (h // 2), 64 * (h // 2) + 64)
            scores = dot_last(r_q_low[:, 64 * h:64 * h + 64], r_k_low[:, at]) * HEAD_SIZE ** (-0.5)
            scores = jnp.where(moves[9], scores, -1e30)
            weights = jnp.exp(scores - jnp.max(scores, axis=-1, keepdims=True))
            p = weights / jnp.sum(weights, axis=-1, keepdims=True)
            r_p[h] = p
            out.append(jnp.dot(p.astype(bf), r_v_low[:, at], preferred_element_type=f32))
        heads_out = jnp.concatenate(out, axis=1).astype(bf)
        r_heads_out[...] = heads_out
        r_part[...] = jnp.dot(heads_out, r_w_output[...], preferred_element_type=f32)

    def mlp_norm():
        gain = r_mlp_gain[...]

        def block(at, v):
            hidden = r_x[at, :].astype(f32) + r_attended[at, :].astype(f32)
            r_hidden[at, :] = hidden
            inverse = lax.rsqrt(jnp.mean(hidden * hidden, axis=-1, keepdims=True) + EPS)
            r_normed_two[at, :] = (hidden * inverse * gain).astype(bf)
            return v

        row_blocks(block, 0)

    def back_down():
        loads[2].wait()

        def tile(j, v):
            at = pl.ds(pl.multiple_of(j * 384, 128), 384)
            r_d_act[:, at] = dot_last(r_cot[...], w_down[at, :])
            return v

        lax.fori_loop(0, 3, tile, 0)

    def mlp_units():
        for load in loads[:2]:
            load.wait()

        def tile(j, v):
            at = pl.ds(pl.multiple_of(j * 384, 128), 384)
            gate = jnp.dot(r_normed_two[...], w_gate[:, at], preferred_element_type=f32)
            up = jnp.dot(r_normed_two[...], w_up[:, at], preferred_element_type=f32)
            s = jax.nn.sigmoid(gate)
            silu = gate * s
            r_act[:, at] = (silu * up).astype(bf)
            d_act = r_d_act[:, at]
            r_d_gate[:, at] = (d_act * up * s * (1.0 + gate * (1.0 - s))).astype(bf)
            r_d_up[:, at] = (d_act * silu).astype(bf)
            return v

        lax.fori_loop(0, 3, tile, 0)

    def weight_grad(left, right, out, h=None):
        def tile(j, v):
            part = dot_rows(left[:, columns(j)], right[...]).astype(bf)
            out[j // 2, pl.ds((j % 2) * 2, 2)] = part.reshape(2, 4, 32, right.shape[1])
            return v

        first, last = (0, 4) if h is None else (2 * h, 2 * h + 2)
        return lambda: lax.fori_loop(first, last, tile, 0)

    def swap_y(k, src, dst):
        c = pltpu.make_async_remote_copy(
            src_ref=src, dst_ref=dst, send_sem=sems[0].at[32 + k], recv_sem=sems[1].at[32 + k],
            device_id={"dp": c0.ynb["dp"]}, device_id_type=MESH)
        c.start()
        moves[20 + k] = c

    def swap_cot():
        half = lambda v: pl.ds(pl.multiple_of(v * 512, 512), 512)
        swap_y(0, r_cot.at[:, half(1 - y)], r_cots.at[pl.ds(144, 144)])
        r_cots[0:144, :] = r_cot[:, half(y)]

    def swap_act():
        swap_y(1, r_act, r_acts.at[pl.ds(144, 144)])

    def down_grad():
        moves[20].wait()
        moves[21].wait()

        def tile(j, v):
            grads[0][j] = dot_rows(r_cots[:, columns(j)], r_acts[...]).astype(bf).reshape(4, 4, 16, 1152)
            return v

        lax.fori_loop(0, 2, tile, 0)

    gate_low, gate_high = [weight_grad(r_normed_two, r_d_gate, grads[1], h) for h in range(2)]
    up_grad = weight_grad(r_normed_two, r_d_up, grads[2])

    def mlp_back():
        def tile(j, v):
            at = columns(j)
            r_d_two_part[:, at] = dot_last(r_d_gate[...], w_gate[at, :]) + dot_last(r_d_up[...], w_up[at, :])
            return v

        lax.fori_loop(0, 4, tile, 0)

    def mlp_out():
        def tile(j, v):
            at = columns(j)
            r_mlp_part[:, at] = jnp.dot(r_act[...], w_down[:, at], preferred_element_type=f32)
            return v

        lax.fori_loop(0, 4, tile, 0)

    def back_mlp_norm():
        gain = r_mlp_gain[...]

        def block(b, total):
            at = pl.ds(pl.multiple_of(b * 16, 16), 16)
            hidden = r_hidden[at, :]
            inverse = lax.rsqrt(jnp.mean(hidden * hidden, axis=-1, keepdims=True) + EPS)
            plain = hidden * inverse
            d_two = r_d_two[at, :].astype(jnp.float32)
            u = d_two * gain
            d_hidden = r_cot[at, :].astype(jnp.float32) + inverse * (
                u - plain * jnp.mean(u * plain, axis=-1, keepdims=True))
            r_d_hidden[at, :] = d_hidden
            r_d_low[at, :] = d_hidden.astype(jnp.bfloat16)
            return total + jnp.sum(d_two * plain, axis=0, keepdims=True)

        total = lax.fori_loop(0, rows // 16, block, jnp.zeros((1, 1024), jnp.float32))
        r_vec[...] = jnp.zeros((8, 1024), jnp.float32)
        r_vec[1:2, :] = total
        mine = columns(me)
        r_block_out[...] = (r_hidden[:, mine] + r_own[...]).astype(jnp.bfloat16)

    hold = {}

    def back_output():
        d_low = r_d_low[...]
        hold[0] = dot_last(d_low, r_w_output[...]).astype(jnp.bfloat16)
        r_attn[:, :, :, :, 512:768] = dot_rows(d_low, r_heads_out[...]).astype(jnp.bfloat16).reshape(2, 4, 4, 32, 256)

    def back_scores():
        d_heads = hold[0]
        scale = HEAD_SIZE ** (-0.5)
        d_query, d_key, d_value = [], [], []
        for j in range(2):
            at = slice(64 * j, 64 * j + 64)
            key, value = r_k_low[:, at], r_v_low[:, at]
            dk, dv = 0.0, 0.0
            for h in (2 * j, 2 * j + 1):
                p = r_p[h]
                dh = d_heads[:, 64 * h:64 * h + 64]
                d_probs = dot_last(dh, value)
                ds = (p * (d_probs - jnp.sum(d_probs * p, axis=-1, keepdims=True))).astype(jnp.bfloat16)
                d_query.append(jnp.dot(ds, key, preferred_element_type=jnp.float32) * scale)
                dk = dk + dot_rows(ds, r_q_low[:, 64 * h:64 * h + 64])
                dv = dv + dot_rows(p.astype(jnp.bfloat16), dh)
            d_key.append(dk * scale)
            d_value.append(dv)
        r_d_qkv[:, 384:512] = jnp.concatenate(d_value, axis=1).astype(jnp.bfloat16)
        hold[1] = jnp.concatenate(d_query, axis=1)
        hold[2] = jnp.concatenate(d_key, axis=1)

    def back_head_norm():
        r_gains[...] = jnp.zeros((8, 128), jnp.float32)
        for d, plain_ref, gain_ref, inv_ref, heads, put, place_at in (
            (hold[1], r_q_plain, r_q_gain, r_q_inv, 4, 0, 0), (hold[2], r_k_plain, r_k_gain, r_k_inv, 2, 256, 64)):
            width = 64 * heads
            turned = d * r_cosine[:, :width] - swap_halves(d) * r_sine[:, :width]
            plain = plain_ref[...]
            sums = jnp.sum(turned * plain, axis=0, keepdims=True)
            total = sums[:, :64]
            for h in range(1, heads):
                total = total + sums[:, 64 * h:64 * h + 64]
            r_gains[0:1, place_at:place_at + 64] = total
            u = turned * jnp.concatenate([gain_ref[...]] * heads, axis=1)
            inv = inv_ref[...]
            back = inv * (u - plain * spread(head_means(u * plain, heads), heads))
            r_d_qkv[:, put:put + width] = back.astype(jnp.bfloat16)

    def back_project():
        dq, dk, dv = r_d_qkv[:, :256], r_d_qkv[:, 256:384], r_d_qkv[:, 384:512]
        r_part[...] = (
            dot_last(dq, r_w_query[...]) + dot_last(dk, r_w_key[...]) + dot_last(dv, r_w_value[...]))

    def back_attn_weights():
        r_attn[:, :, :, :, 0:512] = dot_rows(r_normed_one[...], r_d_qkv[...]).astype(jnp.bfloat16).reshape(2, 4, 4, 32, 512)

    def back_attn_norm():
        gain = r_attn_gain[...]
        mine = columns(me)

        def block(b, total):
            at = pl.ds(pl.multiple_of(b * 16, 16), 16)
            resid = r_x[at, :].astype(jnp.float32)
            inverse = lax.rsqrt(jnp.mean(resid * resid, axis=-1, keepdims=True) + EPS)
            plain = resid * inverse
            d_one = r_d_one[at, :].astype(jnp.float32)
            u = d_one * gain
            r_d_hidden[at, :] = r_d_hidden[at, :] + inverse * (
                u - plain * jnp.mean(u * plain, axis=-1, keepdims=True))
            return total + jnp.sum(d_one * plain, axis=0, keepdims=True)

        total = lax.fori_loop(0, rows // 16, block, jnp.zeros((1, 1024), jnp.float32))
        r_vec[0:1, :] = total
        r_vec[2:3, 0:128] = r_gains_sum[0:1, :]
        r_input_grad[...] = r_d_hidden[:, mine].astype(jnp.bfloat16)

    for step in (
        gather_start, tables, lambda: gather_pass(0), lambda: gather_pass(1), lambda: gather_end(0), attn_norm, attention, attended[0],
        lambda: gather_end(1), attended[1], back_down, attended[2], swap_cot, attended[3], mlp_norm, mlp_units, swap_act, gate_low,
        lambda: c1.begin(0), gate_high, lambda: c1.begin(1), mlp_back, two[0], up_grad, two[1], c2.start1, down_grad, c0.start1, mlp_out,
        two[2], own[0], two[3], own[1], c1.mid1, own[2], c0.mid1, own[3], back_mlp_norm, back_output, c2.mid1, c1.fin1, back_scores,
        c0.fin1, back_head_norm, back_project, one[0], gains[0], back_attn_weights, c3.start1, c0.mid2, c1.mid2, one[1], gains[1],
        c0.fin2, c2.fin1, one[2], gains[2], c0.ag2, c1.fin2, one[3], back_attn_norm, small.one, c0.ag1s, c3.mid1, c2.mid2, c1.finy,
        small.two, c0.ag1, c2.fin2, c0.ya, c3.fin1, c1.ag2, c2.finy, c3.mid2, small.three, c1.ag1s, c3.fin2, c0.ybc, c0.last, c0.yd,
        c2.ag2, c3.finy, c2.ag1s, c1.ag1, c3.ag2, small.four, c3.ag1s, c2.ag1, leave(1, c1), c3.ag1, leave(0, c0), leave(2, c2), leave(3,
        c3),
    ):
        step()
    for out in stores:
        out.wait()


def big(arrays):
    V, A = pl.BlockSpec(memory_space=pltpu.VMEM), pl.BlockSpec(memory_space=pl.ANY)
    f32, bf = jnp.float32, jnp.bfloat16
    S = jax.ShapeDtypeStruct
    out_shape = [S(s, bf) for s in SUM_SHAPES] + [S((8, 1024), f32), S((144, 256), bf), S((144, 256), bf)]
    B = lambda *shape: pltpu.VMEM(shape, bf)
    F = lambda *shape: pltpu.VMEM(shape, f32)
    D = lambda n: pltpu.SemaphoreType.DMA((n,))
    scratch = sum([scratch_for(s) for s in CHUNK_SHAPES], [])
    scratch += [F(3, 4, 8, 1024), F(3, 8, 1024), D(9), D(9)]
    scratch += [B(*s) for s in CHUNK_SHAPES] + [B(*s) for s in SUM_SHAPES]
    scratch += [F(8, 1024), B(144, 1024), F(144, 256), B(144, 1024), F(8, 128), F(8, 128), F(144, 1024), F(144, 1024), B(144, 1024), B(144, 512)]
    scratch += [B(144, 1024), B(144, 1024), B(144, 1024), B(144, 1024), B(144, 1024), F(144, 1024), F(144, 1024), F(144, 1024)]
    scratch += [B(144, 256), B(144, 128), B(144, 128), F(144, 256), F(144, 128), F(144, 256), F(144, 128), F(144, 256), F(144, 256), F(4, 144, 144), B(144, 256)]
    scratch += [B(288, 1152), B(144, 1152), B(144, 1152), B(1024, 1152), B(1024, 1152), B(1152, 1024), B(288, 512), F(144, 1152)]
    scratch += ([B(144, 1024)] + [B(2, 144, 256)] * 3) * 4 + [F(8, 128)] * 3
    scratch += [D(34), D(34), D(3), D(4)]
    return pl.pallas_call(
        big_kernel, out_shape=out_shape, in_specs=[V] * 11 + [A] * 3, out_specs=[A] * 4 + [V] * 3, scratch_shapes=scratch,
        compiler_params=pltpu.CompilerParams(collective_id=0, has_side_effects=True, vmem_limit_bytes=61 * 1024 * 1024),
        name="block",
    )(*arrays)


def widen_kernel(gate, up, down, attn, vec, block, grad, o_gate, o_up, o_down, o_q, o_k, o_v, o_out, o_attn, o_mlp, o_qg, o_kg, o_block, o_grad):
    o_gate[...] = gate[...].astype(jnp.float32)
    o_up[...] = up[...].astype(jnp.float32)
    o_down[...] = down[...].astype(jnp.float32).T
    wide = attn[...].astype(jnp.float32)
    o_q[...] = wide[:, :256]
    o_k[...] = wide[:, 256:384]
    o_v[...] = wide[:, 384:512]
    o_out[...] = wide[:, 512:768].T

    @pl.when(pl.program_id(0) == 0)
    def _():
        o_attn[...] = vec[0, :]
        o_mlp[...] = vec[1, :]
        o_qg[...] = vec[2, 0:64]
        o_kg[...] = vec[2, 64:128]
        o_block[...] = block[...]
        o_grad[...] = grad[...]


def widen(gate, up, down, attn, vec, block, grad):
    S = lambda *s: jax.ShapeDtypeStruct(s, jnp.float32)
    row = lambda w: pl.BlockSpec((512, w), lambda b: (b, 0))
    col = lambda h: pl.BlockSpec((h, 512), lambda b: (0, b))
    all_of = lambda *s: pl.BlockSpec(s, lambda b: (0,) * len(s))
    own = jax.ShapeDtypeStruct(block.shape, block.dtype)
    return pl.pallas_call(
        widen_kernel, grid=(2,),
        in_specs=[row(1152), row(1152), row(1152), row(768), all_of(8, 1024), all_of(144, 256), all_of(144, 256)],
        out_specs=[row(1152), row(1152), col(1152), row(256), row(128), row(128), col(256),
                   all_of(1024), all_of(1024), all_of(64), all_of(64), all_of(144, 256), all_of(144, 256)],
        out_shape=[S(1024, 1152), S(1024, 1152), S(1152, 1024), S(1024, 256), S(1024, 128), S(1024, 128), S(256, 1024),
                   S(1024), S(1024), S(64), S(64), own, own],
        compiler_params=pltpu.CompilerParams(vmem_limit_bytes=60 * 1024 * 1024),
        name="widen",
    )(gate, up, down, attn, vec, block, grad)


EPS = 1e-05
THETA = 1000000.0


def dot_rows(left_side, right_side):
    return lax.dot_general(
        left_side, right_side, (((0,), (0,)), ((), ())), preferred_element_type=jnp.float32
    )


def dot_last(left_side, right_side):
    return lax.dot_general(
        left_side, right_side, (((1,), (1,)), ((), ())), preferred_element_type=jnp.float32
    )


def body(
    tokens,
    lengths,
    attn_gain,
    w_query,
    key_weight,
    value_weight,
    query_gain,
    key_gain,
    w_output,
    mlp_gain,
    w_gate,
    w_up,
    w_down,
    cotangent,
):
    down, gate, up, attn, vec, block_out, input_grad = big(
        (
            tokens,
            cotangent,
            lengths,
            attn_gain[None],
            mlp_gain[None],
            query_gain[None],
            key_gain[None],
            w_query,
            key_weight,
            value_weight,
            w_output,
            w_gate,
            w_up,
            w_down,
        )
    )
    gate, up, down, w_q, w_k, w_v, w_o, attn_g, mlp_g, query_g, key_g, block_out, input_grad = widen(
        gate.reshape(1024, 1152), up.reshape(1024, 1152), down.reshape(1024, 1152), attn.reshape(1024, 768), vec, block_out, input_grad
    )
    return (block_out, input_grad, attn_g, w_q, w_k, w_v, query_g, key_g, w_o, mlp_g, gate, up, down)


def solution(mesh):
    in_specs = (
        P("dp", "tensor"),
        P("dp", None),
        P(),
        P(None, "tensor"),
        P(None, "tensor"),
        P(None, "tensor"),
        P(),
        P(),
        P("tensor", None),
        P(),
        P(None, "tensor"),
        P(None, "tensor"),
        P("tensor", None),
        P("dp", "tensor"),
    )
    out_specs = (
        P("dp", "tensor"),
        P("dp", "tensor"),
        P(),
        P(None, "tensor"),
        P(None, "tensor"),
        P(None, "tensor"),
        P(),
        P(),
        P("tensor", None),
        P(),
        P(None, "tensor"),
        P(None, "tensor"),
        P("tensor", None),
    )
    return jax.shard_map(body, mesh=mesh, in_specs=in_specs, out_specs=out_specs, check_vma=False)
```
